32 devices in a mesh: seq: 16 (over z, y, core), rep: 2 (over x).
Axes of the slice: x: 2, y: 2, z: 4, core: 2. Of those that a mesh axis runs over, the one named last changes fastest.
Arguments:
- tokens: bfloat16 [4096, 2048], P(('seq', 'rep')), may hold values from -6 to 6
- cotangent: bfloat16 [4096, 2048], P(('seq', 'rep')), may hold values from -6 to 6
- domain_tags: int32 [4096], P(('seq', 'rep')), may hold values from 0 to 3, as said below
- doc_ids: int32 [4096], replicated, may hold values from 0 to 7, never falling along the last dimension, each value on 1 to 1024 neighbouring positions
- counts: int32 [4], replicated, may hold values from 1 to 1, as said below
- w_in: bfloat16 [2048, 2048], P('seq'), may hold values from -0.125 to 0.125
- w_forget: bfloat16 [2048, 2048], P('seq'), may hold values from -0.125 to 0.125
- w_gate_out: bfloat16 [2048, 2048], P('seq'), may hold values from -0.125 to 0.125
- w_out: bfloat16 [2048, 2048], P('seq'), may hold values from -0.25 to 0.25
- ffn_gate: bfloat16 [2048, 5632], P('seq'), may hold values from -0.125 to 0.125
- ffn_up: bfloat16 [2048, 5632], P('seq'), may hold values from -0.125 to 0.125
- ffn_down: bfloat16 [5632, 2048], P('seq'), may hold values from -0.15625 to 0.15625
- norm_gain: float32 [2048], replicated, may hold values from 0.25 to 1.75
- out_gain: float32 [2048], replicated, may hold values from 0.25 to 1.75
- ffn_gain: float32 [2048], replicated, may hold values from 0.25 to 1.75
- bound_logits: float32 [24, 2048], P(None, ('seq', 'rep')), may hold values from -6 to 6
Outputs:
- output_rows: bfloat16 [4096, 2048], P(('seq', 'rep'))
- grad_tokens: float32 [4096, 2048], P(('seq', 'rep'))
- grad_w_in: float32 [2048, 2048], P(('seq', 'rep'))
- grad_w_forget: float32 [2048, 2048], P(('seq', 'rep'))
- grad_w_gate_out: float32 [2048, 2048], P(('seq', 'rep'))
- grad_w_out: float32 [2048, 2048], P(('seq', 'rep'))
- grad_ffn_gate: float32 [2048, 5632], P(('seq', 'rep'))
- grad_ffn_up: float32 [2048, 5632], P(('seq', 'rep'))
- grad_ffn_down: float32 [5632, 2048], P(None, ('seq', 'rep'))
- grad_norm_gain: float32 [2048], P(('seq', 'rep'))
- grad_out_gain: float32 [2048], P(('seq', 'rep'))
- grad_ffn_gain: float32 [2048], P(('seq', 'rep'))
- grad_bound_logits: float32 [24, 2048], P(None, ('seq', 'rep'))
The draws below stay inside these ranges and needn't reach their ends.
Inputs may be any that keep to these rules, and one draw needn't show every extreme that they name: `domain_tags`: all 1024 tokens of a sequence share one domain, and every domain has at least one sequence. counts is the number of sequences whose tokens carry each domain.
All inputs are finite; a program needn't handle non-finite values.
Results may differ from the reference program's by a relative error of at most 0.011.
Values may be sent and summed in bfloat16 or wider, within the bound.
A program may use at most 704 MiB of HBM per device.

```python
import math
import jax
import jax.numpy as jnp
import numpy as np
from jax import lax

D = 2048
FF = 5632
LAYERS = 24
LAYER_AT = 12
NDOM = 4
SEQ_LEN = 1024
TOKENS = 4096
SEQS = 4
DOCS = 8


def domain_rows(key):
    smallest = max(1, SEQS * 3 // 26)
    third = max(1, SEQS * 5 // 26)
    second = max(1, SEQS * 7 // 26)
    largest = SEQS - second - third - smallest
    shares = jnp.array([largest, second, third, smallest], dtype=jnp.int32)
    owners = jax.random.permutation(key, NDOM).astype(jnp.int32)
    domains = jnp.repeat(owners, shares, total_repeat_length=SEQS).astype(jnp.int32)
    order = jax.random.permutation(jax.random.fold_in(key, 1), SEQS)
    return domains[order]


def draw_domain_tags(key, part):
    domains = domain_rows(key)
    return jnp.repeat(domains, SEQ_LEN, total_repeat_length=SEQS * SEQ_LEN).astype(jnp.int32)


def draw_counts(key, part):
    domains = domain_rows(key)
    hits = domains[:, None] == jnp.arange(NDOM, dtype=jnp.int32)[None, :]
    return jnp.sum(hits.astype(jnp.int32), axis=0).astype(jnp.int32)


def block_levels(stream_key, dims, cuts, low, top_value):
    def one(position, blocks):
        draws = jax.random.uniform(jax.random.fold_in(jax.random.fold_in(stream_key, 6), position), (blocks,), jnp.float32, low / len(cuts), top_value / len(cuts))
        return jnp.repeat(jnp.exp(draws), dims[position] // blocks).reshape((-1,) + (1,) * (len(dims) - position - 1))

    loudness = one(*cuts[0])
    for cut in cuts[1:]:
        loudness = loudness * one(*cut)
    return loudness


def length_profile(number_of, total, bound, skew):
    weights = [(1 << 20) // math.isqrt(grade ** skew) + 1 for grade in range(2, number_of + 1)]
    surplus, given = total - bound - (number_of - 1), [1] * (number_of - 1)
    while surplus > 0:
        free = [i for i in range(number_of - 1) if given[i] < bound]
        pool, left = sum([weights[i] for i in free]), surplus
        for i in free:
            extra = min(bound - given[i], max(1, left * weights[i] // pool), surplus)
            given[i] = given[i] + extra
            surplus = surplus - extra
    return np.array([bound] + given)


def ragged(rng, count, total, limit, slope):
    if count == 2:
        one = jax.random.randint(rng, (), max(1, total - limit), min(limit, total - 1) + 1)
        return jnp.stack([one, total - one])
    lengths = jnp.asarray(length_profile(count, total, limit, slope), jnp.int32)
    couples = (count - 1) // 2
    donor, sink = lengths[1:1 + 2 * couples:2], lengths[2:2 + 2 * couples:2]
    margin = jnp.minimum(donor - 1, limit - sink)
    moved = jax.random.randint(jax.random.fold_in(rng, 1), (couples,), 0, 1 << 20) % (margin + 1)
    lengths = lengths.at[1:1 + 2 * couples:2].set(donor - moved).at[2:2 + 2 * couples:2].set(sink + moved)
    return lengths[jax.random.permutation(jax.random.fold_in(rng, 2), count)]


def scatter_about(own_key, shape, width, reach, shards=(), kind=jnp.bfloat16):
    values = width * jax.random.normal(own_key, shape, jnp.float32)
    if shards:
        values = values * block_levels(own_key, shape, shards, -0.22, 0.18)
    return jnp.clip(values, -reach, reach).astype(kind)


def setup_inputs(seed: int = 0) -> dict:
    streams_of = jax.random.split(jax.random.key(seed), 17)
    tokens = scatter_about(streams_of[0], (TOKENS, D), 1.0, 6.0, ((0, 32),))
    cotangent = scatter_about(streams_of[1], (TOKENS, D), 1.0, 6.0, ((0, 32),))
    domain_tags = draw_domain_tags(jax.random.fold_in(streams_of[16], 71), 0)
    doc_ids = jnp.searchsorted(jnp.cumsum(ragged(streams_of[3], DOCS, TOKENS, SEQ_LEN, 0)), jnp.arange(TOKENS), side="right").astype(jnp.int32)
    counts = draw_counts(jax.random.fold_in(streams_of[16], 71), 0)
    w_in = scatter_about(streams_of[5], (D, D), D ** -0.5, 0.125, ((0, 16),))
    w_forget = scatter_about(streams_of[6], (D, D), D ** -0.5, 0.125, ((0, 16),))
    w_gate_out = scatter_about(streams_of[7], (D, D), D ** -0.5, 0.125, ((0, 16),))
    w_out = scatter_about(streams_of[8], (D, D), (D // 4) ** -0.5, 0.25, ((0, 16),))
    ffn_gate = scatter_about(streams_of[9], (D, FF), D ** -0.5, 0.125, ((0, 16),))
    ffn_up = scatter_about(streams_of[10], (D, FF), D ** -0.5, 0.125, ((0, 16),))
    ffn_down = scatter_about(streams_of[11], (FF, D), (FF // 4) ** -0.5, 0.15625, ((0, 16),))
    norm_gain = jnp.clip(1.0 + 0.15 * jax.random.normal(streams_of[12], (D,), jnp.float32), 0.25, 1.75)
    out_gain = jnp.clip(1.0 + 0.15 * jax.random.normal(streams_of[13], (D,), jnp.float32), 0.25, 1.75)
    ffn_gain = jnp.clip(1.0 + 0.15 * jax.random.normal(streams_of[14], (D,), jnp.float32), 0.25, 1.75)
    bound_logits = scatter_about(streams_of[15], (LAYERS, D), 1.5, 6.0, ((1, 32),), jnp.float32)
    return {"tokens": tokens, "cotangent": cotangent, "domain_tags": domain_tags, "doc_ids": doc_ids, "counts": counts, "w_in": w_in, "w_forget": w_forget, "w_gate_out": w_gate_out, "w_out": w_out, "ffn_gate": ffn_gate, "ffn_up": ffn_up, "ffn_down": ffn_down, "norm_gain": norm_gain, "out_gain": out_gain, "ffn_gain": ffn_gain, "bound_logits": bound_logits}


@jax.custom_vjp
def low(v):
    return lax.optimization_barrier(v.astype(jnp.bfloat16)).astype(jnp.float32)

@jax.custom_vjp
def low_back(v):
    return v

def low_keep(v):
    return (low(v), None)

def low_pass(kept, grad):
    return (grad,)

def back_keep(v):
    return (v, None)

def back_low(kept, grad):
    return (low(grad),)
low.defvjp(low_keep, low_pass)
low_back.defvjp(back_keep, back_low)
EPS = 1e-06
HIGH = lax.Precision.HIGHEST

def matmul(left, right):
    return jnp.dot(left, right, precision=HIGH, preferred_element_type=jnp.float32)

def rms_norm(values, gain):
    return values * lax.rsqrt(lax.optimization_barrier(jnp.mean(values * values, axis=-1, keepdims=True)) + EPS) * gain

def chain_link(earlier, later):
    return (earlier[0] * later[0], later[0] * earlier[1] + later[1])

def layer(params, keep_mask):
    tokens, w_in, w_forget, w_gate_out, w_out, ffn_gate, ffn_up, ffn_down, norm_gain, out_gain, ffn_gain, bound_logits = params
    act_one = low(rms_norm(tokens, norm_gain))
    in_proj = low(low_back(matmul(act_one, w_in)))
    forget_proj = low(low_back(matmul(act_one, w_forget)))
    gate_proj = low_back(matmul(act_one, w_gate_out))
    layer_probs = jax.nn.softmax(bound_logits, axis=0)
    lower_bound = lax.optimization_barrier(jnp.sum(layer_probs[1:LAYER_AT + 1], axis=0))
    forget = lower_bound + (1.0 - lower_bound) * jax.nn.sigmoid(forget_proj)
    drive_in = jax.nn.silu(in_proj) * (1.0 - forget)
    decay_step = forget * keep_mask[:, None]
    _, states = lax.associative_scan(chain_link, (decay_step, drive_in), axis=0)
    states = low_back(low(states))
    state_norm = rms_norm(states, out_gain) * jax.nn.silu(gate_proj)
    branch = low_back(matmul(low(state_norm), w_out))
    residual = tokens + branch
    act_two = low(rms_norm(residual, ffn_gain))
    gate_ffn = low_back(matmul(act_two, ffn_gate))
    up_ffn = low_back(matmul(act_two, ffn_up))
    hidden = low(jax.nn.silu(gate_ffn) * up_ffn)
    return residual + low_back(matmul(hidden, ffn_down))

def reference(tokens, cotangent, domain_tags, doc_ids, counts, w_in, w_forget, w_gate_out, w_out, ffn_gate, ffn_up, ffn_down, norm_gain, out_gain, ffn_gain, bound_logits):
    places = jnp.arange(TOKENS, dtype=jnp.int32)
    previous = jnp.concatenate([doc_ids[:1], doc_ids[:-1]])
    keep_mask = jnp.where((places % SEQ_LEN != 0) & (doc_ids == previous), 1.0, 0.0).astype(jnp.float32)
    floats = (tokens.astype(jnp.float32), w_in.astype(jnp.float32), w_forget.astype(jnp.float32), w_gate_out.astype(jnp.float32), w_out.astype(jnp.float32), ffn_gate.astype(jnp.float32), ffn_up.astype(jnp.float32), ffn_down.astype(jnp.float32), norm_gain.astype(jnp.float32), out_gain.astype(jnp.float32), ffn_gain.astype(jnp.float32), bound_logits.astype(jnp.float32))
    result, pullback = jax.vjp(lambda *params: layer(params, keep_mask), *floats)
    domain_hits = domain_tags[:, None] == jnp.arange(NDOM, dtype=jnp.int32)[None, :]
    per_token = lax.optimization_barrier(jnp.sum(jnp.where(domain_hits, counts[None, :], 0), axis=1)).astype(jnp.float32)
    weighting = SEQS / (NDOM * per_token)
    grads = pullback(cotangent.astype(jnp.float32) * weighting[:, None])
    return (result.astype(jnp.bfloat16), grads[0], grads[1], grads[2], grads[3], grads[4], grads[5], grads[6], grads[7], grads[8], grads[9], grads[10], grads[11])
```

```python
import functools

import jax
import jax.numpy as jnp
from jax import lax
from jax.experimental import pallas as pl
from jax.experimental.pallas import tpu as pltpu
from jax.sharding import Mesh
from jax.sharding import PartitionSpec as P

LAYER_AT = 12
SEQ_LEN = 1024
EPS = 1e-06
ROWS = 16
PLANE = ("p", "c", "x")
ALL = ("g", "p", "c", "x")
f32 = jnp.float32
bf16 = jnp.bfloat16


def split_hi_lo(v):
    hi = v.astype(bf16)
    return hi, (v - hi.astype(f32)).astype(bf16)


def gates(proj, chan, lower):
    ip = proj[:, :chan].astype(bf16).astype(f32)
    sf = jax.nn.sigmoid(proj[:, chan : 2 * chan].astype(bf16).astype(f32))
    forget = lower + (1.0 - lower) * sf
    sig_in = jax.nn.sigmoid(ip)
    return ip, sig_in, sf, forget


def forward_scan(chan, proj_ref, keep_ref, lower_ref, gain_ref, h_ref, o_ref, ss_ref):
    lower = lower_ref[...]
    gain = gain_ref[...]
    row = lax.broadcasted_iota(jnp.int32, (ROWS, chan), 0)

    def step(i, carry):
        rows = pl.ds(pl.multiple_of(i * ROWS, ROWS), ROWS)
        proj = proj_ref[rows, :]
        ip, sig_in, _, forget = gates(proj, chan, lower)
        u = ip * sig_in * (1.0 - forget)
        e = forget * keep_ref[rows, :]
        shift = 1
        while shift < ROWS:
            u = u + e * jnp.where(row >= shift, pltpu.roll(u, shift, 0), 0.0)
            e = e * jnp.where(row >= shift, pltpu.roll(e, shift, 0), 1.0)
            shift *= 2
        h = u + e * carry
        h_ref[rows, :] = h
        hb = h.astype(bf16).astype(f32)
        gate = proj[:, 2 * chan :]
        o_ref[rows, :] = (hb * gain * (gate * jax.nn.sigmoid(gate))).astype(bf16)
        ss_ref[rows, :] = jnp.sum(hb * hb, axis=1, keepdims=True)
        return h[ROWS - 1 : ROWS, :]

    lax.fori_loop(0, proj_ref.shape[0] // ROWS, step, jnp.zeros((1, chan), f32))


def backward_scan(
    chan, proj_ref, h_ref, do_ref, info_ref, keep_ref, lower_ref, gain_ref, grad_ref, o_ref, sums_ref
):
    lower = lower_ref[...]
    gain = gain_ref[...]
    row = lax.broadcasted_iota(jnp.int32, (ROWS, chan), 0)
    blocks = proj_ref.shape[0] // ROWS

    def step(j, carried):
        later, sum_lower, sum_gain = carried
        i = blocks - 1 - j
        rows = pl.ds(pl.multiple_of(i * ROWS, ROWS), ROWS)
        proj = proj_ref[rows, :]
        ip, sig_in, sf, forget = gates(proj, chan, lower)
        keep = keep_ref[rows, :]
        act_in = ip * sig_in
        h = h_ref[rows, :]
        before = h_ref[pl.ds(pl.multiple_of(jnp.maximum(i * ROWS - 8, 0), 8), 8), :][7:8, :]
        h_prev = jnp.where(row >= 1, pltpu.roll(h, 1, 0), before)
        scale = info_ref[rows, 0:1]
        mean = info_ref[rows, 1:2]
        hn = h.astype(bf16).astype(f32) * scale
        gate = proj[:, 2 * chan :]
        sig_gate = jax.nn.sigmoid(gate)
        gate_act = gate * sig_gate
        do = do_ref[rows, :]
        o_ref[rows, :] = (hn * gain * gate_act).astype(bf16)
        sum_gain = sum_gain + jnp.sum(do * hn * gate_act, axis=0, keepdims=True)
        dgp = do * hn * gain * (sig_gate * (1.0 + gate * (1.0 - sig_gate)))
        dhb = scale * (do * gain * gate_act - hn * mean)
        d = dhb.astype(bf16).astype(f32)
        e = forget * keep
        c = jnp.where(row < ROWS - 1, pltpu.roll(e, ROWS - 1, 0), 1.0)
        shift = 1
        while shift < ROWS:
            inside = row < ROWS - shift
            d = d + c * jnp.where(inside, pltpu.roll(d, ROWS - shift, 0), 0.0)
            c = c * jnp.where(inside, pltpu.roll(c, ROWS - shift, 0), 1.0)
            shift *= 2
        dh = d + c * later
        dip = dh * (1.0 - forget) * (sig_in * (1.0 + ip * (1.0 - sig_in)))
        df = dh * (h_prev * keep - act_in)
        tail = df * (1.0 - sf)
        dfp = tail * (1.0 - lower) * sf
        grad_ref[rows, :] = jnp.concatenate([dip, dfp, dgp], axis=1).astype(bf16)
        sum_lower = sum_lower + jnp.sum(tail, axis=0, keepdims=True)
        return (e * dh)[0:1, :], sum_lower, sum_gain

    zero = jnp.zeros((1, chan), f32)
    _, sum_lower, sum_gain = lax.fori_loop(0, blocks, step, (zero, zero, zero))
    sums_ref[...] = jnp.concatenate([sum_lower, sum_gain], axis=0)


def kernel_call(kernel, outs, *args):
    vmem = pl.BlockSpec(memory_space=pltpu.VMEM)
    return pl.pallas_call(
        kernel,
        out_shape=outs,
        in_specs=[vmem] * len(args),
        out_specs=[vmem] * len(outs),
        compiler_params=pltpu.CompilerParams(vmem_limit_bytes=48 * 2**20),
    )(*args)


def gather_plane(v):
    return lax.all_gather(v, PLANE, axis=0, tiled=True)


def scatter_plane(part, n):
    got = lax.all_to_all(
        part.reshape(n, part.shape[0] // n, part.shape[1]), PLANE, split_axis=0, concat_axis=0, tiled=True
    )
    return jnp.sum(got.astype(f32), axis=0)


def dot(a, b):
    return jnp.dot(a, b, preferred_element_type=f32)


def dot_nt(a, b):
    return lax.dot_general(a, b, (((1,), (1,)), ((), ())), preferred_element_type=f32)


def dot_tn(a, b):
    return lax.dot_general(a, b, (((0,), (0,)), ((), ())), preferred_element_type=f32)


def body(
    tokens,
    cotangent,
    domain_tags,
    doc_ids,
    counts,
    w_in,
    w_forget,
    w_gate_out,
    w_out,
    ffn_gate,
    ffn_up,
    ffn_down,
    norm_gain,
    out_gain,
    ffn_gain,
    bound_logits,
):
    groups = lax.axis_size("g")
    members = lax.axis_size("p") * lax.axis_size("c")
    copies = lax.axis_size("x")
    ranks = members * copies
    rows, width = tokens.shape
    plane_rows = rows * ranks
    units = ffn_gate.shape[1]
    g, x = lax.axis_index("g"), lax.axis_index("x")
    rank = (lax.axis_index("p") * lax.axis_size("c") + lax.axis_index("c")) * copies + x
    ce = width // (groups * ranks)
    fe = units // (groups * ranks)
    chan, unit = ce * groups, fe * groups

    def columns(w, size):
        w = w.reshape(w.shape[0], groups, members, copies, size)
        w = lax.dynamic_index_in_dim(w, x, axis=3, keepdims=False)
        return jnp.moveaxis(w, 2, 0).reshape(members, w.shape[0], groups * size)

    def half_rows(w):
        half = w.shape[0] // copies
        return lax.dynamic_slice_in_dim(w, x * half, half, axis=0)

    def own_columns(v, size):
        v = v.reshape(groups, ranks, size)
        return lax.dynamic_index_in_dim(v, rank, axis=1, keepdims=False).reshape(1, groups * size)

    def gather_rows(v):
        return lax.all_gather(v, "g", axis=0, tiled=True)

    mix = jnp.concatenate([columns(w_in, ce), columns(w_forget, ce), columns(w_gate_out, ce)], axis=2)
    mix = lax.all_to_all(mix, ("p", "c"), split_axis=0, concat_axis=0, tiled=True)
    mix_w = gather_rows(mix.reshape(-1, 3 * chan))
    out_w = gather_rows(half_rows(w_out))
    ffn = jnp.concatenate([columns(ffn_gate, fe), columns(ffn_up, fe)], axis=2)
    ffn = lax.all_to_all(ffn, ("p", "c"), split_axis=0, concat_axis=0, tiled=True)
    ffn_w = gather_rows(ffn.reshape(-1, 2 * unit))
    down_w = gather_rows(half_rows(ffn_down))

    layer_count = bound_logits.shape[0]
    layer_probs = jax.nn.softmax(bound_logits, axis=0)
    layer_index = jnp.arange(layer_count, dtype=jnp.int32)
    layer_pick = ((layer_index >= 1) & (layer_index <= LAYER_AT)).astype(f32)[:, None]
    lower = jnp.sum(layer_probs * layer_pick, axis=0)
    lower = lax.all_gather(lower, "g", axis=0, tiled=True).reshape(1, chan)
    gain = own_columns(out_gain, ce)

    places = jnp.arange(doc_ids.shape[0], dtype=jnp.int32)
    previous = jnp.concatenate([doc_ids[:1], doc_ids[:-1]])
    keep = ((places % SEQ_LEN != 0) & (doc_ids == previous)).astype(f32)[:, None]
    keep = lax.dynamic_slice_in_dim(keep, g * plane_rows, plane_rows, axis=0)

    token_f = tokens.astype(f32)
    scale_one = lax.rsqrt(jnp.mean(token_f * token_f, axis=-1, keepdims=True) + EPS)
    normed_one = token_f * scale_one
    act_one_own = (normed_one * norm_gain).astype(bf16)

    domain_count = counts.shape[0]
    domain_hits = domain_tags[:, None] == jnp.arange(domain_count, dtype=jnp.int32)[None, :]
    per_token = jnp.sum(jnp.where(domain_hits, counts[None, :], 0), axis=1).astype(f32)
    seq_total = doc_ids.shape[0] // SEQ_LEN
    grad_z = cotangent.astype(f32) * (seq_total / (domain_count * per_token))[:, None]

    both = gather_plane(jnp.concatenate([act_one_own, grad_z.astype(bf16)], axis=1))
    act_one, grad_m = both[:, :width], both[:, width:]

    proj = dot(act_one, mix_w)
    states, mixed_raw, squares = kernel_call(
        functools.partial(forward_scan, chan),
        [
            jax.ShapeDtypeStruct((plane_rows, chan), f32),
            jax.ShapeDtypeStruct((plane_rows, chan), bf16),
            jax.ShapeDtypeStruct((plane_rows, 1), f32),
        ],
        proj,
        keep,
        lower,
        gain,
    )
    pad = jnp.zeros((plane_rows, 126), bf16)
    part = jnp.concatenate(
        [dot(mixed_raw, out_w).astype(bf16), *split_hi_lo(squares), pad], axis=1
    )
    total = scatter_plane(part, ranks)
    state_scale = lax.rsqrt((total[:, width : width + 1] + total[:, width + 1 : width + 2]) / width + EPS)
    branch = total[:, :width] * state_scale
    residual = token_f + branch
    scale_two = lax.rsqrt(jnp.mean(residual * residual, axis=-1, keepdims=True) + EPS)
    normed_two = residual * scale_two
    act_two = gather_plane((normed_two * ffn_gain).astype(bf16))

    pre = dot(act_two, ffn_w)
    gate_ffn, up_ffn = pre[:, :unit], pre[:, unit:]
    sig = jax.nn.sigmoid(gate_ffn)
    gate_silu = gate_ffn * sig
    hidden = (gate_silu * up_ffn).astype(bf16)
    down_part = dot(hidden, down_w).astype(bf16)
    grad_hidden = dot_nt(grad_m, down_w)
    grad_gate = (grad_hidden * up_ffn * (sig * (1.0 + gate_ffn * (1.0 - sig)))).astype(bf16)
    grad_up = (grad_hidden * gate_silu).astype(bf16)
    grad_pre = jnp.concatenate([grad_gate, grad_up], axis=1)
    back_part = dot_nt(grad_pre, ffn_w).astype(bf16)

    def scatter_rows(v):
        return lax.psum_scatter(v.astype(bf16), "g", scatter_dimension=0, tiled=True)

    ffn_sum = scatter_rows(jnp.concatenate([dot_tn(act_two, grad_pre), dot_tn(grad_m, hidden)], axis=1))

    back_term = scatter_plane(back_part, ranks)
    gain_two = jnp.sum(back_term * normed_two, axis=0)
    scaled_two = back_term * ffn_gain
    grad_resid = grad_z + scale_two * (
        scaled_two - normed_two * jnp.mean(scaled_two * normed_two, axis=-1, keepdims=True)
    )
    grad_branch_own = grad_resid.astype(bf16)
    mean_out = jnp.sum(grad_branch_own.astype(f32) * branch, axis=-1, keepdims=True) / width
    sent = jnp.concatenate(
        [
            grad_branch_own,
            *split_hi_lo(state_scale),
            *split_hi_lo(mean_out),
            jnp.zeros((rows, 124), bf16),
        ],
        axis=1,
    )
    got = gather_plane(sent)
    grad_branch = got[:, :width]
    info = got[:, width:].astype(f32)
    info = jnp.concatenate([info[:, 0:1] + info[:, 1:2], info[:, 2:3] + info[:, 3:4]], axis=1)
    grad_mixed = dot_nt(grad_branch, out_w)
    grad_proj, mixed_out, sums = kernel_call(
        functools.partial(backward_scan, chan),
        [
            jax.ShapeDtypeStruct((plane_rows, 3 * chan), bf16),
            jax.ShapeDtypeStruct((plane_rows, chan), bf16),
            jax.ShapeDtypeStruct((2, chan), f32),
        ],
        proj,
        states,
        grad_mixed,
        info,
        keep,
        lower,
        gain,
    )
    in_part = dot_nt(grad_proj, mix_w).astype(bf16)
    mix_sum = scatter_rows(dot_tn(act_one, grad_proj))
    summed_wout = scatter_rows(dot_tn(mixed_out, grad_branch)).astype(f32)
    down_term = scatter_plane(down_part, ranks)
    output_rows = (residual + down_term).astype(bf16)

    grad_act = scatter_plane(in_part, ranks)
    gain_one = jnp.sum(grad_act * normed_one, axis=0)
    scaled_one = grad_act * norm_gain
    grad_tokens = grad_resid + scale_one * (
        scaled_one - normed_one * jnp.mean(scaled_one * normed_one, axis=-1, keepdims=True)
    )

    def spread_rows(v):
        v = lax.all_to_all(
            v.reshape(ranks, -1, v.shape[1]), PLANE, split_axis=0, concat_axis=0, tiled=True
        )
        return v

    def whole_columns(v, size):
        v = v.reshape(ranks, v.shape[1], groups, size)
        return v.transpose(1, 2, 0, 3).reshape(v.shape[1], -1).astype(f32)

    ffn_rows = spread_rows(ffn_sum)
    summed_fgate = whole_columns(ffn_rows[:, :, :unit], fe)
    summed_fup = whole_columns(ffn_rows[:, :, unit : 2 * unit], fe)
    summed_fdown = whole_columns(ffn_rows[:, :, 2 * unit :], fe).T
    mix_rows = spread_rows(mix_sum)
    summed_win = whole_columns(mix_rows[:, :, :chan], ce)
    summed_wforget = whole_columns(mix_rows[:, :, chan : 2 * chan], ce)
    summed_wgate = whole_columns(mix_rows[:, :, 2 * chan :], ce)

    sums = sums.reshape(2, groups, ce).transpose(1, 0, 2)
    sums = lax.psum_scatter(sums, "g", scatter_dimension=0, tiled=True)[0]
    grad_lower, summed_outg = sums[0], sums[1]
    grad_probs = layer_pick * grad_lower[None, :]
    grad_bounds = layer_probs * (
        grad_probs - jnp.sum(layer_probs * grad_probs, axis=0, keepdims=True)
    )
    gains = jnp.stack([gain_one.reshape(-1, ce), gain_two.reshape(-1, ce)], axis=1)
    gains = lax.psum_scatter(gains, ALL, scatter_dimension=0, tiled=True)[0]
    return (
        output_rows,
        grad_tokens,
        summed_win,
        summed_wforget,
        summed_wgate,
        summed_wout,
        summed_fgate,
        summed_fup,
        summed_fdown,
        gains[0],
        summed_outg,
        gains[1],
        grad_bounds,
    )


def solution(mesh):
    seqs, copies = mesh.shape["seq"], mesh.shape["rep"]
    mesh = Mesh(mesh.devices.reshape(seqs // 4, 2, 2, copies), ALL)
    by_rows = P(ALL, None)
    by_seq = P(("g", "p", "c"), None)
    placed = (
        (by_rows, by_rows, P(ALL), P(), P()) + (by_seq,) * 7 + (P(), P(), P(), P(None, ALL))
    )
    return jax.shard_map(
        body,
        mesh=mesh,
        in_specs=placed,
        out_specs=(by_rows,) * 8 + (P(None, ALL),) + (P(ALL),) * 3 + (P(None, ALL),),
        check_vma=False,
    )
```

```python
import functools

import jax
import jax.numpy as jnp
from jax import lax
from jax.experimental import pallas as pl
from jax.experimental.pallas import tpu as pltpu
from jax.sharding import Mesh
from jax.sharding import PartitionSpec as P

LAYER_AT = 12
SEQ_LEN = 1024
EPS = 1e-06
ROWS = 16
PLANE = ("p", "c", "x")
ALL = ("g", "p", "c", "x")
f32 = jnp.float32
bf16 = jnp.bfloat16


def split_hi_lo(v):
    hi = v.astype(bf16)
    return hi, (v - hi.astype(f32)).astype(bf16)


def gates(proj, chan, lower):
    ip = proj[:, :chan].astype(bf16).astype(f32)
    sf = jax.nn.sigmoid(proj[:, chan : 2 * chan].astype(bf16).astype(f32))
    forget = lower + (1.0 - lower) * sf
    sig_in = jax.nn.sigmoid(ip)
    return ip, sig_in, sf, forget


def forward_scan(chan, proj_ref, keep_ref, lower_ref, gain_ref, h_ref, o_ref, ss_ref):
    lower = lower_ref[...]
    gain = gain_ref[...]
    row = lax.broadcasted_iota(jnp.int32, (ROWS, chan), 0)

    def step(i, carry):
        rows = pl.ds(pl.multiple_of(i * ROWS, ROWS), ROWS)
        proj = proj_ref[rows, :]
        ip, sig_in, _, forget = gates(proj, chan, lower)
        u = ip * sig_in * (1.0 - forget)
        e = forget * keep_ref[rows, :]
        shift = 1
        while shift < ROWS:
            u = u + e * jnp.where(row >= shift, pltpu.roll(u, shift, 0), 0.0)
            e = e * jnp.where(row >= shift, pltpu.roll(e, shift, 0), 1.0)
            shift *= 2
        h = u + e * carry
        h_ref[rows, :] = h
        hb = h.astype(bf16).astype(f32)
        gate = proj[:, 2 * chan :]
        o_ref[rows, :] = (hb * gain * (gate * jax.nn.sigmoid(gate))).astype(bf16)
        ss_ref[rows, :] = jnp.sum(hb * hb, axis=1, keepdims=True)
        return h[ROWS - 1 : ROWS, :]

    lax.fori_loop(0, proj_ref.shape[0] // ROWS, step, jnp.zeros((1, chan), f32))


def backward_scan(
    chan, proj_ref, h_ref, do_ref, info_ref, keep_ref, lower_ref, gain_ref, grad_ref, o_ref, sums_ref
):
    lower = lower_ref[...]
    gain = gain_ref[...]
    row = lax.broadcasted_iota(jnp.int32, (ROWS, chan), 0)
    blocks = proj_ref.shape[0] // ROWS

    def step(j, carried):
        later, sum_lower = carried
        i = blocks - 1 - j
        rows = pl.ds(pl.multiple_of(i * ROWS, ROWS), ROWS)
        proj = proj_ref[rows, :]
        ip, sig_in, sf, forget = gates(proj, chan, lower)
        keep = keep_ref[rows, :]
        act_in = ip * sig_in
        h = h_ref[rows, :]
        before = h_ref[pl.ds(pl.multiple_of(jnp.maximum(i * ROWS - 8, 0), 8), 8), :][7:8, :]
        h_prev = jnp.where(row >= 1, pltpu.roll(h, 1, 0), before)
        scale = info_ref[rows, 0:1]
        mean = info_ref[rows, 1:2]
        hn = h.astype(bf16).astype(f32) * scale
        gate = proj[:, 2 * chan :]
        sig_gate = jax.nn.sigmoid(gate)
        gate_act = gate * sig_gate
        do = do_ref[rows, :]
        o_ref[rows, :] = (hn * gain * gate_act).astype(bf16)
        dgp = do * hn * gain * (sig_gate * (1.0 + gate * (1.0 - sig_gate)))
        dhb = scale * (do * gain * gate_act - hn * mean)
        d = dhb.astype(bf16).astype(f32)
        e = forget * keep
        c = jnp.where(row < ROWS - 1, pltpu.roll(e, ROWS - 1, 0), 1.0)
        shift = 1
        while shift < ROWS:
            inside = row < ROWS - shift
            d = d + c * jnp.where(inside, pltpu.roll(d, ROWS - shift, 0), 0.0)
            c = c * jnp.where(inside, pltpu.roll(c, ROWS - shift, 0), 1.0)
            shift *= 2
        dh = d + c * later
        dip = dh * (1.0 - forget) * (sig_in * (1.0 + ip * (1.0 - sig_in)))
        df = dh * (h_prev * keep - act_in)
        tail = df * (1.0 - sf)
        dfp = tail * (1.0 - lower) * sf
        grad_ref[rows, :] = jnp.concatenate([dip, dfp, dgp], axis=1).astype(bf16)
        sum_lower = sum_lower + jnp.sum(tail, axis=0, keepdims=True)
        return (e * dh)[0:1, :], sum_lower

    zero = jnp.zeros((1, chan), f32)
    _, sum_lower = lax.fori_loop(0, blocks, step, (zero, zero))
    sums_ref[...] = sum_lower


def kernel_call(kernel, outs, *args):
    vmem = pl.BlockSpec(memory_space=pltpu.VMEM)
    return pl.pallas_call(
        kernel,
        out_shape=outs,
        in_specs=[vmem] * len(args),
        out_specs=[vmem] * len(outs),
        compiler_params=pltpu.CompilerParams(vmem_limit_bytes=48 * 2**20),
    )(*args)


MESH = pl.DeviceIdType.MESH


def places():
    g, p, c, x = (lax.axis_index(a) for a in ALL)
    flips = ((1, 1), (0, 1), (1, 0), (0, 0))
    chips = [(g, p + dp * (1 - 2 * p), x + dx * (1 - 2 * x)) for dp, dx in flips]
    return chips, c


def device_at(chip, core):
    return (chip[0], chip[1], core, chip[2])


def rank_at(chip, core):
    return (chip[1] * 2 + core) * 2 + chip[2]


def greet(partners):
    barrier = pltpu.get_barrier_semaphore()
    for partner in partners:
        pl.semaphore_signal(barrier, inc=1, device_id=partner, device_id_type=MESH)
    pl.semaphore_wait(barrier, len(partners))


def remote(src, dst, send_sem, recv_sem, device):
    copy = pltpu.make_async_remote_copy(
        src_ref=src, dst_ref=dst, send_sem=send_sem, recv_sem=recv_sem, device_id=device, device_id_type=MESH
    )
    copy.start()
    return copy


def gather_kernel(own_ref, out_ref, local_sem, send_sem, recv_sem):
    chips, core = places()
    here = chips[3]
    sibling = device_at(here, 1 - core)
    greet([device_at(chip, core) for chip in chips[:3]] + [sibling])
    slot = out_ref.at[rank_at(here, core)]
    local = pltpu.make_async_copy(own_ref, slot, local_sem)
    local.start()
    direct = [
        remote(own_ref, slot, send_sem.at[i], recv_sem.at[i], device_at(chips[i], core)) for i in range(3)
    ]
    passed = [remote(own_ref, slot, send_sem.at[3], recv_sem.at[3], sibling)]
    for i in (1, 2, 0):
        direct[i].wait_recv()
        got = out_ref.at[rank_at(chips[i], core)]
        passed.append(remote(got, got, send_sem.at[4 + i], recv_sem.at[4 + i], sibling))
    for copy in direct:
        copy.wait_send()
    for copy in passed:
        copy.wait()
    local.wait()


def scatter_kernel(part_ref, out_ref, mine, theirs, outgoing, landing, local_sem, send_sem, recv_sem):
    chips, core = places()
    sibling = device_at(chips[3], 1 - core)
    greet([device_at(chip, core) for chip in chips[:3]] + [sibling])
    swaps, locals_ = [], []
    for j, chip in enumerate(chips):
        swaps.append(
            remote(
                part_ref.at[rank_at(chip, 1 - core)], theirs.at[j], send_sem.at[j], recv_sem.at[j], sibling
            )
        )
        local = pltpu.make_async_copy(part_ref.at[rank_at(chip, core)], mine.at[j], local_sem.at[j])
        local.start()
        locals_.append(local)
    steps = out_ref.shape[0] // ROWS
    sent = []
    for j in range(4):
        locals_[j].wait()
        swaps[j].wait_recv()

        def add(i, _, j=j):
            rows = pl.ds(pl.multiple_of(i * ROWS, ROWS), ROWS)
            total = mine[j, rows, :].astype(f32) + theirs[j, rows, :].astype(f32)
            if j < 3:
                outgoing[j, rows, :] = total.astype(bf16)
            else:
                out_ref[rows, :] = total
            return 0

        lax.fori_loop(0, steps, add, 0)
        if j < 3:
            sent.append(
                remote(
                    outgoing.at[j],
                    landing.at[j],
                    send_sem.at[4 + j],
                    recv_sem.at[4 + j],
                    device_at(chips[j], core),
                )
            )
    for copy in sent:
        copy.wait_recv()

    def finish(i, _):
        rows = pl.ds(pl.multiple_of(i * ROWS, ROWS), ROWS)
        total = out_ref[rows, :]
        for j in range(3):
            total = total + landing[j, rows, :].astype(f32)
        out_ref[rows, :] = total
        return 0

    lax.fori_loop(0, steps, finish, 0)
    for copy in swaps + sent:
        copy.wait_send()


def gather_plane(v, ident):
    hbm = pl.BlockSpec(memory_space=pl.ANY)
    out = pl.pallas_call(
        gather_kernel,
        out_shape=jax.ShapeDtypeStruct((8,) + v.shape, v.dtype),
        in_specs=[hbm],
        out_specs=hbm,
        scratch_shapes=[
            pltpu.SemaphoreType.DMA,
            pltpu.SemaphoreType.DMA((7,)),
            pltpu.SemaphoreType.DMA((7,)),
        ],
        compiler_params=pltpu.CompilerParams(
            collective_id=ident, has_side_effects=True, vmem_limit_bytes=48 * 2**20
        ),
    )(v)
    return out.reshape(-1, v.shape[1])


def scatter_plane(part, ident):
    rows, wide = part.shape[0] // 8, part.shape[1]
    return pl.pallas_call(
        scatter_kernel,
        out_shape=jax.ShapeDtypeStruct((rows, wide), f32),
        in_specs=[pl.BlockSpec(memory_space=pl.ANY)],
        out_specs=pl.BlockSpec(memory_space=pltpu.VMEM),
        scratch_shapes=[
            pltpu.VMEM((4, rows, wide), bf16),
            pltpu.VMEM((4, rows, wide), bf16),
            pltpu.VMEM((3, rows, wide), bf16),
            pltpu.VMEM((3, rows, wide), bf16),
            pltpu.SemaphoreType.DMA((4,)),
            pltpu.SemaphoreType.DMA((7,)),
            pltpu.SemaphoreType.DMA((7,)),
        ],
        compiler_params=pltpu.CompilerParams(
            collective_id=ident, has_side_effects=True, vmem_limit_bytes=48 * 2**20
        ),
    )(part.reshape(8, rows, wide))


def dot(a, b):
    return jnp.dot(a, b, preferred_element_type=f32)


def dot_nt(a, b):
    return lax.dot_general(a, b, (((1,), (1,)), ((), ())), preferred_element_type=f32)


def dot_tn(a, b):
    return lax.dot_general(a, b, (((0,), (0,)), ((), ())), preferred_element_type=f32)


def body(
    tokens,
    cotangent,
    domain_tags,
    doc_ids,
    counts,
    w_in,
    w_forget,
    w_gate_out,
    w_out,
    ffn_gate,
    ffn_up,
    ffn_down,
    norm_gain,
    out_gain,
    ffn_gain,
    bound_logits,
):
    groups = lax.axis_size("g")
    members = lax.axis_size("p") * lax.axis_size("c")
    copies = lax.axis_size("x")
    ranks = members * copies
    rows, width = tokens.shape
    plane_rows = rows * ranks
    units = ffn_gate.shape[1]
    g, x = lax.axis_index("g"), lax.axis_index("x")
    rank = (lax.axis_index("p") * lax.axis_size("c") + lax.axis_index("c")) * copies + x
    ce = width // (groups * ranks)
    fe = units // (groups * ranks)
    chan, unit = ce * groups, fe * groups

    def columns(w, size):
        w = w.reshape(w.shape[0], groups, members, copies, size)
        w = lax.dynamic_index_in_dim(w, x, axis=3, keepdims=False)
        return jnp.moveaxis(w, 2, 0).reshape(members, w.shape[0], groups * size)

    def half_rows(w):
        half = w.shape[0] // copies
        return lax.dynamic_slice_in_dim(w, x * half, half, axis=0)

    def own_columns(v, size):
        v = v.reshape(groups, ranks, size)
        return lax.dynamic_index_in_dim(v, rank, axis=1, keepdims=False).reshape(1, groups * size)

    def gather_rows(v):
        return lax.all_gather(v, "g", axis=0, tiled=True)

    mix = jnp.concatenate([columns(w_in, ce), columns(w_forget, ce), columns(w_gate_out, ce)], axis=2)
    mix = lax.all_to_all(mix, ("p", "c"), split_axis=0, concat_axis=0, tiled=True)
    mix_w = gather_rows(mix.reshape(-1, 3 * chan))
    layer_count = bound_logits.shape[0]
    layer_probs = jax.nn.softmax(bound_logits, axis=0)
    layer_index = jnp.arange(layer_count, dtype=jnp.int32)
    layer_pick = ((layer_index >= 1) & (layer_index <= LAYER_AT)).astype(f32)[:, None]
    own_lower = jnp.sum(layer_probs * layer_pick, axis=0)[:, None]
    top, rest = split_hi_lo(own_lower)
    out_ext = gather_rows(
        jnp.concatenate(
            [
                half_rows(w_out),
                top,
                rest,
                (own_lower - top.astype(f32) - rest.astype(f32)).astype(bf16),
                jnp.zeros((ce, 125), bf16),
            ],
            axis=1,
        )
    )
    out_w = out_ext[:, :width]
    lower = jnp.sum(out_ext[:, width : width + 3].astype(f32), axis=1).reshape(1, chan)
    ffn = jnp.concatenate([columns(ffn_gate, fe), columns(ffn_up, fe)], axis=2)
    ffn = lax.all_to_all(ffn, ("p", "c"), split_axis=0, concat_axis=0, tiled=True)
    ffn_w = gather_rows(ffn.reshape(-1, 2 * unit))
    down_w = gather_rows(half_rows(ffn_down))

    gain = own_columns(out_gain, ce)

    places = jnp.arange(doc_ids.shape[0], dtype=jnp.int32)
    previous = jnp.concatenate([doc_ids[:1], doc_ids[:-1]])
    keep = ((places % SEQ_LEN != 0) & (doc_ids == previous)).astype(f32)[:, None]
    keep = lax.dynamic_slice_in_dim(keep, g * plane_rows, plane_rows, axis=0)

    token_f = tokens.astype(f32)
    scale_one = lax.rsqrt(jnp.mean(token_f * token_f, axis=-1, keepdims=True) + EPS)
    normed_one = token_f * scale_one
    act_one_own = (normed_one * norm_gain).astype(bf16)

    domain_count = counts.shape[0]
    domain_hits = domain_tags[:, None] == jnp.arange(domain_count, dtype=jnp.int32)[None, :]
    per_token = jnp.sum(jnp.where(domain_hits, counts[None, :], 0), axis=1).astype(f32)
    seq_total = doc_ids.shape[0] // SEQ_LEN
    grad_z = cotangent.astype(f32) * (seq_total / (domain_count * per_token))[:, None]

    both = gather_plane(jnp.concatenate([act_one_own, grad_z.astype(bf16)], axis=1), 0)
    act_one, grad_m = both[:, :width], both[:, width:]

    proj = dot(act_one, mix_w)
    states, mixed_raw, squares = kernel_call(
        functools.partial(forward_scan, chan),
        [
            jax.ShapeDtypeStruct((plane_rows, chan), f32),
            jax.ShapeDtypeStruct((plane_rows, chan), bf16),
            jax.ShapeDtypeStruct((plane_rows, 1), f32),
        ],
        proj,
        keep,
        lower,
        gain,
    )
    pad = jnp.zeros((plane_rows, 126), bf16)
    part = jnp.concatenate(
        [dot(mixed_raw, out_w).astype(bf16), *split_hi_lo(squares), pad], axis=1
    )
    total = scatter_plane(part, 1)
    state_scale = lax.rsqrt((total[:, width : width + 1] + total[:, width + 1 : width + 2]) / width + EPS)
    branch = total[:, :width] * state_scale
    residual = token_f + branch
    scale_two = lax.rsqrt(jnp.mean(residual * residual, axis=-1, keepdims=True) + EPS)
    normed_two = residual * scale_two
    act_two = gather_plane((normed_two * ffn_gain).astype(bf16), 2)

    pre = dot(act_two, ffn_w)
    gate_ffn, up_ffn = pre[:, :unit], pre[:, unit:]
    sig = jax.nn.sigmoid(gate_ffn)
    gate_silu = gate_ffn * sig
    hidden = (gate_silu * up_ffn).astype(bf16)
    down_part = dot(hidden, down_w).astype(bf16)
    grad_hidden = dot_nt(grad_m, down_w)
    grad_gate = (grad_hidden * up_ffn * (sig * (1.0 + gate_ffn * (1.0 - sig)))).astype(bf16)
    grad_up = (grad_hidden * gate_silu).astype(bf16)
    grad_pre = jnp.concatenate([grad_gate, grad_up], axis=1)
    back_part = dot_nt(grad_pre, ffn_w).astype(bf16)

    def scatter_rows(v):
        return lax.psum_scatter(v.astype(bf16), "g", scatter_dimension=0, tiled=True)

    ffn_grads = jnp.concatenate([dot_tn(act_two, grad_pre), dot_tn(grad_m, hidden)], axis=1).astype(bf16)
    ffn_grads, back_part = lax.optimization_barrier((ffn_grads, back_part))
    ffn_sum = scatter_rows(ffn_grads)

    back_term = scatter_plane(back_part, 3)
    scaled_two = back_term * ffn_gain
    grad_resid = grad_z + scale_two * (
        scaled_two - normed_two * jnp.mean(scaled_two * normed_two, axis=-1, keepdims=True)
    )
    grad_branch_own = grad_resid.astype(bf16)
    mean_out = jnp.sum(grad_branch_own.astype(f32) * branch, axis=-1, keepdims=True) / width
    sent = jnp.concatenate(
        [
            grad_branch_own,
            *split_hi_lo(state_scale),
            *split_hi_lo(mean_out),
            jnp.zeros((rows, 124), bf16),
        ],
        axis=1,
    )
    got = gather_plane(sent, 4)
    grad_branch = got[:, :width]
    info = got[:, width:].astype(f32)
    info = jnp.concatenate([info[:, 0:1] + info[:, 1:2], info[:, 2:3] + info[:, 3:4]], axis=1)
    grad_mixed = dot_nt(grad_branch, out_w)
    grad_proj, mixed_out, sums = kernel_call(
        functools.partial(backward_scan, chan),
        [
            jax.ShapeDtypeStruct((plane_rows, 3 * chan), bf16),
            jax.ShapeDtypeStruct((plane_rows, chan), bf16),
            jax.ShapeDtypeStruct((1, chan), f32),
        ],
        proj,
        states,
        grad_mixed,
        info,
        keep,
        lower,
        gain,
    )
    in_part = dot_nt(grad_proj, mix_w).astype(bf16)
    mix_grads = dot_tn(act_one, grad_proj).astype(bf16).reshape(groups, -1, 3 * chan)
    top, rest = split_hi_lo(sums.reshape(chan, 1))
    out_grads = jnp.concatenate(
        [dot_tn(mixed_out, grad_branch).astype(bf16), top, rest, jnp.zeros((chan, 3 * chan - 2), bf16)],
        axis=1,
    )
    folds = out_grads.shape[1] // (3 * chan)
    out_grads = out_grads[:, : folds * 3 * chan].reshape(groups, ce, folds, 3 * chan)
    out_grads = jnp.moveaxis(out_grads, 2, 1).reshape(groups, folds * ce, 3 * chan)
    late_grads = jnp.concatenate([mix_grads, out_grads], axis=1).reshape(-1, 3 * chan)
    late_grads, ffn_sum = lax.optimization_barrier((late_grads, ffn_sum))
    late_sum = scatter_rows(late_grads)
    mix_sum = late_sum[: width // groups]
    out_sum = jnp.moveaxis(late_sum[width // groups :].reshape(folds, ce, 3 * chan), 1, 0)
    out_sum = out_sum.reshape(ce, -1).astype(f32)
    summed_wout = out_sum[:, :width]
    grad_lower = out_sum[:, width] + out_sum[:, width + 1]
    down_term = scatter_plane(down_part, 5)
    output_rows = (residual + down_term).astype(bf16)

    grad_act = scatter_plane(in_part, 6)
    scaled_one = grad_act * norm_gain
    grad_tokens = grad_resid + scale_one * (
        scaled_one - normed_one * jnp.mean(scaled_one * normed_one, axis=-1, keepdims=True)
    )

    def spread_rows(v):
        v = lax.all_to_all(
            v.reshape(ranks, -1, v.shape[1]), PLANE, split_axis=0, concat_axis=0, tiled=True
        )
        return v

    def whole_columns(v, size):
        v = v.reshape(ranks, v.shape[1], groups, size)
        return v.transpose(1, 2, 0, 3).reshape(v.shape[1], -1).astype(f32)

    ffn_rows = spread_rows(ffn_sum)
    summed_fgate = whole_columns(ffn_rows[:, :, :unit], fe)
    summed_fup = whole_columns(ffn_rows[:, :, unit : 2 * unit], fe)
    summed_fdown = whole_columns(ffn_rows[:, :, 2 * unit :], fe).T
    mix_rows = spread_rows(mix_sum)
    summed_win = whole_columns(mix_rows[:, :, :chan], ce)
    summed_wforget = whole_columns(mix_rows[:, :, chan : 2 * chan], ce)
    summed_wgate = whole_columns(mix_rows[:, :, 2 * chan :], ce)

    first = (g * ranks + rank) * ce

    def own_gain(gain, pairs):
        total = sum(jnp.sum(grad * half_rows(w).astype(f32), axis=1) for grad, w in pairs)
        return total / lax.dynamic_slice_in_dim(gain, first, ce, axis=0)

    summed_norm = own_gain(
        norm_gain, ((summed_win, w_in), (summed_wforget, w_forget), (summed_wgate, w_gate_out))
    )
    summed_outg = own_gain(out_gain, ((summed_wout, w_out),))
    summed_ffng = own_gain(ffn_gain, ((summed_fgate, ffn_gate), (summed_fup, ffn_up)))
    grad_probs = layer_pick * grad_lower[None, :]
    grad_bounds = layer_probs * (
        grad_probs - jnp.sum(layer_probs * grad_probs, axis=0, keepdims=True)
    )
    return (
        output_rows,
        grad_tokens,
        summed_win,
        summed_wforget,
        summed_wgate,
        summed_wout,
        summed_fgate,
        summed_fup,
        summed_fdown,
        summed_norm,
        summed_outg,
        summed_ffng,
        grad_bounds,
    )


def solution(mesh):
    seqs, copies = mesh.shape["seq"], mesh.shape["rep"]
    mesh = Mesh(mesh.devices.reshape(seqs // 4, 2, 2, copies), ALL)
    by_rows = P(ALL, None)
    by_seq = P(("g", "p", "c"), None)
    placed = (
        (by_rows, by_rows, P(ALL), P(), P()) + (by_seq,) * 7 + (P(), P(), P(), P(None, ALL))
    )
    return jax.shard_map(
        body,
        mesh=mesh,
        in_specs=placed,
        out_specs=(by_rows,) * 8 + (P(None, ALL),) + (P(ALL),) * 3 + (P(None, ALL),),
        check_vma=False,
    )
```

```python
import functools

import jax
import jax.numpy as jnp
from jax import lax
from jax.experimental import pallas as pl
from jax.experimental.pallas import tpu as pltpu
from jax.sharding import Mesh
from jax.sharding import PartitionSpec as P

LAYER_AT = 12
SEQ_LEN = 1024
EPS = 1e-06
ROWS = 16
HALVES = 2
PLANE = ("p", "c", "x")
ALL = ("g", "p", "c", "x")
f32 = jnp.float32
bf16 = jnp.bfloat16


def split_hi_lo(v):
    hi = v.astype(bf16)
    return hi, (v - hi.astype(f32)).astype(bf16)


def gates(proj, chan, lower):
    ip = proj[:, :chan].astype(bf16).astype(f32)
    sf = jax.nn.sigmoid(proj[:, chan : 2 * chan].astype(bf16).astype(f32))
    forget = lower + (1.0 - lower) * sf
    sig_in = jax.nn.sigmoid(ip)
    return ip, sig_in, sf, forget


def forward_scan(chan, proj_ref, keep_ref, lower_ref, gain_ref, h_ref, o_ref, ss_ref):
    lower = lower_ref[...]
    gain = gain_ref[...]
    row = lax.broadcasted_iota(jnp.int32, (ROWS, chan), 0)

    def step(i, carry):
        rows = pl.ds(pl.multiple_of(i * ROWS, ROWS), ROWS)
        proj = proj_ref[rows, :]
        ip, sig_in, _, forget = gates(proj, chan, lower)
        u = ip * sig_in * (1.0 - forget)
        e = forget * keep_ref[rows, :]
        shift = 1
        while shift < ROWS:
            u = u + e * jnp.where(row >= shift, pltpu.roll(u, shift, 0), 0.0)
            e = e * jnp.where(row >= shift, pltpu.roll(e, shift, 0), 1.0)
            shift *= 2
        h = u + e * carry
        h_ref[rows, :] = h
        hb = h.astype(bf16).astype(f32)
        gate = proj[:, 2 * chan :]
        o_ref[rows, :] = (hb * gain * (gate * jax.nn.sigmoid(gate))).astype(bf16)
        ss_ref[rows, :] = jnp.sum(hb * hb, axis=1, keepdims=True)
        return h[ROWS - 1 : ROWS, :]

    lax.fori_loop(0, proj_ref.shape[0] // ROWS, step, jnp.zeros((1, chan), f32))


def backward_scan(
    chan, proj_ref, h_ref, do_ref, info_ref, keep_ref, lower_ref, gain_ref, grad_ref, o_ref, sums_ref
):
    lower = lower_ref[...]
    gain = gain_ref[...]
    row = lax.broadcasted_iota(jnp.int32, (ROWS, chan), 0)
    blocks = proj_ref.shape[0] // ROWS

    def step(j, carried):
        later, sum_lower = carried
        i = blocks - 1 - j
        rows = pl.ds(pl.multiple_of(i * ROWS, ROWS), ROWS)
        proj = proj_ref[rows, :]
        ip, sig_in, sf, forget = gates(proj, chan, lower)
        keep = keep_ref[rows, :]
        act_in = ip * sig_in
        h = h_ref[rows, :]
        before = h_ref[pl.ds(pl.multiple_of(jnp.maximum(i * ROWS - 8, 0), 8), 8), :][7:8, :]
        h_prev = jnp.where(row >= 1, pltpu.roll(h, 1, 0), before)
        scale = info_ref[rows, 0:1]
        mean = info_ref[rows, 1:2]
        hn = h.astype(bf16).astype(f32) * scale
        gate = proj[:, 2 * chan :]
        sig_gate = jax.nn.sigmoid(gate)
        gate_act = gate * sig_gate
        do = do_ref[rows, :]
        o_ref[rows, :] = (hn * gain * gate_act).astype(bf16)
        dgp = do * hn * gain * (sig_gate * (1.0 + gate * (1.0 - sig_gate)))
        dhb = scale * (do * gain * gate_act - hn * mean)
        d = dhb.astype(bf16).astype(f32)
        e = forget * keep
        c = jnp.where(row < ROWS - 1, pltpu.roll(e, ROWS - 1, 0), 1.0)
        shift = 1
        while shift < ROWS:
            inside = row < ROWS - shift
            d = d + c * jnp.where(inside, pltpu.roll(d, ROWS - shift, 0), 0.0)
            c = c * jnp.where(inside, pltpu.roll(c, ROWS - shift, 0), 1.0)
            shift *= 2
        dh = d + c * later
        dip = dh * (1.0 - forget) * (sig_in * (1.0 + ip * (1.0 - sig_in)))
        df = dh * (h_prev * keep - act_in)
        tail = df * (1.0 - sf)
        dfp = tail * (1.0 - lower) * sf
        grad_ref[rows, :] = jnp.concatenate([dip, dfp, dgp], axis=1).astype(bf16)
        sum_lower = sum_lower + jnp.sum(tail, axis=0, keepdims=True)
        return (e * dh)[0:1, :], sum_lower

    zero = jnp.zeros((1, chan), f32)
    _, sum_lower = lax.fori_loop(0, blocks, step, (zero, zero))
    sums_ref[...] = sum_lower


def kernel_call(kernel, outs, *args):
    vmem = pl.BlockSpec(memory_space=pltpu.VMEM)
    return pl.pallas_call(
        kernel,
        out_shape=outs,
        in_specs=[vmem] * len(args),
        out_specs=[vmem] * len(outs),
        compiler_params=pltpu.CompilerParams(vmem_limit_bytes=48 * 2**20),
    )(*args)


MESH = pl.DeviceIdType.MESH


def places():
    g, p, c, x = (lax.axis_index(a) for a in ALL)
    flips = ((1, 1), (0, 1), (1, 0), (0, 0))
    chips = [(g, p + dp * (1 - 2 * p), x + dx * (1 - 2 * x)) for dp, dx in flips]
    return chips, c


def device_at(chip, core):
    return (chip[0], chip[1], core, chip[2])


def rank_at(chip, core):
    return (chip[1] * 2 + core) * 2 + chip[2]


def greet(partners):
    barrier = pltpu.get_barrier_semaphore()
    for partner in partners:
        pl.semaphore_signal(barrier, inc=1, device_id=partner, device_id_type=MESH)
    pl.semaphore_wait(barrier, len(partners))


def remote(src, dst, send_sem, recv_sem, device):
    copy = pltpu.make_async_remote_copy(
        src_ref=src, dst_ref=dst, send_sem=send_sem, recv_sem=recv_sem, device_id=device, device_id_type=MESH
    )
    copy.start()
    return copy


def gather_kernel(own_ref, out_ref, local_sem, send_sem, recv_sem):
    chips, core = places()
    here = chips[3]
    sibling = device_at(here, 1 - core)
    greet([device_at(chip, core) for chip in chips[:3]] + [sibling])
    slot = out_ref.at[rank_at(here, core)]
    local = pltpu.make_async_copy(own_ref, slot, local_sem)
    local.start()
    direct = [
        remote(own_ref, slot, send_sem.at[i], recv_sem.at[i], device_at(chips[i], core)) for i in range(3)
    ]
    passed = [remote(own_ref, slot, send_sem.at[3], recv_sem.at[3], sibling)]
    for i in (1, 2, 0):
        direct[i].wait_recv()
        got = out_ref.at[rank_at(chips[i], core)]
        passed.append(remote(got, got, send_sem.at[4 + i], recv_sem.at[4 + i], sibling))
    for copy in direct:
        copy.wait_send()
    for copy in passed:
        copy.wait()
    local.wait()


class Line:
    def __init__(self, groups, own_ref, out_ref, send_sem, recv_sem):
        self.groups, self.own, self.out = groups, own_ref, out_ref
        self.send_sem, self.recv_sem = send_sem, recv_sem
        self.g, self.p, self.c, self.x = (lax.axis_index(a) for a in ALL)

    def at_step(self, way, k):
        block = self.g - (k - 1) if way == 0 else self.g + (k - 1)
        return pltpu.make_async_remote_copy(
            src_ref=self.own if k == 1 else self.out.at[block],
            dst_ref=self.out.at[block],
            send_sem=self.send_sem.at[way, k - 1],
            recv_sem=self.recv_sem.at[way, k - 1],
            device_id=(self.g + (1 if way == 0 else -1), self.p, self.c, self.x),
            device_id_type=MESH,
        )

    def behind(self, way, k):
        return self.g >= k if way == 0 else self.g + k < self.groups

    def sends(self, way, k):
        return self.behind(way, k - 1) & self.behind(1 - way, 1)

    def send(self, k):
        for way in (0, 1):

            @pl.when(self.sends(way, k))
            def _(way=way):
                self.at_step(way, k).start()

    def step(self, k):
        for way in (0, 1):

            @pl.when(self.behind(way, k))
            def _(way=way):
                block = self.g - k if way == 0 else self.g + k
                got = self.out.at[block]
                pltpu.make_async_remote_copy(
                    src_ref=got,
                    dst_ref=got,
                    send_sem=self.send_sem.at[way, k - 1],
                    recv_sem=self.recv_sem.at[way, k - 1],
                    device_id=(self.g, self.p, self.c, self.x),
                    device_id_type=MESH,
                ).wait_recv()

        if k + 1 < self.groups:
            self.send(k + 1)

    def finish(self):
        for k in range(1, self.groups):
            for way in (0, 1):

                @pl.when(self.sends(way, k))
                def _(way=way, k=k):
                    self.at_step(way, k).wait_send()


def line_partners(groups):
    g, p, c, x = (lax.axis_index(a) for a in ALL)
    offsets = sorted({1 % groups, -1 % groups} - {0})
    return [(lax.rem(g + k, groups), p, c, x) for k in offsets]


class Plane:
    def __init__(self, own_ref, out_ref, local_sem, send_sem, recv_sem):
        self.own, self.out = own_ref, out_ref
        self.send_sem, self.recv_sem = send_sem, recv_sem
        self.chips, self.core = places()
        self.slot = out_ref.at[rank_at(self.chips[3], self.core)]
        self.sibling = device_at(self.chips[3], 1 - self.core)
        self.local = pltpu.make_async_copy(own_ref, self.slot, local_sem)
        self.direct, self.passed = {}, []

    def start_own(self):
        self.local.start()
        self.passed.append(
            remote(self.own, self.slot, self.send_sem.at[3], self.recv_sem.at[3], self.sibling)
        )

    def start(self, i):
        self.direct[i] = remote(
            self.own, self.slot, self.send_sem.at[i], self.recv_sem.at[i], device_at(self.chips[i], self.core)
        )

    def hand_on(self, i):
        self.direct[i].wait_recv()
        got = self.out.at[rank_at(self.chips[i], self.core)]
        self.passed.append(remote(got, got, self.send_sem.at[4 + i], self.recv_sem.at[4 + i], self.sibling))

    def finish(self):
        for copy in self.direct.values():
            copy.wait_send()
        for copy in self.passed:
            copy.wait()
        self.local.wait()


def spread_kernel(
    groups,
    mix_ref,
    ffn_ref,
    out_ref,
    act_ref,
    grad_ref,
    mix_all,
    ffn_all,
    out_all,
    act_all,
    grad_all,
    local_sem,
    swap_send,
    swap_recv,
    mix_send,
    mix_recv,
    out_send,
    out_recv,
    act_send,
    act_recv,
    grad_send,
    grad_recv,
):
    chips, core = places()
    here, other = chips[3], chips[2]
    g = here[0]
    swaps = [device_at(here, 1 - core), device_at(other, core), device_at(other, 1 - core)]
    greet([device_at(chip, core) for chip in chips[:3]] + [swaps[0], swaps[2]] + line_partners(groups))
    own = here[1] * 2 + core
    targets = [here[1] * 2 + 1 - core, other[1] * 2 + core, other[1] * 2 + 1 - core]

    def swap(src, dst, first):
        return [
            remote(
                src.at[targets[i]], dst, swap_send.at[first + i], swap_recv.at[first + i], swaps[i]
            )
            for i in range(3)
        ]

    mix_copies = swap(mix_ref, mix_all.at[g, own], 0)
    locals_ = [
        pltpu.make_async_copy(mix_ref.at[own], mix_all.at[g, own], local_sem.at[0]),
        pltpu.make_async_copy(ffn_ref.at[own], ffn_all.at[own], local_sem.at[1]),
        pltpu.make_async_copy(out_ref, out_all.at[g], local_sem.at[2]),
    ]
    for copy in locals_:
        copy.start()
    out_line = Line(groups, out_ref, out_all, out_send, out_recv)
    mix_line = Line(groups, mix_all.at[g], mix_all, mix_send, mix_recv)
    out_line.send(1)
    act = Plane(act_ref, act_all, local_sem.at[3], act_send, act_recv)
    grad = Plane(grad_ref, grad_all, local_sem.at[4], grad_send, grad_recv)
    act.start_own()
    grad.start_own()
    act.start(1)
    for copy in mix_copies:
        copy.wait()
    locals_[0].wait()
    mix_line.send(1)
    act.start(2)
    act.start(0)
    ffn_copies = swap(ffn_ref, ffn_all.at[own], 3)
    out_line.step(1)
    for i in (1, 2, 0):
        grad.start(i)
    mix_line.step(1)
    for i in (1, 2, 0):
        act.hand_on(i)
    for k in range(2, groups):
        out_line.step(k)
        mix_line.step(k)
    for i in (1, 2, 0):
        grad.hand_on(i)
    for copy in ffn_copies:
        copy.wait()
    locals_[1].wait()
    locals_[2].wait()
    out_line.finish()
    mix_line.finish()
    act.finish()
    grad.finish()


def spread(groups, mix, ffn, out, act, grad, ident):
    hbm = pl.BlockSpec(memory_space=pl.ANY)
    dma = pltpu.SemaphoreType.DMA
    return pl.pallas_call(
        functools.partial(spread_kernel, groups),
        out_shape=[
            jax.ShapeDtypeStruct((groups,) + mix.shape, bf16),
            jax.ShapeDtypeStruct(ffn.shape, bf16),
            jax.ShapeDtypeStruct((groups,) + out.shape, bf16),
            jax.ShapeDtypeStruct((8,) + act.shape, bf16),
            jax.ShapeDtypeStruct((8,) + grad.shape, bf16),
        ],
        in_specs=[hbm] * 5,
        out_specs=[hbm] * 5,
        scratch_shapes=[dma((5,)), dma((6,)), dma((6,))]
        + [dma((2, groups - 1))] * 4
        + [dma((7,))] * 4,
        compiler_params=pltpu.CompilerParams(
            collective_id=ident, has_side_effects=True, vmem_limit_bytes=48 * 2**20
        ),
    )(mix, ffn, out, act, grad)


def scatter_kernel(part_ref, out_ref, mine, theirs, outgoing, landing, local_sem, send_sem, recv_sem):
    chips, core = places()
    sibling = device_at(chips[3], 1 - core)
    greet([device_at(chip, core) for chip in chips[:3]] + [sibling])
    swaps, locals_ = [], []
    for j, chip in enumerate(chips):
        swaps.append(
            remote(
                part_ref.at[rank_at(chip, 1 - core)], theirs.at[j], send_sem.at[j], recv_sem.at[j], sibling
            )
        )
        local = pltpu.make_async_copy(part_ref.at[rank_at(chip, core)], mine.at[j], local_sem.at[j])
        local.start()
        locals_.append(local)
    steps = out_ref.shape[0] // ROWS
    sent = []
    for j in range(4):
        locals_[j].wait()
        swaps[j].wait_recv()

        def add(i, _, j=j):
            rows = pl.ds(pl.multiple_of(i * ROWS, ROWS), ROWS)
            total = mine[j, rows, :].astype(f32) + theirs[j, rows, :].astype(f32)
            if j < 3:
                outgoing[j, rows, :] = total.astype(bf16)
            else:
                out_ref[rows, :] = total
            return 0

        lax.fori_loop(0, steps, add, 0)
        if j < 3:
            sent.append(
                remote(
                    outgoing.at[j],
                    landing.at[j],
                    send_sem.at[4 + j],
                    recv_sem.at[4 + j],
                    device_at(chips[j], core),
                )
            )
    for copy in sent:
        copy.wait_recv()

    def finish(i, _):
        rows = pl.ds(pl.multiple_of(i * ROWS, ROWS), ROWS)
        total = out_ref[rows, :]
        for j in range(3):
            total = total + landing[j, rows, :].astype(f32)
        out_ref[rows, :] = total
        return 0

    lax.fori_loop(0, steps, finish, 0)
    for copy in swaps + sent:
        copy.wait_send()


def collect_kernel(count, size, *refs):
    parts, outs = refs[:count], refs[count : count + 3]
    landing = refs[count + 3 : 2 * count + 3]
    local_sem, send_sem, recv_sem = refs[2 * count + 3 :]
    chips, core = places()
    others = [(j, chips[j], other) for j in range(4) for other in (core, 1 - core)]
    own = rank_at(chips[3], core)
    targets = [(chip, other) for j, chip, other in others if not (j == 3 and other is core)]
    greet([device_at(chip, other) for chip, other in targets])
    copies, locals_ = [], []
    for n in range(count):
        for i, (chip, other) in enumerate(targets):
            copies.append(
                remote(
                    parts[n].at[rank_at(chip, other)],
                    landing[n].at[own],
                    send_sem.at[n, i],
                    recv_sem.at[n, i],
                    device_at(chip, other),
                )
            )
        local = pltpu.make_async_copy(parts[n].at[own], landing[n].at[own], local_sem.at[n])
        local.start()
        locals_.append(local)
    for copy in locals_:
        copy.wait()
    for copy in copies:
        copy.wait_recv()
    span = landing[0].shape[2] // 3
    groups = span // size
    for which in range(3):
        for n in range(count):
            for k in range(8):
                for g in range(groups):
                    start = which * span + g * size
                    place = ((n * groups + g) * 8 + k) * size
                    outs[which][:, place : place + size] = landing[n][k, :, start : start + size].astype(f32)
    for copy in copies:
        copy.wait_send()


def collect(parts, size, ident):
    count, rows, wide = len(parts), parts[0].shape[1], parts[0].shape[2]
    vmem = pl.BlockSpec(memory_space=pltpu.VMEM)
    dma = pltpu.SemaphoreType.DMA
    return pl.pallas_call(
        functools.partial(collect_kernel, count, size),
        out_shape=[jax.ShapeDtypeStruct((rows, count * 8 * wide // 3), f32)] * 3,
        in_specs=[pl.BlockSpec(memory_space=pl.ANY)] * count,
        out_specs=[vmem] * 3,
        scratch_shapes=[pltpu.VMEM((8, rows, wide), bf16)] * count + [dma((count,)), dma((count, 7)), dma((count, 7))],
        compiler_params=pltpu.CompilerParams(
            collective_id=ident, has_side_effects=True, vmem_limit_bytes=48 * 2**20
        ),
    )(*parts)


def gather_plane(v, ident):
    hbm = pl.BlockSpec(memory_space=pl.ANY)
    out = pl.pallas_call(
        gather_kernel,
        out_shape=jax.ShapeDtypeStruct((8,) + v.shape, v.dtype),
        in_specs=[hbm],
        out_specs=hbm,
        scratch_shapes=[
            pltpu.SemaphoreType.DMA,
            pltpu.SemaphoreType.DMA((7,)),
            pltpu.SemaphoreType.DMA((7,)),
        ],
        compiler_params=pltpu.CompilerParams(
            collective_id=ident, has_side_effects=True, vmem_limit_bytes=48 * 2**20
        ),
    )(v)
    return out.reshape(-1, v.shape[1])


def scatter_plane(part, ident):
    rows, wide = part.shape[0] // 8, part.shape[1]
    return pl.pallas_call(
        scatter_kernel,
        out_shape=jax.ShapeDtypeStruct((rows, wide), f32),
        in_specs=[pl.BlockSpec(memory_space=pl.ANY)],
        out_specs=pl.BlockSpec(memory_space=pltpu.VMEM),
        scratch_shapes=[
            pltpu.VMEM((4, rows, wide), bf16),
            pltpu.VMEM((4, rows, wide), bf16),
            pltpu.VMEM((3, rows, wide), bf16),
            pltpu.VMEM((3, rows, wide), bf16),
            pltpu.SemaphoreType.DMA((4,)),
            pltpu.SemaphoreType.DMA((7,)),
            pltpu.SemaphoreType.DMA((7,)),
        ],
        compiler_params=pltpu.CompilerParams(
            collective_id=ident, has_side_effects=True, vmem_limit_bytes=48 * 2**20
        ),
    )(part.reshape(8, rows, wide))


def dot(a, b):
    return jnp.dot(a, b, preferred_element_type=f32)


def dot_nt(a, b):
    return lax.dot_general(a, b, (((1,), (1,)), ((), ())), preferred_element_type=f32)


def dot_tn(a, b):
    return lax.dot_general(a, b, (((0,), (0,)), ((), ())), preferred_element_type=f32)


def body(
    tokens,
    cotangent,
    domain_tags,
    doc_ids,
    counts,
    w_in,
    w_forget,
    w_gate_out,
    w_out,
    ffn_gate,
    ffn_up,
    ffn_down,
    norm_gain,
    out_gain,
    ffn_gain,
    bound_logits,
):
    groups = lax.axis_size("g")
    members = lax.axis_size("p") * lax.axis_size("c")
    copies = lax.axis_size("x")
    ranks = members * copies
    rows, width = tokens.shape
    plane_rows = rows * ranks
    units = ffn_gate.shape[1]
    g, x = lax.axis_index("g"), lax.axis_index("x")
    rank = (lax.axis_index("p") * lax.axis_size("c") + lax.axis_index("c")) * copies + x
    ce = width // (groups * ranks)
    fe = units // (groups * ranks)
    chan, part_unit = ce * groups, fe * groups // HALVES

    def columns(w, size):
        w = w.reshape(w.shape[0], groups, members, copies, size)
        w = lax.dynamic_index_in_dim(w, x, axis=3, keepdims=False)
        return jnp.moveaxis(w, 2, 0).reshape(members, w.shape[0], groups * size)

    def ffn_columns(w):
        w = w.reshape(w.shape[0], HALVES, groups // HALVES, members, copies, fe)
        w = lax.dynamic_index_in_dim(w, x, axis=4, keepdims=False)
        return w.transpose(3, 1, 0, 2, 4).reshape(members, HALVES, w.shape[0], part_unit)

    def half_rows(w):
        half = w.shape[0] // copies
        return lax.dynamic_slice_in_dim(w, x * half, half, axis=0)

    def own_columns(v, size):
        v = v.reshape(groups, ranks, size)
        return lax.dynamic_index_in_dim(v, rank, axis=1, keepdims=False).reshape(1, groups * size)

    def gather_rows(v):
        return lax.all_gather(v, "g", axis=0, tiled=True)

    layer_count = bound_logits.shape[0]
    layer_probs = jax.nn.softmax(bound_logits, axis=0)
    layer_index = jnp.arange(layer_count, dtype=jnp.int32)
    layer_pick = ((layer_index >= 1) & (layer_index <= LAYER_AT)).astype(f32)[:, None]
    own_lower = jnp.sum(layer_probs * layer_pick, axis=0)[:, None]
    top, rest = split_hi_lo(own_lower)
    out_own = jnp.concatenate(
        [
            half_rows(w_out),
            top,
            rest,
            (own_lower - top.astype(f32) - rest.astype(f32)).astype(bf16),
            jnp.zeros((ce, 125), bf16),
        ],
        axis=1,
    )
    down_w = gather_rows(half_rows(ffn_down))
    gain = own_columns(out_gain, ce)

    places = jnp.arange(doc_ids.shape[0], dtype=jnp.int32)
    previous = jnp.concatenate([doc_ids[:1], doc_ids[:-1]])
    keep = ((places % SEQ_LEN != 0) & (doc_ids == previous)).astype(f32)[:, None]
    keep = lax.dynamic_slice_in_dim(keep, g * plane_rows, plane_rows, axis=0)

    token_f = tokens.astype(f32)
    scale_one = lax.rsqrt(jnp.mean(token_f * token_f, axis=-1, keepdims=True) + EPS)
    normed_one = token_f * scale_one
    act_one_own = (normed_one * norm_gain).astype(bf16)

    domain_count = counts.shape[0]
    domain_hits = domain_tags[:, None] == jnp.arange(domain_count, dtype=jnp.int32)[None, :]
    per_token = jnp.sum(jnp.where(domain_hits, counts[None, :], 0), axis=1).astype(f32)
    seq_total = doc_ids.shape[0] // SEQ_LEN
    grad_z = cotangent.astype(f32) * (seq_total / (domain_count * per_token))[:, None]

    mix_w, ffn, out_ext, act_one, grad_m = spread(
        groups,
        jnp.concatenate([columns(w_in, ce), columns(w_forget, ce), columns(w_gate_out, ce)], axis=2),
        jnp.concatenate([ffn_columns(ffn_gate), ffn_columns(ffn_up)], axis=3),
        out_own,
        act_one_own,
        grad_z.astype(bf16),
        0,
    )
    mix_w = mix_w.reshape(width, 3 * chan)
    ffn, down_w = lax.optimization_barrier((ffn, down_w))
    ffn_w = [gather_rows(ffn[:, h].reshape(-1, 2 * part_unit)) for h in range(HALVES)]
    act_one, grad_m = act_one.reshape(plane_rows, width), grad_m.reshape(plane_rows, width)
    out_ext = out_ext.reshape(chan, -1)
    out_w = out_ext[:, :width]
    lower = jnp.sum(out_ext[:, width : width + 3].astype(f32), axis=1).reshape(1, chan)

    proj = dot(act_one, mix_w)
    states, mixed_raw, squares = kernel_call(
        functools.partial(forward_scan, chan),
        [
            jax.ShapeDtypeStruct((plane_rows, chan), f32),
            jax.ShapeDtypeStruct((plane_rows, chan), bf16),
            jax.ShapeDtypeStruct((plane_rows, 1), f32),
        ],
        proj,
        keep,
        lower,
        gain,
    )
    pad = jnp.zeros((plane_rows, 126), bf16)
    part = jnp.concatenate(
        [dot(mixed_raw, out_w).astype(bf16), *split_hi_lo(squares), pad], axis=1
    )
    total = scatter_plane(part, 1)
    state_scale = lax.rsqrt((total[:, width : width + 1] + total[:, width + 1 : width + 2]) / width + EPS)
    branch = total[:, :width] * state_scale
    residual = token_f + branch
    scale_two = lax.rsqrt(jnp.mean(residual * residual, axis=-1, keepdims=True) + EPS)
    normed_two = residual * scale_two
    act_two = gather_plane((normed_two * ffn_gain).astype(bf16), 2)

    def scatter_rows(v):
        return lax.psum_scatter(v, "g", scatter_dimension=0, tiled=True)

    down_part, back_part, ffn_sums = 0.0, 0.0, []
    for h in range(HALVES):
        down = down_w[h * part_unit : (h + 1) * part_unit]
        grad_hidden = dot_nt(grad_m, down)
        pre = dot(act_two, ffn_w[h])
        gate_ffn, up_ffn = pre[:, :part_unit], pre[:, part_unit:]
        sig = jax.nn.sigmoid(gate_ffn)
        gate_silu = gate_ffn * sig
        hidden = (gate_silu * up_ffn).astype(bf16)
        grad_gate = (grad_hidden * up_ffn * (sig * (1.0 + gate_ffn * (1.0 - sig)))).astype(bf16)
        grad_up = (grad_hidden * gate_silu).astype(bf16)
        grad_pre = jnp.concatenate([grad_gate, grad_up], axis=1)
        grads = jnp.concatenate(
            [dot_tn(act_two, grad_pre).astype(bf16), dot_tn(grad_m, hidden).astype(bf16)], axis=1
        )
        grads, grad_pre, hidden = lax.optimization_barrier((grads, grad_pre, hidden))
        ffn_sums.append(scatter_rows(grads))
        down_part = down_part + dot(hidden, down)
        back_part = back_part + dot_nt(grad_pre, ffn_w[h])
    down_part, back_part = down_part.astype(bf16), back_part.astype(bf16)

    back_term = scatter_plane(back_part, 3)
    scaled_two = back_term * ffn_gain
    grad_resid = grad_z + scale_two * (
        scaled_two - normed_two * jnp.mean(scaled_two * normed_two, axis=-1, keepdims=True)
    )
    grad_branch_own = grad_resid.astype(bf16)
    mean_out = jnp.sum(grad_branch_own.astype(f32) * branch, axis=-1, keepdims=True) / width
    sent = jnp.concatenate(
        [
            grad_branch_own,
            *split_hi_lo(state_scale),
            *split_hi_lo(mean_out),
            jnp.zeros((rows, 124), bf16),
        ],
        axis=1,
    )
    got = gather_plane(sent, 4)
    grad_branch = got[:, :width]
    info = got[:, width:].astype(f32)
    info = jnp.concatenate([info[:, 0:1] + info[:, 1:2], info[:, 2:3] + info[:, 3:4]], axis=1)
    grad_mixed = dot_nt(grad_branch, out_w)
    grad_proj, mixed_out, sums = kernel_call(
        functools.partial(backward_scan, chan),
        [
            jax.ShapeDtypeStruct((plane_rows, 3 * chan), bf16),
            jax.ShapeDtypeStruct((plane_rows, chan), bf16),
            jax.ShapeDtypeStruct((1, chan), f32),
        ],
        proj,
        states,
        grad_mixed,
        info,
        keep,
        lower,
        gain,
    )
    in_part = dot_nt(grad_proj, mix_w).astype(bf16)
    mix_grads = dot_tn(act_one, grad_proj).astype(bf16).reshape(groups, -1, 3 * chan)
    top, rest = split_hi_lo(sums.reshape(chan, 1))
    out_grads = jnp.concatenate(
        [dot_tn(mixed_out, grad_branch).astype(bf16), top, rest, jnp.zeros((chan, 3 * chan - 2), bf16)],
        axis=1,
    )
    folds = out_grads.shape[1] // (3 * chan)
    out_grads = out_grads[:, : folds * 3 * chan].reshape(groups, ce, folds, 3 * chan)
    out_grads = jnp.moveaxis(out_grads, 2, 1).reshape(groups, folds * ce, 3 * chan)
    late_grads = jnp.concatenate([mix_grads, out_grads], axis=1).reshape(-1, 3 * chan)
    late_grads, ffn_sums = lax.optimization_barrier((late_grads, ffn_sums))
    late_sum = scatter_rows(late_grads)
    mix_sum = late_sum[: width // groups]
    out_sum = jnp.moveaxis(late_sum[width // groups :].reshape(folds, ce, 3 * chan), 1, 0)
    out_sum = out_sum.reshape(ce, -1).astype(f32)
    summed_wout = out_sum[:, :width]
    grad_lower = out_sum[:, width] + out_sum[:, width + 1]
    down_term = scatter_plane(down_part, 5)
    output_rows = (residual + down_term).astype(bf16)

    grad_act = scatter_plane(in_part, 6)
    scaled_one = grad_act * norm_gain
    grad_tokens = grad_resid + scale_one * (
        scaled_one - normed_one * jnp.mean(scaled_one * normed_one, axis=-1, keepdims=True)
    )

    summed_fgate, summed_fup, fdown = collect([v.reshape(ranks, -1, 3 * part_unit) for v in ffn_sums], fe, 7)
    summed_fdown = fdown.T
    summed_win, summed_wforget, summed_wgate = collect([mix_sum.reshape(ranks, -1, 3 * chan)], ce, 8)
    first = (g * ranks + rank) * ce

    def own_gain(gain, pairs):
        total = sum(jnp.sum(grad * half_rows(w).astype(f32), axis=1) for grad, w in pairs)
        return total / lax.dynamic_slice_in_dim(gain, first, ce, axis=0)

    summed_norm = own_gain(
        norm_gain, ((summed_win, w_in), (summed_wforget, w_forget), (summed_wgate, w_gate_out))
    )
    summed_outg = own_gain(out_gain, ((summed_wout, w_out),))
    summed_ffng = own_gain(ffn_gain, ((summed_fgate, ffn_gate), (summed_fup, ffn_up)))
    grad_probs = layer_pick * grad_lower[None, :]
    grad_bounds = layer_probs * (
        grad_probs - jnp.sum(layer_probs * grad_probs, axis=0, keepdims=True)
    )
    return (
        output_rows,
        grad_tokens,
        summed_win,
        summed_wforget,
        summed_wgate,
        summed_wout,
        summed_fgate,
        summed_fup,
        summed_fdown,
        summed_norm,
        summed_outg,
        summed_ffng,
        grad_bounds,
    )


def solution(mesh):
    seqs, copies = mesh.shape["seq"], mesh.shape["rep"]
    mesh = Mesh(mesh.devices.reshape(seqs // 4, 2, 2, copies), ALL)
    by_rows = P(ALL, None)
    by_seq = P(("g", "p", "c"), None)
    placed = (
        (by_rows, by_rows, P(ALL), P(), P()) + (by_seq,) * 7 + (P(), P(), P(), P(None, ALL))
    )
    return jax.shard_map(
        body,
        mesh=mesh,
        in_specs=placed,
        out_specs=(by_rows,) * 8 + (P(None, ALL),) + (P(ALL),) * 3 + (P(None, ALL),),
        check_vma=False,
    )
```

```python
import functools

import jax
import jax.numpy as jnp
from jax import lax
from jax.experimental import pallas as pl
from jax.experimental.pallas import tpu as pltpu
from jax.sharding import Mesh
from jax.sharding import PartitionSpec as P

LAYER_AT = 12
SEQ_LEN = 1024
EPS = 1e-06
ROWS = 16
QUARTERS = 4
PLANE = ("p", "c", "x")
ALL = ("g", "p", "c", "x")
f32 = jnp.float32
bf16 = jnp.bfloat16


def split_hi_lo(v):
    hi = v.astype(bf16)
    return hi, (v - hi.astype(f32)).astype(bf16)


def gates(proj, chan, lower):
    ip = proj[:, :chan].astype(bf16).astype(f32)
    sf = jax.nn.sigmoid(proj[:, chan : 2 * chan].astype(bf16).astype(f32))
    forget = lower + (1.0 - lower) * sf
    sig_in = jax.nn.sigmoid(ip)
    return ip, sig_in, sf, forget


def forward_scan(chan, proj_ref, keep_ref, lower_ref, gain_ref, h_ref, o_ref, ss_ref):
    lower = lower_ref[...]
    gain = gain_ref[...]
    row = lax.broadcasted_iota(jnp.int32, (ROWS, chan), 0)

    def step(i, carry):
        rows = pl.ds(pl.multiple_of(i * ROWS, ROWS), ROWS)
        proj = proj_ref[rows, :]
        ip, sig_in, _, forget = gates(proj, chan, lower)
        u = ip * sig_in * (1.0 - forget)
        e = forget * keep_ref[rows, :]
        shift = 1
        while shift < ROWS:
            u = u + e * jnp.where(row >= shift, pltpu.roll(u, shift, 0), 0.0)
            e = e * jnp.where(row >= shift, pltpu.roll(e, shift, 0), 1.0)
            shift *= 2
        h = u + e * carry
        h_ref[rows, :] = h
        hb = h.astype(bf16).astype(f32)
        gate = proj[:, 2 * chan :]
        o_ref[rows, :] = (hb * gain * (gate * jax.nn.sigmoid(gate))).astype(bf16)
        ss_ref[rows, :] = jnp.sum(hb * hb, axis=1, keepdims=True)
        return h[ROWS - 1 : ROWS, :]

    lax.fori_loop(0, proj_ref.shape[0] // ROWS, step, jnp.zeros((1, chan), f32))


def mixer_kernel(
    chan,
    act_ref,
    mix_ref,
    out_w_ref,
    keep_ref,
    lower_ref,
    gain_ref,
    token_ref,
    ffn_gain_ref,
    proj_ref,
    h_ref,
    residual_ref,
    scale_ref,
    act_two_ref,
    raw,
    squares,
    part,
    theirs,
    outgoing,
    landing,
    own_two,
    swap_send,
    swap_recv,
    send_sem,
    recv_sem,
    local_sem,
    act_send,
    act_recv,
):
    chips, core = places()
    sibling = device_at(chips[3], 1 - core)
    greet([device_at(chip, core) for chip in chips[:3]] + [sibling])
    rows, width = token_ref.shape
    block = 2 * rows

    def project(i, _):
        at = pl.ds(pl.multiple_of(i * block, block), block)
        proj_ref[at, :] = dot(act_ref[at, :], mix_ref[...])
        return 0

    lax.fori_loop(0, act_ref.shape[0] // block, project, 0)
    forward_scan(chan, proj_ref, keep_ref, lower_ref, gain_ref, h_ref, raw, squares)

    lane = lax.broadcasted_iota(jnp.int32, (rows, part.shape[1] - width), 1)

    def mixed(rank):
        at = pl.ds(pl.multiple_of(rank * rows, rows), rows)
        part[at, :width] = dot(raw[at, :], out_w_ref[:, :width]).astype(bf16)
        top, rest = split_hi_lo(squares[at, :])
        side = jnp.where(lane == 0, top.astype(f32), jnp.where(lane == 1, rest.astype(f32), 0.0))
        part[at, width:] = side.astype(bf16)
        return part.at[at]

    swaps = []
    for j, chip in enumerate(chips):
        swaps.append(
            remote(
                mixed(rank_at(chip, 1 - core)), theirs.at[j], swap_send.at[j], swap_recv.at[j], sibling
            )
        )
    scatter = Scatter([], theirs, outgoing, landing, send_sem, recv_sem)
    for j, chip in enumerate(chips):
        scatter.mine.append(mixed(rank_at(chip, core)))
        swaps[j].wait_recv()
        if j < 3:
            scatter.first(j)
    scatter.second()

    def finish(at, total):
        scale = lax.rsqrt((total[:, width : width + 1] + total[:, width + 1 : width + 2]) / width + EPS)
        scale_ref[at, :] = scale
        residual = token_ref[at, :].astype(f32) + total[:, :width] * scale
        residual_ref[at, :] = residual
        norm = lax.rsqrt(jnp.mean(residual * residual, axis=-1, keepdims=True) + EPS)
        own_two[at, :] = (residual * norm * ffn_gain_ref[...]).astype(bf16)

    scatter.totals(finish)
    plane = Plane(own_two, act_two_ref, local_sem.at[0], act_send, act_recv)
    plane.start(1)
    plane.start(2)
    plane.start_own()
    for copy in swaps:
        copy.wait_send()
    scatter.finish()
    for i in (1, 2, 0):
        plane.hand_on(i)
    plane.finish()


def mixer(chan, act, mix_w, out_ext, keep, lower, gain, tokens, ffn_gain, ident):
    total, (rows, width) = act.shape[0], tokens.shape
    vmem, hbm = pl.BlockSpec(memory_space=pltpu.VMEM), pl.BlockSpec(memory_space=pl.ANY)
    dma = pltpu.SemaphoreType.DMA
    wide = width + 128
    return pl.pallas_call(
        functools.partial(mixer_kernel, chan),
        out_shape=[
            jax.ShapeDtypeStruct((total, 3 * chan), f32),
            jax.ShapeDtypeStruct((total, chan), f32),
            jax.ShapeDtypeStruct((rows, width), f32),
            jax.ShapeDtypeStruct((rows, 1), f32),
            jax.ShapeDtypeStruct((8, rows, width), bf16),
        ],
        in_specs=[vmem] * 8,
        out_specs=[vmem] * 4 + [hbm],
        scratch_shapes=[
            pltpu.VMEM((total, chan), bf16),
            pltpu.VMEM((total, 1), f32),
            pltpu.VMEM((total, wide), bf16),
            pltpu.VMEM((4, rows, wide), bf16),
            pltpu.VMEM((6, rows // 2, wide), bf16),
            pltpu.VMEM((6, rows // 2, wide), bf16),
            pltpu.VMEM((rows, width), bf16),
            dma((4,)),
            dma((4,)),
            dma((6,)),
            dma((6,)),
            dma((1,)),
            dma((8,)),
            dma((8,)),
        ],
        compiler_params=pltpu.CompilerParams(
            collective_id=ident, has_side_effects=True, vmem_limit_bytes=56 * 2**20
        ),
    )(act, mix_w, out_ext, keep, lower, gain, tokens, ffn_gain)


def backward_scan(
    chan, proj_ref, h_ref, do_ref, info_ref, keep_ref, lower_ref, gain_ref, grad_ref, o_ref, sums_ref
):
    lower = lower_ref[...]
    gain = gain_ref[...]
    row = lax.broadcasted_iota(jnp.int32, (ROWS, chan), 0)
    blocks = proj_ref.shape[0] // ROWS

    def step(j, carried):
        later, sum_lower = carried
        i = blocks - 1 - j
        rows = pl.ds(pl.multiple_of(i * ROWS, ROWS), ROWS)
        proj = proj_ref[rows, :]
        ip, sig_in, sf, forget = gates(proj, chan, lower)
        keep = keep_ref[rows, :]
        act_in = ip * sig_in
        h = h_ref[rows, :]
        before = h_ref[pl.ds(pl.multiple_of(jnp.maximum(i * ROWS - 8, 0), 8), 8), :][7:8, :]
        h_prev = jnp.where(row >= 1, pltpu.roll(h, 1, 0), before)
        scale = info_ref[rows, 0:1]
        mean = info_ref[rows, 1:2]
        hn = h.astype(bf16).astype(f32) * scale
        gate = proj[:, 2 * chan :]
        sig_gate = jax.nn.sigmoid(gate)
        gate_act = gate * sig_gate
        do = do_ref[rows, :]
        o_ref[rows, :] = (hn * gain * gate_act).astype(bf16)
        dgp = do * hn * gain * (sig_gate * (1.0 + gate * (1.0 - sig_gate)))
        dhb = scale * (do * gain * gate_act - hn * mean)
        d = dhb.astype(bf16).astype(f32)
        e = forget * keep
        c = jnp.where(row < ROWS - 1, pltpu.roll(e, ROWS - 1, 0), 1.0)
        shift = 1
        while shift < ROWS:
            inside = row < ROWS - shift
            d = d + c * jnp.where(inside, pltpu.roll(d, ROWS - shift, 0), 0.0)
            c = c * jnp.where(inside, pltpu.roll(c, ROWS - shift, 0), 1.0)
            shift *= 2
        dh = d + c * later
        dip = dh * (1.0 - forget) * (sig_in * (1.0 + ip * (1.0 - sig_in)))
        df = dh * (h_prev * keep - act_in)
        tail = df * (1.0 - sf)
        dfp = tail * (1.0 - lower) * sf
        grad_ref[rows, :] = jnp.concatenate([dip, dfp, dgp], axis=1).astype(bf16)
        sum_lower = sum_lower + jnp.sum(tail, axis=0, keepdims=True)
        return (e * dh)[0:1, :], sum_lower

    zero = jnp.zeros((1, chan), f32)
    _, sum_lower = lax.fori_loop(0, blocks, step, (zero, zero))
    sums_ref[...] = sum_lower


def kernel_call(kernel, outs, *args):
    vmem = pl.BlockSpec(memory_space=pltpu.VMEM)
    return pl.pallas_call(
        kernel,
        out_shape=outs,
        in_specs=[vmem] * len(args),
        out_specs=[vmem] * len(outs),
        compiler_params=pltpu.CompilerParams(vmem_limit_bytes=48 * 2**20),
    )(*args)


MESH = pl.DeviceIdType.MESH


def places():
    g, p, c, x = (lax.axis_index(a) for a in ALL)
    flips = ((1, 1), (0, 1), (1, 0), (0, 0))
    chips = [(g, p + dp * (1 - 2 * p), x + dx * (1 - 2 * x)) for dp, dx in flips]
    return chips, c


def device_at(chip, core):
    return (chip[0], chip[1], core, chip[2])


def rank_at(chip, core):
    return (chip[1] * 2 + core) * 2 + chip[2]


def greet(partners):
    barrier = pltpu.get_barrier_semaphore()
    for partner in partners:
        pl.semaphore_signal(barrier, inc=1, device_id=partner, device_id_type=MESH)
    pl.semaphore_wait(barrier, len(partners))


def remote(src, dst, send_sem, recv_sem, device):
    copy = pltpu.make_async_remote_copy(
        src_ref=src, dst_ref=dst, send_sem=send_sem, recv_sem=recv_sem, device_id=device, device_id_type=MESH
    )
    copy.start()
    return copy


class Line:
    def __init__(self, groups, own_ref, out_ref, send_sem, recv_sem, local_sem=None):
        self.groups, self.own, self.out = groups, own_ref, out_ref
        self.send_sem, self.recv_sem = send_sem, recv_sem
        self.g, self.p, self.c, self.x = (lax.axis_index(a) for a in ALL)
        self.kept = None
        if local_sem is not None:
            self.kept = pltpu.make_async_copy(own_ref, out_ref.at[self.g], local_sem)
            self.kept.start()

    def at_step(self, way, k):
        block = self.g - (k - 1) if way == 0 else self.g + (k - 1)
        return pltpu.make_async_remote_copy(
            src_ref=self.own if k == 1 else self.out.at[block],
            dst_ref=self.out.at[block],
            send_sem=self.send_sem.at[way, k - 1],
            recv_sem=self.recv_sem.at[way, k - 1],
            device_id=(self.g + (1 if way == 0 else -1), self.p, self.c, self.x),
            device_id_type=MESH,
        )

    def behind(self, way, k):
        return self.g >= k if way == 0 else self.g + k < self.groups

    def sends(self, way, k):
        return self.behind(way, k - 1) & self.behind(1 - way, 1)

    def send(self, k):
        for way in (0, 1):

            @pl.when(self.sends(way, k))
            def _(way=way):
                self.at_step(way, k).start()

    def arrived(self, way, k):
        got = self.out.at[self.g - k if way == 0 else self.g + k]
        pltpu.make_async_remote_copy(
            src_ref=got,
            dst_ref=got,
            send_sem=self.send_sem.at[way, k - 1],
            recv_sem=self.recv_sem.at[way, k - 1],
            device_id=(self.g, self.p, self.c, self.x),
            device_id_type=MESH,
        ).wait_recv()

    def step(self, k):
        for way in (0, 1):

            @pl.when(self.behind(way, k))
            def _(way=way):
                self.arrived(way, k)

        if k + 1 < self.groups:
            self.send(k + 1)

    def finish(self):
        if self.kept is not None:
            self.kept.wait()
        for k in range(1, self.groups):
            for way in (0, 1):

                @pl.when(self.sends(way, k))
                def _(way=way, k=k):
                    self.at_step(way, k).wait_send()


def line_partners(groups):
    g, p, c, x = (lax.axis_index(a) for a in ALL)
    offsets = sorted({1 % groups, -1 % groups} - {0})
    return [(lax.rem(g + k, groups), p, c, x) for k in offsets]


class Plane:
    def __init__(self, own_ref, out_ref, local_sem, send_sem, recv_sem):
        self.own, self.out = own_ref, out_ref
        self.send_sem, self.recv_sem = send_sem, recv_sem
        self.chips, self.core = places()
        self.half = own_ref.shape[0] // 2
        self.slot = out_ref.at[rank_at(self.chips[3], self.core)]
        self.sibling = device_at(self.chips[3], 1 - self.core)
        self.local = pltpu.make_async_copy(own_ref, self.slot, local_sem)
        self.sent, self.passed = {}, []

    def send(self, n, src, dst, device):
        return remote(src, dst, self.send_sem.at[n], self.recv_sem.at[n], device)

    def start_own(self):
        self.local.start()
        self.passed.append(self.send(3, self.own, self.slot, self.sibling))

    def start(self, i):
        self.sent[i] = self.send(i, self.own, self.slot, device_at(self.chips[i], self.core))

    def hand_on(self, i):
        got = self.out.at[rank_at(self.chips[i], self.core)]
        if i:
            self.sent[i].wait_recv()
            n, first = (0, 0) if i == 1 else (7, self.half)
            part = got.at[pl.ds(first, self.half)]
            self.sent[n] = self.send(n, part, part, device_at(self.chips[3 - i], self.core))
        else:
            self.sent[0].wait_recv()
            self.sent[7].wait_recv()
        self.passed.append(self.send(4 + i, got, got, self.sibling))

    def finish(self):
        for copy in self.sent.values():
            copy.wait_send()
        for copy in self.passed:
            copy.wait()
        self.local.wait()


class Scatter:
    def __init__(self, mine, theirs, outgoing, landing, send_sem, recv_sem):
        self.mine, self.theirs, self.outgoing, self.landing = mine, theirs, outgoing, landing
        self.send_sem, self.recv_sem = send_sem, recv_sem
        self.chips, self.core = places()
        self.half = outgoing.shape[1]
        self.sent = []

    def both(self, j, at):
        return self.mine[j][at, :].astype(f32) + self.theirs[j, at, :].astype(f32)

    def send(self, n, j, bottom, to, arrived=None):
        def add(i, _):
            near = pl.ds(pl.multiple_of(i * ROWS, ROWS), ROWS)
            at = pl.ds(pl.multiple_of(i * ROWS + bottom * self.half, ROWS), ROWS)
            total = self.both(j, at)
            if arrived is not None:
                total = total + self.landing[arrived, near, :].astype(f32)
            self.outgoing[n, near, :] = total.astype(bf16)
            return 0

        lax.fori_loop(0, self.half // ROWS, add, 0)
        self.sent.append(
            remote(
                self.outgoing.at[n],
                self.landing.at[n],
                self.send_sem.at[n],
                self.recv_sem.at[n],
                device_at(self.chips[to], self.core),
            )
        )

    def first(self, j):
        if j in (0, 1):
            self.send(j, j, 0, 1)
        if j in (0, 2):
            self.send(2 if j == 0 else 3, j, 1, 2)

    def second(self):
        arrived = [self.sent[n].wait_recv for n in (0, 2, 1, 3)]
        arrived[0]()
        self.send(4, 2, 0, 2, 0)
        arrived[2]()
        self.send(5, 1, 1, 1, 2)
        arrived[1]()
        arrived[3]()
        self.sent[4].wait_recv()
        self.sent[5].wait_recv()

    def totals(self, use):
        for bottom in (0, 1):

            def one(i, _, bottom=bottom):
                near = pl.ds(pl.multiple_of(i * ROWS, ROWS), ROWS)
                at = pl.ds(pl.multiple_of(i * ROWS + bottom * self.half, ROWS), ROWS)
                total = self.both(3, at)
                for n in (1 + 2 * bottom, 4 + bottom):
                    total = total + self.landing[n, near, :].astype(f32)
                use(at, total)
                return 0

            lax.fori_loop(0, self.half // ROWS, one, 0)

    def finish(self):
        for copy in self.sent:
            copy.wait_send()


def gather_kernel(own_ref, out_ref, local_sem, send_sem, recv_sem):
    plane = Plane(own_ref, out_ref, local_sem, send_sem, recv_sem)
    greet([device_at(chip, plane.core) for chip in plane.chips[:3]] + [plane.sibling])
    plane.start(1)
    plane.start(2)
    plane.start_own()
    for i in (1, 2, 0):
        plane.hand_on(i)
    plane.finish()


def spread_kernel(
    groups,
    mix_ref,
    ffn_ref,
    out_ref,
    act_ref,
    grad_ref,
    mix_all,
    out_all,
    act_all,
    grad_all,
    ffn_all,
    local_sem,
    swap_send,
    swap_recv,
    mix_send,
    mix_recv,
    out_send,
    out_recv,
    act_send,
    act_recv,
    grad_send,
    grad_recv,
):
    chips, core = places()
    here, other = chips[3], chips[2]
    g = here[0]
    swaps = [device_at(here, 1 - core), device_at(other, core), device_at(other, 1 - core)]
    greet([device_at(chip, core) for chip in chips[:3]] + [swaps[0], swaps[2]] + line_partners(groups))
    own = here[1] * 2 + core
    targets = [here[1] * 2 + 1 - core, other[1] * 2 + core, other[1] * 2 + 1 - core]

    def swap(src, dst, first):
        return [
            remote(
                src.at[targets[i]], dst, swap_send.at[first + i], swap_recv.at[first + i], swaps[i]
            )
            for i in range(3)
        ]

    mix_copies = swap(mix_ref, mix_all.at[g, own], 0)
    locals_ = [
        pltpu.make_async_copy(mix_ref.at[own], mix_all.at[g, own], local_sem.at[0]),
        pltpu.make_async_copy(ffn_ref.at[own], ffn_all.at[own], local_sem.at[1]),
        pltpu.make_async_copy(out_ref, out_all.at[g], local_sem.at[2]),
    ]
    for copy in locals_:
        copy.start()
    out_line = Line(groups, out_ref, out_all, out_send, out_recv)
    mix_line = Line(groups, mix_all.at[g], mix_all, mix_send, mix_recv)
    out_line.send(1)
    act = Plane(act_ref, act_all, local_sem.at[3], act_send, act_recv)
    grad = Plane(grad_ref, grad_all, local_sem.at[4], grad_send, grad_recv)
    act.start_own()
    grad.start_own()
    act.start(1)
    for copy in mix_copies:
        copy.wait()
    locals_[0].wait()
    mix_line.send(1)
    act.start(2)
    ffn_copies = swap(ffn_ref, ffn_all.at[own], 3)
    out_line.step(1)
    act.hand_on(1)
    act.hand_on(2)
    grad.start(1)
    grad.start(2)
    mix_line.step(1)
    act.hand_on(0)
    for k in range(2, groups):
        out_line.step(k)
        mix_line.step(k)
        if k == 2:
            grad.hand_on(1)
            grad.hand_on(2)
    grad.hand_on(0)
    for copy in ffn_copies:
        copy.wait()
    for copy in locals_[1:]:
        copy.wait()
    out_line.finish()
    mix_line.finish()
    act.finish()
    grad.finish()


def spread(groups, mix, ffn, out, act, grad, ident):
    hbm = pl.BlockSpec(memory_space=pl.ANY)
    dma = pltpu.SemaphoreType.DMA
    return pl.pallas_call(
        functools.partial(spread_kernel, groups),
        out_shape=[
            jax.ShapeDtypeStruct((groups,) + mix.shape, bf16),
            jax.ShapeDtypeStruct((groups,) + out.shape, bf16),
            jax.ShapeDtypeStruct((8,) + act.shape, bf16),
            jax.ShapeDtypeStruct((8,) + grad.shape, bf16),
            jax.ShapeDtypeStruct(ffn.shape, bf16),
        ],
        in_specs=[hbm] * 5,
        out_specs=[hbm] * 5,
        scratch_shapes=[dma((5,)), dma((6,)), dma((6,))]
        + [dma((2, groups - 1))] * 4
        + [dma((8,))] * 4,
        compiler_params=pltpu.CompilerParams(
            collective_id=ident, has_side_effects=True, vmem_limit_bytes=48 * 2**20
        ),
    )(mix, ffn, out, act, grad)


def scatter_kernel(count, *refs):
    parts, outs = refs[:count], refs[count : 2 * count]
    mine, theirs, outgoing, landing, local_sem, send_sem, recv_sem = refs[2 * count :]
    chips, core = places()
    sibling = device_at(chips[3], 1 - core)
    greet([device_at(chip, core) for chip in chips[:3]] + [sibling])
    swaps, locals_, sent = [], [], []
    for n in range(count):
        for j, chip in enumerate(chips):
            swaps.append(
                remote(
                    parts[n].at[rank_at(chip, 1 - core)],
                    theirs.at[n, j],
                    send_sem.at[n, j],
                    recv_sem.at[n, j],
                    sibling,
                )
            )
            local = pltpu.make_async_copy(
                parts[n].at[rank_at(chip, core)], mine.at[n, j], local_sem.at[n, j]
            )
            local.start()
            locals_.append(local)
    scatters = []
    for n in range(count):
        scatter = Scatter(
            [mine.at[n, j] for j in range(4)],
            theirs.at[n],
            outgoing.at[n],
            landing.at[n],
            send_sem.at[n, pl.ds(4, 6)],
            recv_sem.at[n, pl.ds(4, 6)],
        )
        for j in range(4):
            locals_[4 * n + j].wait()
            swaps[4 * n + j].wait_recv()
            if j < 3:
                scatter.first(j)
        scatters.append(scatter)
    for n, scatter in enumerate(scatters):
        scatter.second()

        def store(at, total, n=n):
            outs[n][at, :] = total

        scatter.totals(store)
    for scatter in scatters:
        scatter.finish()
    for copy in swaps:
        copy.wait_send()


def collect_kernel(count, splits, size, *refs):
    parts, outs = refs[:count], refs[count : count + 3]
    landing = refs[count + 3 : 2 * count + 3]
    wholes = refs[2 * count + 3 : 2 * count + 6]
    local_sem, send_sem, recv_sem = refs[2 * count + 6 :]
    chips, core = places()
    others = [(j, chips[j], other) for j in range(4) for other in (core, 1 - core)]
    own = rank_at(chips[3], core)
    targets = [(chip, other) for j, chip, other in others if not (j == 3 and other is core)]
    greet([device_at(chip, other) for chip, other in targets])
    copies, locals_ = [], []
    for n in range(count):
        for i, (chip, other) in enumerate(targets):
            copies.append(
                remote(
                    parts[n].at[rank_at(chip, other)],
                    landing[n].at[own],
                    send_sem.at[n, i],
                    recv_sem.at[n, i],
                    device_at(chip, other),
                )
            )
        local = pltpu.make_async_copy(parts[n].at[own], landing[n].at[own], local_sem.at[n])
        local.start()
        locals_.append(local)
    for copy in locals_:
        copy.wait()
    for copy in copies:
        copy.wait_recv()
    edges = [0]
    for n in range(count):
        edges.append(edges[-1] + landing[n].shape[2])
    for first, last in zip(splits[:-1], splits[1:]):
        for which in range(3):
            for k in range(8):
                for group in range(first // size, last // size):
                    start = 3 * first + which * (last - first) + group * size - first
                    place = (group * 8 + k) * size
                    for n in range(count):
                        low, high = max(start, edges[n]), min(start + size, edges[n + 1])
                        if low < high:
                            wholes[which][:, place + low - start : place + high - start] = landing[n][
                                k, :, low - edges[n] : high - edges[n]
                            ].astype(f32)
    for out, whole in zip(outs, wholes):
        out[...] = whole[...].astype(bf16)
    for copy in copies:
        copy.wait_send()


def collect(parts, splits, size, ident):
    count, rows, wide = len(parts), parts[0].shape[1], 8 * splits[-1]
    vmem = pl.BlockSpec(memory_space=pltpu.VMEM)
    dma = pltpu.SemaphoreType.DMA
    return pl.pallas_call(
        functools.partial(collect_kernel, count, splits, size),
        out_shape=[jax.ShapeDtypeStruct((rows, wide), bf16)] * 3,
        in_specs=[pl.BlockSpec(memory_space=pl.ANY)] * count,
        out_specs=[vmem] * 3,
        scratch_shapes=[pltpu.VMEM(part.shape, bf16) for part in parts]
        + [pltpu.VMEM((rows, wide), f32)] * 3
        + [dma((count,)), dma((count, 7)), dma((count, 7))],
        compiler_params=pltpu.CompilerParams(
            collective_id=ident, has_side_effects=True, vmem_limit_bytes=48 * 2**20
        ),
    )(*parts)


def gather_plane(v, ident):
    hbm = pl.BlockSpec(memory_space=pl.ANY)
    out = pl.pallas_call(
        gather_kernel,
        out_shape=jax.ShapeDtypeStruct((8,) + v.shape, v.dtype),
        in_specs=[hbm],
        out_specs=hbm,
        scratch_shapes=[
            pltpu.SemaphoreType.DMA,
            pltpu.SemaphoreType.DMA((8,)),
            pltpu.SemaphoreType.DMA((8,)),
        ],
        compiler_params=pltpu.CompilerParams(
            collective_id=ident, has_side_effects=True, vmem_limit_bytes=48 * 2**20
        ),
    )(v)
    return out.reshape(-1, v.shape[1])


def scatter_plane(parts, ident):
    count, rows, wide = len(parts), parts[0].shape[0] // 8, parts[0].shape[1]
    return pl.pallas_call(
        functools.partial(scatter_kernel, count),
        out_shape=[jax.ShapeDtypeStruct((rows, wide), f32)] * count,
        in_specs=[pl.BlockSpec(memory_space=pl.ANY)] * count,
        out_specs=[pl.BlockSpec(memory_space=pltpu.VMEM)] * count,
        scratch_shapes=[
            pltpu.VMEM((count, 4, rows, wide), bf16),
            pltpu.VMEM((count, 4, rows, wide), bf16),
            pltpu.VMEM((count, 6, rows // 2, wide), bf16),
            pltpu.VMEM((count, 6, rows // 2, wide), bf16),
            pltpu.SemaphoreType.DMA((count, 4)),
            pltpu.SemaphoreType.DMA((count, 10)),
            pltpu.SemaphoreType.DMA((count, 10)),
        ],
        compiler_params=pltpu.CompilerParams(
            collective_id=ident, has_side_effects=True, vmem_limit_bytes=48 * 2**20
        ),
    )(*[part.reshape(8, rows, wide) for part in parts])


def dot(a, b):
    return jnp.dot(a, b, preferred_element_type=f32)


def dot_nt(a, b):
    return lax.dot_general(a, b, (((1,), (1,)), ((), ())), preferred_element_type=f32)


def dot_tn(a, b):
    return lax.dot_general(a, b, (((0,), (0,)), ((), ())), preferred_element_type=f32)


def body(
    tokens,
    cotangent,
    domain_tags,
    doc_ids,
    counts,
    w_in,
    w_forget,
    w_gate_out,
    w_out,
    ffn_gate,
    ffn_up,
    ffn_down,
    norm_gain,
    out_gain,
    ffn_gain,
    bound_logits,
):
    groups = lax.axis_size("g")
    members = lax.axis_size("p") * lax.axis_size("c")
    copies = lax.axis_size("x")
    ranks = members * copies
    rows, width = tokens.shape
    plane_rows = rows * ranks
    units = ffn_gate.shape[1]
    g, x = lax.axis_index("g"), lax.axis_index("x")
    rank = (lax.axis_index("p") * lax.axis_size("c") + lax.axis_index("c")) * copies + x
    ce = width // (groups * ranks)
    fe = units // (groups * ranks)
    chan, unit = ce * groups, fe * groups
    splits = (0, unit // QUARTERS, unit)

    def columns(w, size):
        w = w.reshape(w.shape[0], groups, members, copies, size)
        w = lax.dynamic_index_in_dim(w, x, axis=3, keepdims=False)
        return jnp.moveaxis(w, 2, 0).reshape(members, w.shape[0], groups * size)

    def half_rows(w):
        half = w.shape[0] // copies
        return lax.dynamic_slice_in_dim(w, x * half, half, axis=0)

    def gather_rows(v):
        return lax.all_gather(v, "g", axis=0, tiled=True)

    def own_columns(v, size):
        v = v.reshape(groups, ranks, size)
        return lax.dynamic_index_in_dim(v, rank, axis=1, keepdims=False).reshape(1, groups * size)

    layer_count = bound_logits.shape[0]
    layer_probs = jax.nn.softmax(bound_logits, axis=0)
    layer_index = jnp.arange(layer_count, dtype=jnp.int32)
    layer_pick = ((layer_index >= 1) & (layer_index <= LAYER_AT)).astype(f32)[:, None]
    own_lower = jnp.sum(layer_probs * layer_pick, axis=0)[:, None]
    top, rest = split_hi_lo(own_lower)
    out_own = jnp.concatenate(
        [
            half_rows(w_out),
            top,
            rest,
            (own_lower - top.astype(f32) - rest.astype(f32)).astype(bf16),
            jnp.zeros((ce, 125), bf16),
        ],
        axis=1,
    )
    gain = own_columns(out_gain, ce)

    places = jnp.arange(doc_ids.shape[0], dtype=jnp.int32)
    previous = jnp.concatenate([doc_ids[:1], doc_ids[:-1]])
    keep = ((places % SEQ_LEN != 0) & (doc_ids == previous)).astype(f32)[:, None]
    keep = lax.dynamic_slice_in_dim(keep, g * plane_rows, plane_rows, axis=0)

    token_f = tokens.astype(f32)
    scale_one = lax.rsqrt(jnp.mean(token_f * token_f, axis=-1, keepdims=True) + EPS)
    normed_one = token_f * scale_one
    act_one_own = (normed_one * norm_gain).astype(bf16)

    domain_count = counts.shape[0]
    domain_hits = domain_tags[:, None] == jnp.arange(domain_count, dtype=jnp.int32)[None, :]
    per_token = jnp.sum(jnp.where(domain_hits, counts[None, :], 0), axis=1).astype(f32)
    seq_total = doc_ids.shape[0] // SEQ_LEN
    grad_z = cotangent.astype(f32) * (seq_total / (domain_count * per_token))[:, None]

    ffn_own = jnp.concatenate(
        [
            columns(w, fe)[:, :, first:last]
            for first, last in zip(splits[:-1], splits[1:])
            for w in (ffn_gate, ffn_up)
        ],
        axis=2,
    )
    mix_w, out_ext, act_one, grad_m, ffn = spread(
        groups,
        jnp.concatenate([columns(w_in, ce), columns(w_forget, ce), columns(w_gate_out, ce)], axis=2),
        ffn_own,
        out_own,
        act_one_own,
        grad_z.astype(bf16),
        0,
    )
    mix_w = mix_w.reshape(width, 3 * chan)
    down_w = gather_rows(half_rows(ffn_down))
    ffn, down_w = lax.optimization_barrier((ffn.reshape(-1, 2 * unit), down_w))
    ffn_all = gather_rows(ffn)
    act_one, grad_m = act_one.reshape(plane_rows, width), grad_m.reshape(plane_rows, width)
    out_ext = out_ext.reshape(chan, -1)
    out_w = out_ext[:, :width]
    lower = jnp.sum(out_ext[:, width : width + 3].astype(f32), axis=1).reshape(1, chan)

    proj, states, residual, state_scale, act_two = mixer(
        chan,
        act_one,
        mix_w,
        out_ext,
        keep,
        lower,
        gain,
        tokens,
        ffn_gain.reshape(1, width),
        1,
    )
    act_two = act_two.reshape(plane_rows, width)
    branch = residual - token_f
    scale_two = lax.rsqrt(jnp.mean(residual * residual, axis=-1, keepdims=True) + EPS)
    normed_two = residual * scale_two

    def scatter_rows(v):
        return lax.psum_scatter(v, "g", scatter_dimension=0, tiled=True)

    backs = [dot_nt(grad_m, down_w[first:last]) for first, last in zip(splits[:-1], splits[1:])]
    backs, ffn_all = lax.optimization_barrier((backs, ffn_all))
    grads, pre_grads, hiddens, ffn_sums = [], [], [], []
    for first, last in zip(splits[:-1], splits[1:]):
        some = last - first
        pre = dot(act_two, ffn_all[:, 2 * first : 2 * last])
        gate_ffn, up_ffn = pre[:, :some], pre[:, some:]
        sig = jax.nn.sigmoid(gate_ffn)
        gate_silu = gate_ffn * sig
        hidden = (gate_silu * up_ffn).astype(bf16)
        back = backs[first > 0]
        grad_gate = (back * up_ffn * (sig * (1.0 + gate_ffn * (1.0 - sig)))).astype(bf16)
        grad_up = (back * gate_silu).astype(bf16)
        pre_grads.append(jnp.concatenate([grad_gate, grad_up], axis=1))
        hiddens.append(hidden)
        grads.append(
            jnp.concatenate(
                [dot_tn(act_two, pre_grads[-1]).astype(bf16), dot_tn(grad_m, hidden).astype(bf16)], axis=1
            )
        )
        if first == 0:
            kept = grads[0].shape[1] // 128 * 128
            ffn_sums.append(scatter_rows(grads[0][:, :kept]))
            grads[0], act_two = lax.optimization_barrier((grads[0][:, kept:], act_two))
    far_grads = jnp.concatenate(grads, axis=1)
    pre_grads, hiddens, far_grads = lax.optimization_barrier((pre_grads, hiddens, far_grads))
    ffn_sums.append(scatter_rows(far_grads))
    down_part = dot(jnp.concatenate(hiddens, axis=1), down_w).astype(bf16)
    back_part = dot_nt(jnp.concatenate(pre_grads, axis=1), ffn_all).astype(bf16)

    (back_term,) = scatter_plane([back_part], 3)
    scaled_two = back_term * ffn_gain
    grad_resid = grad_z + scale_two * (
        scaled_two - normed_two * jnp.mean(scaled_two * normed_two, axis=-1, keepdims=True)
    )
    grad_branch_own = grad_resid.astype(bf16)
    mean_out = jnp.sum(grad_branch_own.astype(f32) * branch, axis=-1, keepdims=True) / width
    sent = jnp.concatenate(
        [
            grad_branch_own,
            *split_hi_lo(state_scale),
            *split_hi_lo(mean_out),
            jnp.zeros((rows, 124), bf16),
        ],
        axis=1,
    )
    got = gather_plane(sent, 4)
    grad_branch = got[:, :width]
    info = got[:, width:].astype(f32)
    info = jnp.concatenate([info[:, 0:1] + info[:, 1:2], info[:, 2:3] + info[:, 3:4]], axis=1)
    grad_mixed = dot_nt(grad_branch, out_w)
    grad_proj, mixed_out, sums = kernel_call(
        functools.partial(backward_scan, chan),
        [
            jax.ShapeDtypeStruct((plane_rows, 3 * chan), bf16),
            jax.ShapeDtypeStruct((plane_rows, chan), bf16),
            jax.ShapeDtypeStruct((1, chan), f32),
        ],
        proj,
        states,
        grad_mixed,
        info,
        keep,
        lower,
        gain,
    )
    in_part = dot_nt(grad_proj, mix_w).astype(bf16)
    mix_grads = dot_tn(act_one, grad_proj).astype(bf16).reshape(groups, -1, 3 * chan)
    top, rest = split_hi_lo(sums.reshape(chan, 1))
    out_grads = jnp.concatenate(
        [dot_tn(mixed_out, grad_branch).astype(bf16), top, rest, jnp.zeros((chan, 3 * chan - 2), bf16)],
        axis=1,
    )
    folds = out_grads.shape[1] // (3 * chan)
    out_grads = out_grads[:, : folds * 3 * chan].reshape(groups, ce, folds, 3 * chan)
    out_grads = jnp.moveaxis(out_grads, 2, 1).reshape(groups, folds * ce, 3 * chan)
    late_grads = jnp.concatenate([mix_grads, out_grads], axis=1).reshape(-1, 3 * chan)
    late_grads, ffn_sums, in_part, down_part = lax.optimization_barrier(
        (late_grads, ffn_sums, in_part, down_part)
    )
    late_sum = scatter_rows(late_grads)
    mix_sum = late_sum[: width // groups]
    out_sum = jnp.moveaxis(late_sum[width // groups :].reshape(folds, ce, 3 * chan), 1, 0)
    out_sum = out_sum.reshape(ce, -1).astype(f32)
    summed_wout = out_sum[:, :width]
    grad_lower = out_sum[:, width] + out_sum[:, width + 1]
    grad_act, down_term = scatter_plane([in_part, down_part], 6)
    output_rows = (residual + down_term).astype(bf16)

    scaled_one = grad_act * norm_gain
    grad_tokens = grad_resid + scale_one * (
        scaled_one - normed_one * jnp.mean(scaled_one * normed_one, axis=-1, keepdims=True)
    )

    summed_fgate, summed_fup, fdown = [
        v.astype(f32)
        for v in collect([v.reshape(ranks, -1, v.shape[1]) for v in ffn_sums], splits, fe, 7)
    ]
    summed_fdown = fdown.T
    summed_win, summed_wforget, summed_wgate = [
        v.astype(f32) for v in collect([mix_sum.reshape(ranks, -1, 3 * chan)], (0, chan), ce, 8)
    ]
    first = (g * ranks + rank) * ce

    def own_gain(gain, pairs):
        total = sum(jnp.sum(grad * half_rows(w).astype(f32), axis=1) for grad, w in pairs)
        return total / lax.dynamic_slice_in_dim(gain, first, ce, axis=0)

    summed_norm = own_gain(
        norm_gain, ((summed_win, w_in), (summed_wforget, w_forget), (summed_wgate, w_gate_out))
    )
    summed_outg = own_gain(out_gain, ((summed_wout, w_out),))
    summed_ffng = own_gain(ffn_gain, ((summed_fgate, ffn_gate), (summed_fup, ffn_up)))
    grad_probs = layer_pick * grad_lower[None, :]
    grad_bounds = layer_probs * (
        grad_probs - jnp.sum(layer_probs * grad_probs, axis=0, keepdims=True)
    )
    return (
        output_rows,
        grad_tokens,
        summed_win,
        summed_wforget,
        summed_wgate,
        summed_wout,
        summed_fgate,
        summed_fup,
        summed_fdown,
        summed_norm,
        summed_outg,
        summed_ffng,
        grad_bounds,
    )


def solution(mesh):
    seqs, copies = mesh.shape["seq"], mesh.shape["rep"]
    mesh = Mesh(mesh.devices.reshape(seqs // 4, 2, 2, copies), ALL)
    by_rows = P(ALL, None)
    by_seq = P(("g", "p", "c"), None)
    placed = (
        (by_rows, by_rows, P(ALL), P(), P()) + (by_seq,) * 7 + (P(), P(), P(), P(None, ALL))
    )
    return jax.shard_map(
        body,
        mesh=mesh,
        in_specs=placed,
        out_specs=(by_rows,) * 8 + (P(None, ALL),) + (P(ALL),) * 3 + (P(None, ALL),),
        check_vma=False,
    )
```

```python
import functools

import jax
import jax.numpy as jnp
from jax import lax
from jax.experimental import pallas as pl
from jax.experimental.pallas import tpu as pltpu
from jax.sharding import Mesh
from jax.sharding import PartitionSpec as P

LAYER_AT = 12
SEQ_LEN = 1024
EPS = 1e-06
ROWS = 16
QUARTERS = 4
TILES = 12
PLANE = ("p", "c", "x")
ALL = ("g", "p", "c", "x")
f32 = jnp.float32
bf16 = jnp.bfloat16


def split_hi_lo(v):
    hi = v.astype(bf16)
    return hi, (v - hi.astype(f32)).astype(bf16)


def gates(proj, chan, lower):
    ip = proj[:, :chan].astype(bf16).astype(f32)
    sf = jax.nn.sigmoid(proj[:, chan : 2 * chan].astype(bf16).astype(f32))
    forget = lower + (1.0 - lower) * sf
    sig_in = jax.nn.sigmoid(ip)
    return ip, sig_in, sf, forget


def forward_scan(chan, proj_ref, keep_ref, lower_ref, gain_ref, h_ref, o_ref, ss_ref):
    lower = lower_ref[...]
    gain = gain_ref[...]
    row = lax.broadcasted_iota(jnp.int32, (ROWS, chan), 0)

    def step(i, carry):
        rows = pl.ds(pl.multiple_of(i * ROWS, ROWS), ROWS)
        proj = proj_ref[rows, :]
        ip, sig_in, _, forget = gates(proj, chan, lower)
        u = ip * sig_in * (1.0 - forget)
        e = forget * keep_ref[rows, :]
        shift = 1
        while shift < ROWS:
            u = u + e * jnp.where(row >= shift, pltpu.roll(u, shift, 0), 0.0)
            e = e * jnp.where(row >= shift, pltpu.roll(e, shift, 0), 1.0)
            shift *= 2
        h = u + e * carry
        h_ref[rows, :] = h
        hb = h.astype(bf16).astype(f32)
        gate = proj[:, 2 * chan :]
        o_ref[rows, :] = (hb * gain * (gate * jax.nn.sigmoid(gate))).astype(bf16)
        ss_ref[rows, :] = jnp.sum(hb * hb, axis=1, keepdims=True)
        return h[ROWS - 1 : ROWS, :]

    lax.fori_loop(0, proj_ref.shape[0] // ROWS, step, jnp.zeros((1, chan), f32))


def mixer_kernel(
    groups,
    chan,
    act_hbm,
    mix_hbm,
    grad_hbm,
    down_hbm,
    near_ref,
    far_ref,
    out_w_hbm,
    keep_ref,
    gain_ref,
    token_hbm,
    ffn_gain_ref,
    proj_hbm,
    h_hbm,
    pre_grad_hbm,
    kept_hbm,
    near_hbm,
    residual_hbm,
    hidden_hbm,
    rest_hbm,
    act_two_ref,
    far_all,
    scale_ref,
    lower_ref,
    token_ref,
    out_w_ref,
    act_ref,
    mix_ref,
    grad_ref,
    down_ref,
    proj_ref,
    h_ref,
    pre_grad_ref,
    kept_ref,
    near_all,
    residual_ref,
    hidden_ref,
    rest_ref,
    raw,
    squares,
    part,
    theirs,
    outgoing,
    landing,
    own_two,
    two,
    pre_ref,
    grad_tmp,
    swap_send,
    swap_recv,
    send_sem,
    recv_sem,
    local_sem,
    move_sem,
    act_send,
    act_recv,
    line_send,
    line_recv,
):
    moves = []

    def move(src, dst):
        copy = pltpu.make_async_copy(src, dst, move_sem.at[len(moves)])
        copy.start()
        moves.append(copy)
        return copy

    loads = [
        move(*pair)
        for pair in ((act_hbm, act_ref), (mix_hbm, mix_ref), (grad_hbm, grad_ref), (out_w_hbm, out_w_ref), (token_hbm, token_ref))
    ]
    chips, core = places()
    sibling = device_at(chips[3], 1 - core)
    greet([device_at(chip, core) for chip in chips[:3]] + [sibling] + line_partners(groups))
    near = Line(groups, near_ref, near_all, line_send.at[0], line_recv.at[0], local_sem.at[1])
    far = Line(groups, far_ref, far_all, line_send.at[1], line_recv.at[1], local_sem.at[2])
    near.send(1)
    far.send(1)
    loads.append(move(down_hbm.at[pl.ds(0, down_ref.shape[0])], down_ref))
    rows, width = token_hbm.shape
    block = 2 * rows
    loads[3].wait()
    loads[4].wait()
    turned = jnp.transpose(out_w_ref[:, width:].astype(f32))
    lower_ref[...] = turned[0:1, :] + turned[1:2, :] + turned[2:3, :]
    loads[0].wait()
    loads[1].wait()

    def project(i, _):
        at = pl.ds(pl.multiple_of(i * block, block), block)
        proj_ref[at, :] = dot(act_ref[at, :], mix_ref[...])
        return 0

    lax.fori_loop(0, act_ref.shape[0] // block, project, 0)
    forward_scan(chan, proj_ref, keep_ref, lower_ref, gain_ref, h_ref, raw, squares)
    near.step(1)
    move(proj_ref, proj_hbm)
    move(h_ref, h_hbm)

    lane = lax.broadcasted_iota(jnp.int32, (rows, part.shape[1] - width), 1)

    def mixed(rank):
        at = pl.ds(pl.multiple_of(rank * rows, rows), rows)
        part[at, :width] = dot(raw[at, :], out_w_ref[:, :width]).astype(bf16)
        top, rest = split_hi_lo(squares[at, :])
        side = jnp.where(lane == 0, top.astype(f32), jnp.where(lane == 1, rest.astype(f32), 0.0))
        part[at, width:] = side.astype(bf16)
        return part.at[at]

    swaps = []
    for j, chip in enumerate(chips):
        swaps.append(
            remote(
                mixed(rank_at(chip, 1 - core)), theirs.at[j], swap_send.at[j], swap_recv.at[j], sibling
            )
        )
    scatter = Scatter([], theirs, outgoing, landing, send_sem, recv_sem)
    for j, chip in enumerate(chips):
        scatter.mine.append(mixed(rank_at(chip, core)))
        swaps[j].wait_recv()
        if j < 3:
            scatter.first(j)
    far.step(1)
    scatter.second()

    def finish(at, total):
        scale = lax.rsqrt((total[:, width : width + 1] + total[:, width + 1 : width + 2]) / width + EPS)
        scale_ref[at, :] = scale
        residual = token_ref[at, :].astype(f32) + total[:, :width] * scale
        residual_ref[at, :] = residual
        norm = lax.rsqrt(jnp.mean(residual * residual, axis=-1, keepdims=True) + EPS)
        own_two[at, :] = (residual * norm * ffn_gain_ref[...]).astype(bf16)

    scatter.totals(finish)
    move(residual_ref, residual_hbm)
    plane = Plane(own_two, two, local_sem.at[0], act_send, act_recv)
    plane.start(1)
    plane.start(2)
    plane.start_own()
    for copy in swaps:
        copy.wait_send()
    scatter.finish()
    near.step(2)
    plane.hand_on(1)
    plane.hand_on(2)
    far.step(2)
    plane.hand_on(0)
    for k in range(3, groups):
        near.step(k)
    plane.finish()
    near.finish()
    move(two, act_two_ref)
    move(near_all, near_hbm)
    loads[2].wait()
    loads[5].wait()

    some = hidden_ref.shape[1]
    depth = near_all.shape[1]

    def quarter(i, _):
        at = pl.ds(pl.multiple_of(i * block, block), block)
        act = two[pl.ds(2 * i, 2)].reshape(block, width)
        pre = jnp.zeros((block, near_all.shape[2]), f32)
        for g in range(groups):
            pre += dot(act[:, g * depth : (g + 1) * depth], near_all[g])
        pre_ref[...] = pre
        gate, up = pre_ref[:, :some], pre_ref[:, some : 2 * some]
        back = dot_nt(grad_ref[at, :], down_ref[...])
        sig = jax.nn.sigmoid(gate)
        gate_silu = gate * sig
        hidden_ref[at, :] = (gate_silu * up).astype(bf16)
        pre_ref[:, :some] = back * up * (sig * (1.0 + gate * (1.0 - sig)))
        pre_ref[:, some : 2 * some] = back * gate_silu
        pre_grad_ref[at, :] = pre_ref[:, : 2 * some].astype(bf16)
        return 0

    lax.fori_loop(0, act_ref.shape[0] // block, quarter, 0)

    def weights(i, _):
        at = pl.ds(pl.multiple_of(i * block, block), block)
        act = two[:, :, at].reshape(act_ref.shape[0], block)
        grad_tmp[:, : 2 * some] = dot_tn(act, pre_grad_ref[...])
        grad_tmp[:, 2 * some : 3 * some] = dot_tn(grad_ref[:, at], hidden_ref[...])
        kept = kept_ref.shape[1]
        kept_ref[at, :] = grad_tmp[:, :kept].astype(bf16)
        rest_ref[at, :] = grad_tmp[:, kept : 3 * some].astype(bf16)
        return 0

    lax.fori_loop(0, width // block, weights, 0)
    move(pre_grad_ref, pre_grad_hbm)
    move(kept_ref, kept_hbm)
    move(hidden_ref, hidden_hbm)
    move(rest_ref, rest_hbm)
    for k in range(3, groups):
        far.step(k)
    far.finish()
    for copy in moves[6:]:
        copy.wait()


def mixer(
    groups, chan, act, mix_w, out_ext, keep, gain, tokens, ffn_gain, grad, down, some, near, far, ident
):
    total, (rows, width) = act.shape[0], tokens.shape
    vmem, hbm = pl.BlockSpec(memory_space=pltpu.VMEM), pl.BlockSpec(memory_space=pl.ANY)
    dma = pltpu.SemaphoreType.DMA
    wide = width + 128
    kept = 3 * some // 128 * 128
    moved = [
        jax.ShapeDtypeStruct((total, 3 * chan), f32),
        jax.ShapeDtypeStruct((total, chan), f32),
        jax.ShapeDtypeStruct((total, 2 * some), bf16),
        jax.ShapeDtypeStruct((width, kept), bf16),
        jax.ShapeDtypeStruct((groups,) + near.shape, bf16),
        jax.ShapeDtypeStruct((rows, width), f32),
        jax.ShapeDtypeStruct((total, some), bf16),
        jax.ShapeDtypeStruct((width, 3 * some - kept), bf16),
    ]
    return pl.pallas_call(
        functools.partial(mixer_kernel, groups, chan),
        out_shape=moved
        + [
            jax.ShapeDtypeStruct((8, rows, width), bf16),
            jax.ShapeDtypeStruct((groups,) + far.shape, bf16),
            jax.ShapeDtypeStruct((rows, 1), f32),
            jax.ShapeDtypeStruct((1, chan), f32),
        ],
        in_specs=[hbm] * 7 + [vmem] * 2 + [hbm, vmem],
        out_specs=[hbm] * 10 + [vmem] * 2,
        scratch_shapes=[pltpu.VMEM(v.shape, v.dtype) for v in (tokens, out_ext, act, mix_w, grad)]
        + [pltpu.VMEM((some, width), bf16)]
        + [pltpu.VMEM(v.shape, v.dtype) for v in moved]
        + [
            pltpu.VMEM((total, chan), bf16),
            pltpu.VMEM((total, 1), f32),
            pltpu.VMEM((total, wide), bf16),
            pltpu.VMEM((4, rows, wide), bf16),
            pltpu.VMEM((6, rows // 2, wide), bf16),
            pltpu.VMEM((6, rows // 2, wide), bf16),
            pltpu.VMEM((rows, width), bf16),
            pltpu.VMEM((8, rows, width), bf16),
            pltpu.VMEM((2 * rows, near.shape[1]), f32),
            pltpu.VMEM((2 * rows, 3 * some), f32),
            dma((4,)),
            dma((4,)),
            dma((6,)),
            dma((6,)),
            dma((3,)),
            dma((15,)),
            dma((8,)),
            dma((8,)),
            dma((2, 2, groups - 1)),
            dma((2, 2, groups - 1)),
        ],
        compiler_params=pltpu.CompilerParams(
            collective_id=ident, has_side_effects=True, vmem_limit_bytes=60 * 2**20
        ),
    )(act, mix_w, grad, down, near, far, out_ext, keep, gain, tokens, ffn_gain)


def feed_kernel(
    first,
    act_hbm,
    grad_hbm,
    near_hbm,
    far_hbm,
    down_hbm,
    pre_first_ref,
    rest_ref,
    weights_hbm,
    pre_grad_hbm,
    hidden_hbm,
    act_ref,
    grad_ref,
    near_ref,
    far_ref,
    down_ref,
    weights_ref,
    pre_grad_ref,
    hidden_ref,
    wide_ref,
    side_ref,
    lead_ref,
    fold_ref,
    move_sem,
    store_sem,
):
    moves = []

    def move(src, dst):
        copy = pltpu.make_async_copy(src, dst, move_sem.at[len(moves)])
        copy.start()
        moves.append(copy)

    for pair in (
        (act_hbm, act_ref),
        (near_hbm, near_ref),
        (far_hbm, far_ref),
        (grad_hbm, grad_ref),
        (down_hbm, down_ref),
    ):
        move(*pair)
    loads = len(moves)
    for copy in moves[:3]:
        copy.wait()
    near, width = near_ref.shape[1], act_ref.shape[1]
    unit = down_ref.shape[0]
    some, lead = unit - first, near - 2 * first
    block = 256

    def tokens(i, _):
        at = pl.ds(pl.multiple_of(i * block, block), block)
        wide_ref[:, :near] = dot(act_ref[at, :], near_ref[...])
        wide_ref[:, near:] = dot(act_ref[at, :], far_ref[...])

        @pl.when(i == 0)
        def _():
            moves[3].wait()
            moves[4].wait()

        gate = wide_ref[:, 2 * first : 2 * first + some]
        up = wide_ref[:, 2 * first + some :]
        back = dot_nt(grad_ref[at, :], down_ref[first:, :])
        sig = jax.nn.sigmoid(gate)
        gate_silu = gate * sig
        hidden_ref[at, :] = (gate_silu * up).astype(bf16)
        wide_ref[:, : 2 * first] = pre_first_ref[at, :].astype(f32)
        wide_ref[:, 2 * first : 2 * first + some] = back * up * (sig * (1.0 + gate * (1.0 - sig)))
        wide_ref[:, 2 * first + some :] = back * gate_silu
        pre_grad_ref[at, :] = wide_ref[...].astype(bf16)
        return 0

    lax.fori_loop(0, act_ref.shape[0] // block, tokens, 0)
    move(pre_grad_ref, pre_grad_hbm)
    move(hidden_ref, hidden_hbm)

    groups = weights_ref.shape[0]
    part = width // groups
    rows = part // 8
    tail = 64

    def weights(g, _):
        at = pl.ds(pl.multiple_of(g * part, part), part)
        act, grad = act_ref[:, at], grad_ref[:, at]
        full = dot_tn(act, pre_grad_ref[:, near:]).astype(bf16)
        lead_ref[...] = dot_tn(act, pre_grad_ref[:, near - 128 : near])
        side_ref[:, :lead] = lead_ref[:, 128 - lead :]
        side_ref[:, lead : lead + some] = dot_tn(grad, hidden_ref[...])
        side_ref[:, lead + some :] = rest_ref[at, :].astype(f32)
        side = side_ref[...].astype(bf16)
        for k in range(8):
            for t in range(TILES):
                source, skipped = (full, 0) if t * 128 < 2 * unit - near else (side, 2 * unit - near)
                column = t * 128 - skipped
                place = (k * TILES + t) * rows
                weights_ref[g, place : place + rows, :] = source[
                    k * rows : (k + 1) * rows, column : column + 128
                ]
        last = side_ref.shape[1] - tail
        fold_ref[:, :tail] = side_ref[: part // 2, last:]
        fold_ref[:, tail:] = side_ref[part // 2 :, last:]
        weights_ref[g, 8 * TILES * rows :, :] = fold_ref[...].astype(bf16)
        store(g).start()
        return 0

    def store(g):
        return pltpu.make_async_copy(weights_ref.at[g], weights_hbm.at[g], store_sem.at[g])

    lax.fori_loop(0, groups, weights, 0)
    for g in range(groups):
        store(g).wait()
    for copy in moves[loads:]:
        copy.wait()


def feed(groups, act, grad, near, far, down, pre_first, rest):
    (total, width), unit, first = act.shape, down.shape[0], pre_first.shape[1] // 2
    side = near.shape[1] - 2 * first + unit - first + rest.shape[1]
    vmem, hbm = pl.BlockSpec(memory_space=pltpu.VMEM), pl.BlockSpec(memory_space=pl.ANY)
    outs = [
        jax.ShapeDtypeStruct((groups, (8 * TILES + 4) * (width // (8 * groups)), 128), bf16),
        jax.ShapeDtypeStruct((total, 2 * unit), bf16),
        jax.ShapeDtypeStruct((total, unit - first), bf16),
    ]
    return pl.pallas_call(
        functools.partial(feed_kernel, first),
        out_shape=outs,
        in_specs=[hbm] * 5 + [vmem] * 2,
        out_specs=[hbm] * 3,
        scratch_shapes=[pltpu.VMEM(v.shape, bf16) for v in (act, grad, near, far, down, *outs)]
        + [
            pltpu.VMEM((256, 2 * unit), f32),
            pltpu.VMEM((width // groups, side), f32),
            pltpu.VMEM((width // groups, 128), f32),
            pltpu.VMEM((width // (2 * groups), 128), f32),
            pltpu.SemaphoreType.DMA((7,)),
            pltpu.SemaphoreType.DMA((groups,)),
        ],
        compiler_params=pltpu.CompilerParams(vmem_limit_bytes=60 * 2**20),
    )(act, grad, near, far, down, pre_first, rest)


def backward_scan(
    chan, proj_ref, h_ref, do_ref, info_ref, keep_ref, lower_ref, gain_ref, grad_ref, o_ref, sums_ref
):
    lower = lower_ref[...]
    gain = gain_ref[...]
    row = lax.broadcasted_iota(jnp.int32, (ROWS, chan), 0)
    blocks = proj_ref.shape[0] // ROWS

    def step(j, carried):
        later, sum_lower = carried
        i = blocks - 1 - j
        rows = pl.ds(pl.multiple_of(i * ROWS, ROWS), ROWS)
        proj = proj_ref[rows, :]
        ip, sig_in, sf, forget = gates(proj, chan, lower)
        keep = keep_ref[rows, :]
        act_in = ip * sig_in
        h = h_ref[rows, :]
        before = h_ref[pl.ds(pl.multiple_of(jnp.maximum(i * ROWS - 8, 0), 8), 8), :][7:8, :]
        h_prev = jnp.where(row >= 1, pltpu.roll(h, 1, 0), before)
        scale = info_ref[rows, 0:1]
        mean = info_ref[rows, 1:2]
        hn = h.astype(bf16).astype(f32) * scale
        gate = proj[:, 2 * chan :]
        sig_gate = jax.nn.sigmoid(gate)
        gate_act = gate * sig_gate
        do = do_ref[rows, :]
        o_ref[rows, :] = (hn * gain * gate_act).astype(bf16)
        dgp = do * hn * gain * (sig_gate * (1.0 + gate * (1.0 - sig_gate)))
        dhb = scale * (do * gain * gate_act - hn * mean)
        d = dhb.astype(bf16).astype(f32)
        e = forget * keep
        c = jnp.where(row < ROWS - 1, pltpu.roll(e, ROWS - 1, 0), 1.0)
        shift = 1
        while shift < ROWS:
            inside = row < ROWS - shift
            d = d + c * jnp.where(inside, pltpu.roll(d, ROWS - shift, 0), 0.0)
            c = c * jnp.where(inside, pltpu.roll(c, ROWS - shift, 0), 1.0)
            shift *= 2
        dh = d + c * later
        dip = dh * (1.0 - forget) * (sig_in * (1.0 + ip * (1.0 - sig_in)))
        df = dh * (h_prev * keep - act_in)
        tail = df * (1.0 - sf)
        dfp = tail * (1.0 - lower) * sf
        grad_ref[rows, :] = jnp.concatenate([dip, dfp, dgp], axis=1).astype(bf16)
        sum_lower = sum_lower + jnp.sum(tail, axis=0, keepdims=True)
        return (e * dh)[0:1, :], sum_lower

    zero = jnp.zeros((1, chan), f32)
    _, sum_lower = lax.fori_loop(0, blocks, step, (zero, zero))
    sums_ref[...] = sum_lower


def kernel_call(kernel, outs, *args):
    vmem = pl.BlockSpec(memory_space=pltpu.VMEM)
    return pl.pallas_call(
        kernel,
        out_shape=outs,
        in_specs=[vmem] * len(args),
        out_specs=[vmem] * len(outs),
        compiler_params=pltpu.CompilerParams(vmem_limit_bytes=48 * 2**20),
    )(*args)


MESH = pl.DeviceIdType.MESH


def places():
    g, p, c, x = (lax.axis_index(a) for a in ALL)
    flips = ((1, 1), (0, 1), (1, 0), (0, 0))
    chips = [(g, p + dp * (1 - 2 * p), x + dx * (1 - 2 * x)) for dp, dx in flips]
    return chips, c


def device_at(chip, core):
    return (chip[0], chip[1], core, chip[2])


def rank_at(chip, core):
    return (chip[1] * 2 + core) * 2 + chip[2]


def greet(partners):
    barrier = pltpu.get_barrier_semaphore()
    for partner in partners:
        pl.semaphore_signal(barrier, inc=1, device_id=partner, device_id_type=MESH)
    pl.semaphore_wait(barrier, len(partners))


def remote(src, dst, send_sem, recv_sem, device):
    copy = pltpu.make_async_remote_copy(
        src_ref=src, dst_ref=dst, send_sem=send_sem, recv_sem=recv_sem, device_id=device, device_id_type=MESH
    )
    copy.start()
    return copy


class Line:
    def __init__(self, groups, own_ref, out_ref, send_sem, recv_sem, local_sem=None, part=None):
        self.groups, self.own, self.out, self.part = groups, own_ref, out_ref, part
        self.send_sem, self.recv_sem = send_sem, recv_sem
        self.g, self.p, self.c, self.x = (lax.axis_index(a) for a in ALL)
        self.kept = None
        if local_sem is not None:
            self.kept = pltpu.make_async_copy(own_ref, out_ref.at[self.g], local_sem)
            self.kept.start()

    def view(self, block):
        return self.out.at[block] if self.part is None else self.out.at[block, self.part]

    def at_step(self, way, k):
        block = self.g - (k - 1) if way == 0 else self.g + (k - 1)
        return pltpu.make_async_remote_copy(
            src_ref=self.own if k == 1 else self.view(block),
            dst_ref=self.view(block),
            send_sem=self.send_sem.at[way, k - 1],
            recv_sem=self.recv_sem.at[way, k - 1],
            device_id=(self.g + (1 if way == 0 else -1), self.p, self.c, self.x),
            device_id_type=MESH,
        )

    def behind(self, way, k):
        return self.g >= k if way == 0 else self.g + k < self.groups

    def sends(self, way, k):
        return self.behind(way, k - 1) & self.behind(1 - way, 1)

    def send(self, k):
        for way in (0, 1):

            @pl.when(self.sends(way, k))
            def _(way=way):
                self.at_step(way, k).start()

    def arrived(self, way, k):
        got = self.view(self.g - k if way == 0 else self.g + k)
        pltpu.make_async_remote_copy(
            src_ref=got,
            dst_ref=got,
            send_sem=self.send_sem.at[way, k - 1],
            recv_sem=self.recv_sem.at[way, k - 1],
            device_id=(self.g, self.p, self.c, self.x),
            device_id_type=MESH,
        ).wait_recv()

    def step(self, k):
        for way in (0, 1):

            @pl.when(self.behind(way, k))
            def _(way=way):
                self.arrived(way, k)

        if k + 1 < self.groups:
            self.send(k + 1)

    def finish(self):
        if self.kept is not None:
            self.kept.wait()
        for k in range(1, self.groups):
            for way in (0, 1):

                @pl.when(self.sends(way, k))
                def _(way=way, k=k):
                    self.at_step(way, k).wait_send()


def line_partners(groups):
    g, p, c, x = (lax.axis_index(a) for a in ALL)
    offsets = sorted({1 % groups, -1 % groups} - {0})
    return [(lax.rem(g + k, groups), p, c, x) for k in offsets]


class Plane:
    def __init__(self, own_ref, out_ref, local_sem, send_sem, recv_sem):
        self.own, self.out = own_ref, out_ref
        self.send_sem, self.recv_sem = send_sem, recv_sem
        self.chips, self.core = places()
        self.half = own_ref.shape[0] // 2
        self.slot = out_ref.at[rank_at(self.chips[3], self.core)]
        self.sibling = device_at(self.chips[3], 1 - self.core)
        self.local = pltpu.make_async_copy(own_ref, self.slot, local_sem)
        self.sent, self.passed = {}, []

    def send(self, n, src, dst, device):
        return remote(src, dst, self.send_sem.at[n], self.recv_sem.at[n], device)

    def start_own(self):
        self.local.start()
        self.passed.append(self.send(3, self.own, self.slot, self.sibling))

    def start(self, i):
        self.sent[i] = self.send(i, self.own, self.slot, device_at(self.chips[i], self.core))

    def hand_on(self, i):
        got = self.out.at[rank_at(self.chips[i], self.core)]
        if i:
            self.sent[i].wait_recv()
            n, first = (0, 0) if i == 1 else (7, self.half)
            part = got.at[pl.ds(first, self.half)]
            self.sent[n] = self.send(n, part, part, device_at(self.chips[3 - i], self.core))
        else:
            self.sent[0].wait_recv()
            self.sent[7].wait_recv()
        self.passed.append(self.send(4 + i, got, got, self.sibling))

    def finish(self):
        for copy in self.sent.values():
            copy.wait_send()
        for copy in self.passed:
            copy.wait()
        self.local.wait()


class Scatter:
    def __init__(self, mine, theirs, outgoing, landing, send_sem, recv_sem):
        self.mine, self.theirs, self.outgoing, self.landing = mine, theirs, outgoing, landing
        self.send_sem, self.recv_sem = send_sem, recv_sem
        self.chips, self.core = places()
        self.half = outgoing.shape[1]
        self.sent = []

    def both(self, j, at):
        return self.mine[j][at, :].astype(f32) + self.theirs[j, at, :].astype(f32)

    def send(self, n, j, bottom, to, arrived=None):
        def add(i, _):
            near = pl.ds(pl.multiple_of(i * ROWS, ROWS), ROWS)
            at = pl.ds(pl.multiple_of(i * ROWS + bottom * self.half, ROWS), ROWS)
            total = self.both(j, at)
            if arrived is not None:
                total = total + self.landing[arrived, near, :].astype(f32)
            self.outgoing[n, near, :] = total.astype(bf16)
            return 0

        lax.fori_loop(0, self.half // ROWS, add, 0)
        self.sent.append(
            remote(
                self.outgoing.at[n],
                self.landing.at[n],
                self.send_sem.at[n],
                self.recv_sem.at[n],
                device_at(self.chips[to], self.core),
            )
        )

    def first(self, j):
        if j in (0, 1):
            self.send(j, j, 0, 1)
        if j in (0, 2):
            self.send(2 if j == 0 else 3, j, 1, 2)

    def second(self):
        arrived = [self.sent[n].wait_recv for n in (0, 2, 1, 3)]
        arrived[0]()
        self.send(4, 2, 0, 2, 0)
        arrived[2]()
        self.send(5, 1, 1, 1, 2)
        arrived[1]()
        arrived[3]()
        self.sent[4].wait_recv()
        self.sent[5].wait_recv()

    def totals(self, use):
        for bottom in (0, 1):

            def one(i, _, bottom=bottom):
                near = pl.ds(pl.multiple_of(i * ROWS, ROWS), ROWS)
                at = pl.ds(pl.multiple_of(i * ROWS + bottom * self.half, ROWS), ROWS)
                total = self.both(3, at)
                for n in (1 + 2 * bottom, 4 + bottom):
                    total = total + self.landing[n, near, :].astype(f32)
                use(at, total)
                return 0

            lax.fori_loop(0, self.half // ROWS, one, 0)

    def finish(self):
        for copy in self.sent:
            copy.wait_send()


def gather_kernel(own_ref, out_ref, local_sem, send_sem, recv_sem):
    plane = Plane(own_ref, out_ref, local_sem, send_sem, recv_sem)
    greet([device_at(chip, plane.core) for chip in plane.chips[:3]] + [plane.sibling])
    plane.start(1)
    plane.start(2)
    plane.start_own()
    for i in (1, 2, 0):
        plane.hand_on(i)
    plane.finish()


def spread_kernel(
    groups,
    splits,
    *refs,
):
    mixers, units = refs[:3], refs[3:5]
    out_ref, act_ref, grad_ref, mix_all, out_all, act_all, grad_all, near_all, far_all = refs[5:14]
    mix_ref, near_ref, far_ref, wide_ref = refs[14:18]
    local_sem, swap_send, swap_recv = refs[18:21]
    mix_send, mix_recv, out_send, out_recv, act_send, act_recv, grad_send, grad_recv = refs[21:]
    chips, core = places()
    here, other = chips[3], chips[2]
    g = here[0]
    swaps = [device_at(here, 1 - core), device_at(other, core), device_at(other, 1 - core)]
    greet([device_at(chip, core) for chip in chips[:3]] + [swaps[0], swaps[2]] + line_partners(groups))
    own = here[1] * 2 + core
    targets = [here[1] * 2 + 1 - core, other[1] * 2 + core, other[1] * 2 + 1 - core]

    def swap(src, dst, first):
        return [
            remote(
                src.at[targets[i]], dst, swap_send.at[first + i], swap_recv.at[first + i], swaps[i]
            )
            for i in range(3)
        ]

    out_line = Line(groups, out_ref, out_all, out_send, out_recv)
    out_line.send(1)
    act = Plane(act_ref, act_all, local_sem.at[3], act_send, act_recv)
    grad = Plane(grad_ref, grad_all, local_sem.at[4], grad_send, grad_recv)
    act.start_own()
    grad.start_own()
    act.start(1)

    def gather_columns(pieces, m, x):
        place = 0
        for ref, size, first, last in pieces:
            for group in range(first // size, last // size):
                start = ((group * 4 + m) * 2 + x) * size
                wide_ref[:, place : place + size] = ref[:, start : start + size].astype(f32)
                place += size
        return place

    def fill(make):
        for x in (0, 1):

            @pl.when(here[2] == x)
            def _(x=x):
                for m in range(4):
                    make(m, x)

    def mix_columns(m, x):
        size = mixers[0].shape[1] // (8 * groups)
        place = gather_columns([(ref, size, 0, size * groups) for ref in mixers], m, x)
        mix_ref[m] = wide_ref[:, :place].astype(bf16)

    def unit_columns(m, x):
        size = units[0].shape[1] // (8 * groups)
        place = gather_columns(
            [(ref, size, first, last) for first, last in zip(splits[:-1], splits[1:]) for ref in units], m, x
        )
        near = near_ref.shape[2]
        near_ref[m] = wide_ref[:, :near].astype(bf16)
        far_ref[m] = wide_ref[:, near:place].astype(bf16)

    fill(mix_columns)
    mix_copies = swap(mix_ref, mix_all.at[g, own], 0)
    locals_ = [
        pltpu.make_async_copy(mix_ref.at[own], mix_all.at[g, own], local_sem.at[0]),
        pltpu.make_async_copy(out_ref, out_all.at[g], local_sem.at[2]),
    ]
    for copy in locals_:
        copy.start()
    mix_line = Line(groups, mix_all.at[g], mix_all, mix_send, mix_recv)
    for copy in mix_copies:
        copy.wait()
    locals_[0].wait()
    mix_line.send(1)
    act.start(2)
    fill(unit_columns)
    ffn_copies = swap(near_ref, near_all.at[own], 3) + swap(far_ref, far_all.at[own], 6)
    for copy in (
        pltpu.make_async_copy(near_ref.at[own], near_all.at[own], local_sem.at[1]),
        pltpu.make_async_copy(far_ref.at[own], far_all.at[own], local_sem.at[5]),
    ):
        copy.start()
        locals_.append(copy)
    out_line.step(1)
    act.hand_on(1)
    act.hand_on(2)
    grad.start(1)
    grad.start(2)
    mix_line.step(1)
    act.hand_on(0)
    for k in range(2, groups):
        out_line.step(k)
        mix_line.step(k)
        if k == 2:
            grad.hand_on(1)
            grad.hand_on(2)
    grad.hand_on(0)
    for copy in ffn_copies:
        copy.wait()
    for copy in locals_[1:]:
        copy.wait()
    out_line.finish()
    mix_line.finish()
    act.finish()
    grad.finish()


def spread(groups, splits, near, mixers, units, out, act, grad, ident):
    vmem, hbm, dma = (
        pl.BlockSpec(memory_space=pltpu.VMEM),
        pl.BlockSpec(memory_space=pl.ANY),
        pltpu.SemaphoreType.DMA,
    )
    rows = mixers[0].shape[0]
    mix = (4, rows, 3 * mixers[0].shape[1] // 8)
    sides = [(4, rows, near), (4, rows, 2 * splits[-1] - near)]
    return pl.pallas_call(
        functools.partial(spread_kernel, groups, splits),
        out_shape=[
            jax.ShapeDtypeStruct((groups,) + mix, bf16),
            jax.ShapeDtypeStruct((groups,) + out.shape, bf16),
            jax.ShapeDtypeStruct((8,) + act.shape, bf16),
            jax.ShapeDtypeStruct((8,) + grad.shape, bf16),
        ]
        + [jax.ShapeDtypeStruct(shape, bf16) for shape in sides],
        in_specs=[vmem] * 5 + [hbm] * 3,
        out_specs=[hbm] * 6,
        scratch_shapes=[pltpu.VMEM(shape, bf16) for shape in (mix, *sides)]
        + [pltpu.VMEM((rows, 2 * splits[-1]), f32)]
        + [dma((6,)), dma((9,)), dma((9,))]
        + [dma((2, groups - 1))] * 4
        + [dma((8,))] * 4,
        compiler_params=pltpu.CompilerParams(
            collective_id=ident, has_side_effects=True, vmem_limit_bytes=62 * 2**20
        ),
    )(*mixers, *units, out, act, grad)


def scatter_kernel(count, *refs):
    parts, outs = refs[:count], refs[count : 2 * count]
    mine, theirs, outgoing, landing, local_sem, send_sem, recv_sem = refs[2 * count :]
    chips, core = places()
    sibling = device_at(chips[3], 1 - core)
    greet([device_at(chip, core) for chip in chips[:3]] + [sibling])
    swaps, locals_, sent = [], [], []
    for n in range(count):
        for j, chip in enumerate(chips):
            swaps.append(
                remote(
                    parts[n].at[rank_at(chip, 1 - core)],
                    theirs.at[n, j],
                    send_sem.at[n, j],
                    recv_sem.at[n, j],
                    sibling,
                )
            )
            local = pltpu.make_async_copy(
                parts[n].at[rank_at(chip, core)], mine.at[n, j], local_sem.at[n, j]
            )
            local.start()
            locals_.append(local)
    scatters = []
    for n in range(count):
        scatter = Scatter(
            [mine.at[n, j] for j in range(4)],
            theirs.at[n],
            outgoing.at[n],
            landing.at[n],
            send_sem.at[n, pl.ds(4, 6)],
            recv_sem.at[n, pl.ds(4, 6)],
        )
        for j in range(4):
            locals_[4 * n + j].wait()
            swaps[4 * n + j].wait_recv()
            if j < 3:
                scatter.first(j)
        scatters.append(scatter)
    for n, scatter in enumerate(scatters):
        scatter.second()

        def store(at, total, n=n):
            outs[n][at, :] = total

        scatter.totals(store)
    for scatter in scatters:
        scatter.finish()
    for copy in swaps:
        copy.wait_send()


def collect_kernel(streams, segments, size, rows, *refs):
    count = len(streams)
    parts, outs = refs[:count], refs[count : count + 3]
    landing = refs[count + 3 : 2 * count + 3]
    wholes = refs[2 * count + 3 : 2 * count + 6]
    local_sem, send_sem, recv_sem = refs[2 * count + 6 :]
    chips, core = places()
    others = [(j, chips[j], other) for j in range(4) for other in (core, 1 - core)]
    own = rank_at(chips[3], core)
    targets = [(chip, other) for j, chip, other in others if not (j == 3 and other is core)]
    greet([device_at(chip, other) for chip, other in targets])

    def source(n, rank):
        base, among, step = streams[n]
        return parts[n].at[pl.ds(pl.multiple_of(base + lax.rem(rank, among) * step, step), step)]

    copies, locals_ = [], []
    for n in range(count):
        for i, (chip, other) in enumerate(targets):
            copies.append(
                remote(
                    source(n, rank_at(chip, other)),
                    landing[n].at[own],
                    send_sem.at[n, i],
                    recv_sem.at[n, i],
                    device_at(chip, other),
                )
            )
        local = pltpu.make_async_copy(source(n, own), landing[n].at[own], local_sem.at[n])
        local.start()
        locals_.append(local)
    for copy in locals_:
        copy.wait()
    for copy in copies:
        copy.wait_recv()

    def lay(which, place, n, k, low, high):
        if n == 0:
            wholes[which][:, place : place + high - low] = landing[0][k, :, low:high].astype(f32)
            return
        while low < high:
            tile = low // 128
            end = min(high, (tile + 1) * 128)
            at = slice(place, place + end - low)
            first, last = low - tile * 128, end - tile * 128
            if tile < TILES:
                wholes[which][:, at] = landing[1][k, tile * rows : (tile + 1) * rows, first:last].astype(f32)
            else:
                for side in (0, 1):

                    @pl.when(chips[3][1] == side)
                    def _(side=side, at=at, first=first, last=last):
                        wholes[which][:, at] = landing[2][k, :, 64 * side + first : 64 * side + last].astype(f32)

            place, low = place + end - low, end

    for n, column, which, first, length in segments:
        for group in range(first // size, -(-(first + length) // size)):
            low, high = max(first, group * size), min(first + length, (group + 1) * size)
            for k in range(8):
                lay(which, group * 7 * size + k * size + low, n, k, column + low - first, column + high - first)
    for out, whole in zip(outs, wholes):
        out[...] = whole[...].astype(bf16)
    for copy in copies:
        copy.wait_send()


def collect(parts, streams, rows, segments, size, wide, ident):
    count = len(parts)
    vmem = pl.BlockSpec(memory_space=pltpu.VMEM)
    dma = pltpu.SemaphoreType.DMA
    return pl.pallas_call(
        functools.partial(collect_kernel, streams, segments, size, rows),
        out_shape=[jax.ShapeDtypeStruct((rows, wide), bf16)] * 3,
        in_specs=[pl.BlockSpec(memory_space=pl.ANY)] * count,
        out_specs=[vmem] * 3,
        scratch_shapes=[
            pltpu.VMEM((8, stream[2], part.shape[1]), bf16) for part, stream in zip(parts, streams)
        ]
        + [pltpu.VMEM((rows, wide), f32)] * 3
        + [dma((count,)), dma((count, 7)), dma((count, 7))],
        compiler_params=pltpu.CompilerParams(
            collective_id=ident, has_side_effects=True, vmem_limit_bytes=48 * 2**20
        ),
    )(*parts)


def close_kernel(sum_ref, w_ref, gain_ref, prob_ref, out_ref, sums_ref, bound_ref):
    width = w_ref.shape[1]
    out = sum_ref[:, :width].astype(f32)
    out_ref[...] = out
    gains = jnp.sum(out * w_ref[...].astype(f32), axis=1, keepdims=True)
    side = sum_ref[:, width:].astype(f32)
    lane = lax.broadcasted_iota(jnp.int32, side.shape, 1)
    turned = jnp.transpose(jnp.where(lane == 2, gains, side))
    sums_ref[...] = turned[2:3, :] / gain_ref[...]
    layer = lax.broadcasted_iota(jnp.int32, prob_ref.shape, 0)
    probs = prob_ref[...]
    grads = jnp.where((layer >= 1) & (layer <= LAYER_AT), turned[0:1, :] + turned[1:2, :], 0.0)
    bound_ref[...] = probs * (grads - jnp.sum(probs * grads, axis=0, keepdims=True))


def gather_plane(v, ident):
    hbm = pl.BlockSpec(memory_space=pl.ANY)
    out = pl.pallas_call(
        gather_kernel,
        out_shape=jax.ShapeDtypeStruct((8,) + v.shape, v.dtype),
        in_specs=[hbm],
        out_specs=hbm,
        scratch_shapes=[
            pltpu.SemaphoreType.DMA,
            pltpu.SemaphoreType.DMA((8,)),
            pltpu.SemaphoreType.DMA((8,)),
        ],
        compiler_params=pltpu.CompilerParams(
            collective_id=ident, has_side_effects=True, vmem_limit_bytes=48 * 2**20
        ),
    )(v)
    return out.reshape(-1, v.shape[1])


def scatter_plane(parts, ident):
    count, rows, wide = len(parts), parts[0].shape[0] // 8, parts[0].shape[1]
    return pl.pallas_call(
        functools.partial(scatter_kernel, count),
        out_shape=[jax.ShapeDtypeStruct((rows, wide), f32)] * count,
        in_specs=[pl.BlockSpec(memory_space=pl.ANY)] * count,
        out_specs=[pl.BlockSpec(memory_space=pltpu.VMEM)] * count,
        scratch_shapes=[
            pltpu.VMEM((count, 4, rows, wide), bf16),
            pltpu.VMEM((count, 4, rows, wide), bf16),
            pltpu.VMEM((count, 6, rows // 2, wide), bf16),
            pltpu.VMEM((count, 6, rows // 2, wide), bf16),
            pltpu.SemaphoreType.DMA((count, 4)),
            pltpu.SemaphoreType.DMA((count, 10)),
            pltpu.SemaphoreType.DMA((count, 10)),
        ],
        compiler_params=pltpu.CompilerParams(
            collective_id=ident, has_side_effects=True, vmem_limit_bytes=48 * 2**20
        ),
    )(*[part.reshape(8, rows, wide) for part in parts])


def dot(a, b):
    return jnp.dot(a, b, preferred_element_type=f32)


def dot_nt(a, b):
    return lax.dot_general(a, b, (((1,), (1,)), ((), ())), preferred_element_type=f32)


def dot_tn(a, b):
    return lax.dot_general(a, b, (((0,), (0,)), ((), ())), preferred_element_type=f32)


def body(
    tokens,
    cotangent,
    domain_tags,
    doc_ids,
    counts,
    w_in,
    w_forget,
    w_gate_out,
    w_out,
    ffn_gate,
    ffn_up,
    ffn_down,
    norm_gain,
    out_gain,
    ffn_gain,
    bound_logits,
):
    groups = lax.axis_size("g")
    members = lax.axis_size("p") * lax.axis_size("c")
    copies = lax.axis_size("x")
    ranks = members * copies
    rows, width = tokens.shape
    plane_rows = rows * ranks
    units = ffn_gate.shape[1]
    g, x = lax.axis_index("g"), lax.axis_index("x")
    rank = (lax.axis_index("p") * lax.axis_size("c") + lax.axis_index("c")) * copies + x
    ce = width // (groups * ranks)
    fe = units // (groups * ranks)
    chan, unit = ce * groups, fe * groups
    splits = (0, unit // QUARTERS, unit)
    near = -(-2 * splits[1] // 128) * 128

    def half_rows(w):
        half = w.shape[0] // copies
        return lax.dynamic_slice_in_dim(w, x * half, half, axis=0)

    def gather_rows(v):
        return lax.all_gather(v, "g", axis=0, tiled=True)

    def own_columns(v, size):
        v = v.reshape(groups, ranks, size)
        return lax.dynamic_index_in_dim(v, rank, axis=1, keepdims=False).reshape(1, groups * size)

    layer_count = bound_logits.shape[0]
    layer_probs = jax.nn.softmax(bound_logits, axis=0)
    layer_index = jnp.arange(layer_count, dtype=jnp.int32)
    layer_pick = ((layer_index >= 1) & (layer_index <= LAYER_AT)).astype(f32)[:, None]
    own_lower = jnp.sum(layer_probs * layer_pick, axis=0)[:, None]
    top, rest = split_hi_lo(own_lower)
    out_own = jnp.concatenate(
        [
            half_rows(w_out),
            top,
            rest,
            (own_lower - top.astype(f32) - rest.astype(f32)).astype(bf16),
            jnp.zeros((ce, 125), bf16),
        ],
        axis=1,
    )
    gain = own_columns(out_gain, ce)

    places = jnp.arange(doc_ids.shape[0], dtype=jnp.int32)
    previous = jnp.concatenate([doc_ids[:1], doc_ids[:-1]])
    keep = ((places % SEQ_LEN != 0) & (doc_ids == previous)).astype(f32)[:, None]
    keep = lax.dynamic_slice_in_dim(keep, g * plane_rows, plane_rows, axis=0)

    token_f = tokens.astype(f32)
    scale_one = lax.rsqrt(jnp.mean(token_f * token_f, axis=-1, keepdims=True) + EPS)
    normed_one = token_f * scale_one
    act_one_own = (normed_one * norm_gain).astype(bf16)

    domain_count = counts.shape[0]
    domain_hits = domain_tags[:, None] == jnp.arange(domain_count, dtype=jnp.int32)[None, :]
    per_token = jnp.sum(jnp.where(domain_hits, counts[None, :], 0), axis=1).astype(f32)
    seq_total = doc_ids.shape[0] // SEQ_LEN
    grad_z = cotangent.astype(f32) * (seq_total / (domain_count * per_token))[:, None]

    mix_w, out_ext, act_one, grad_m, *ffn = spread(
        groups,
        splits,
        near,
        (w_in, w_forget, w_gate_out),
        (ffn_gate, ffn_up),
        out_own,
        act_one_own,
        grad_z.astype(bf16),
        0,
    )
    mix_w = mix_w.reshape(width, 3 * chan)
    down_w = gather_rows(half_rows(ffn_down))
    act_one, grad_m = act_one.reshape(plane_rows, width), grad_m.reshape(plane_rows, width)
    out_ext = out_ext.reshape(chan, -1)
    out_w = out_ext[:, :width]

    (
        proj,
        states,
        pre_grad,
        grads_kept,
        ffn_near,
        residual,
        hidden,
        grads_rest,
        act_two,
        ffn_far,
        state_scale,
        lower,
    ) = mixer(
        groups,
        chan,
        act_one,
        mix_w,
        out_ext,
        keep,
        gain,
        tokens,
        ffn_gain.reshape(1, width),
        grad_m,
        down_w,
        splits[1],
        ffn[0].reshape(-1, near),
        ffn[1].reshape(-1, 2 * unit - near),
        1,
    )
    act_two = act_two.reshape(plane_rows, width)
    branch = residual - token_f
    scale_two = lax.rsqrt(jnp.mean(residual * residual, axis=-1, keepdims=True) + EPS)
    normed_two = residual * scale_two

    def scatter_rows(v):
        return lax.psum_scatter(v, "g", scatter_dimension=0, tiled=True)

    ffn_sums = [scatter_rows(grads_kept)]
    ffn_near, ffn_far = ffn_near.reshape(width, near), ffn_far.reshape(width, -1)
    far_grads, pre_grad, hidden_far = feed(
        groups, act_two, grad_m, ffn_near, ffn_far, down_w, pre_grad, grads_rest
    )
    ffn_sums.append(scatter_rows(far_grads.reshape(-1, 128)))
    back_part = dot_nt(pre_grad[:, :near], ffn_near) + dot_nt(pre_grad[:, near:], ffn_far)
    back_part = back_part.astype(bf16)
    down_part = dot(hidden, down_w[: splits[1]]) + dot(hidden_far, down_w[splits[1] :])
    down_part = down_part.astype(bf16)

    (back_term,) = scatter_plane([back_part], 3)
    scaled_two = back_term * ffn_gain
    grad_resid = grad_z + scale_two * (
        scaled_two - normed_two * jnp.mean(scaled_two * normed_two, axis=-1, keepdims=True)
    )
    grad_branch_own = grad_resid.astype(bf16)
    mean_out = jnp.sum(grad_branch_own.astype(f32) * branch, axis=-1, keepdims=True) / width
    sent = jnp.concatenate(
        [
            grad_branch_own,
            *split_hi_lo(state_scale),
            *split_hi_lo(mean_out),
            jnp.zeros((rows, 124), bf16),
        ],
        axis=1,
    )
    got = gather_plane(sent, 4)
    grad_branch = got[:, :width]
    info = got[:, width:].astype(f32)
    info = jnp.concatenate([info[:, 0:1] + info[:, 1:2], info[:, 2:3] + info[:, 3:4]], axis=1)
    grad_mixed = dot_nt(grad_branch, out_w)
    grad_proj, mixed_out, sums = kernel_call(
        functools.partial(backward_scan, chan),
        [
            jax.ShapeDtypeStruct((plane_rows, 3 * chan), bf16),
            jax.ShapeDtypeStruct((plane_rows, chan), bf16),
            jax.ShapeDtypeStruct((1, chan), f32),
        ],
        proj,
        states,
        grad_mixed,
        info,
        keep,
        lower,
        gain,
    )
    in_part = dot_nt(grad_proj, mix_w).astype(bf16)
    down_part, grad_proj = lax.optimization_barrier((down_part, grad_proj))
    (down_term,) = scatter_plane([down_part], 5)
    mix_grads = dot_tn(act_one, grad_proj).astype(bf16)
    top, rest = split_hi_lo(sums.reshape(chan, 1))
    out_grads = jnp.concatenate(
        [dot_tn(mixed_out, grad_branch).astype(bf16), top, rest, jnp.zeros((chan, 126), bf16)], axis=1
    )
    mix_grads, ffn_sums, in_part, out_grads, down_term = lax.optimization_barrier(
        (mix_grads, ffn_sums, in_part, out_grads, down_term)
    )
    mix_sum = scatter_rows(mix_grads)
    out_grads, mix_sum = lax.optimization_barrier((out_grads, mix_sum))
    out_sum = scatter_rows(out_grads)
    first_channel = (g * ranks + rank) * ce
    summed_wout, summed_outg, grad_bounds = kernel_call(
        close_kernel,
        [
            jax.ShapeDtypeStruct((ce, width), f32),
            jax.ShapeDtypeStruct((1, ce), f32),
            jax.ShapeDtypeStruct(bound_logits.shape, f32),
        ],
        out_sum,
        half_rows(w_out),
        lax.dynamic_slice_in_dim(out_gain, first_channel, ce, axis=0).reshape(1, ce),
        layer_probs,
    )
    summed_outg = summed_outg.reshape(ce)
    (grad_act,) = scatter_plane([in_part], 6)
    output_rows = (residual + down_term).astype(bf16)

    scaled_one = grad_act * norm_gain
    grad_tokens = grad_resid + scale_one * (
        scaled_one - normed_one * jnp.mean(scaled_one * normed_one, axis=-1, keepdims=True)
    )

    first, lead, kept = splits[1], near - 2 * splits[1], grads_kept.shape[1]
    some, far = unit - first, 2 * unit - near
    segments = (
        (0, 0, 0, 0, first),
        (0, first, 1, 0, first),
        (0, 2 * first, 2, 0, kept - 2 * first),
        (1, 0, 0, first + lead, some - lead),
        (1, some - lead, 1, first, some),
        (1, far, 0, first, lead),
        (1, far + lead, 2, first, some),
        (1, far + lead + some, 2, kept - 2 * first, 3 * first - kept),
    )
    summed_fgate, summed_fup, fdown = [
        v.astype(f32)
        for v in collect(
            [ffn_sums[0], ffn_sums[1], ffn_sums[1]],
            [(0, 8, ce), (0, 8, TILES * ce), (8 * TILES * ce, 4, ce)],
            ce,
            segments,
            fe,
            units,
            7,
        )
    ]
    summed_fdown = fdown.T
    summed_win, summed_wforget, summed_wgate = [
        v.astype(f32)
        for v in collect(
            [mix_sum], [(0, 8, ce)], ce, [(0, n * chan, n, 0, chan) for n in range(3)], ce, width, 8
        )
    ]
    first = (g * ranks + rank) * ce

    def own_gain(gain, pairs):
        total = sum(jnp.sum(grad * half_rows(w).astype(f32), axis=1) for grad, w in pairs)
        return total / lax.dynamic_slice_in_dim(gain, first, ce, axis=0)

    summed_norm = own_gain(
        norm_gain, ((summed_win, w_in), (summed_wforget, w_forget), (summed_wgate, w_gate_out))
    )
    summed_ffng = own_gain(ffn_gain, ((summed_fgate, ffn_gate), (summed_fup, ffn_up)))
    return (
        output_rows,
        grad_tokens,
        summed_win,
        summed_wforget,
        summed_wgate,
        summed_wout,
        summed_fgate,
        summed_fup,
        summed_fdown,
        summed_norm,
        summed_outg,
        summed_ffng,
        grad_bounds,
    )


def solution(mesh):
    seqs, copies = mesh.shape["seq"], mesh.shape["rep"]
    mesh = Mesh(mesh.devices.reshape(seqs // 4, 2, 2, copies), ALL)
    by_rows = P(ALL, None)
    by_seq = P(("g", "p", "c"), None)
    placed = (
        (by_rows, by_rows, P(ALL), P(), P()) + (by_seq,) * 7 + (P(), P(), P(), P(None, ALL))
    )
    return jax.shard_map(
        body,
        mesh=mesh,
        in_specs=placed,
        out_specs=(by_rows,) * 8 + (P(None, ALL),) + (P(ALL),) * 3 + (P(None, ALL),),
        check_vma=False,
    )
```

```python
import functools

import jax
import jax.numpy as jnp
from jax import lax
from jax.experimental import pallas as pl
from jax.experimental.pallas import tpu as pltpu
from jax.sharding import Mesh
from jax.sharding import PartitionSpec as P

LAYER_AT = 12
SEQ_LEN = 1024
EPS = 1e-06
ROWS = 16
QUARTERS = 4
TILES = 12
PLANE = ("p", "c", "x")
ALL = ("g", "p", "c", "x")
f32 = jnp.float32
bf16 = jnp.bfloat16


def split_hi_lo(v):
    hi = v.astype(bf16)
    return hi, (v - hi.astype(f32)).astype(bf16)


def gates(proj, chan, lower):
    ip = proj[:, :chan].astype(bf16).astype(f32)
    sf = jax.nn.sigmoid(proj[:, chan : 2 * chan].astype(bf16).astype(f32))
    forget = lower + (1.0 - lower) * sf
    sig_in = jax.nn.sigmoid(ip)
    return ip, sig_in, sf, forget


def forward_scan(chan, proj_ref, keep_ref, lower_ref, gain_ref, h_ref, o_ref, ss_ref):
    lower = lower_ref[...]
    gain = gain_ref[...]
    row = lax.broadcasted_iota(jnp.int32, (ROWS, chan), 0)

    def step(i, carry):
        rows = pl.ds(pl.multiple_of(i * ROWS, ROWS), ROWS)
        proj = proj_ref[rows, :]
        ip, sig_in, _, forget = gates(proj, chan, lower)
        u = ip * sig_in * (1.0 - forget)
        e = forget * keep_ref[rows, :]
        shift = 1
        while shift < ROWS:
            u = u + e * jnp.where(row >= shift, pltpu.roll(u, shift, 0), 0.0)
            e = e * jnp.where(row >= shift, pltpu.roll(e, shift, 0), 1.0)
            shift *= 2
        h = u + e * carry
        h_ref[rows, :] = h
        hb = h.astype(bf16).astype(f32)
        gate = proj[:, 2 * chan :]
        o_ref[rows, :] = (hb * gain * (gate * jax.nn.sigmoid(gate))).astype(bf16)
        ss_ref[rows, :] = jnp.sum(hb * hb, axis=1, keepdims=True)
        return h[ROWS - 1 : ROWS, :]

    lax.fori_loop(0, proj_ref.shape[0] // ROWS, step, jnp.zeros((1, chan), f32))


def mixer_kernel(
    groups,
    chan,
    act_hbm,
    mix_hbm,
    grad_hbm,
    down_hbm,
    near_ref,
    far_ref,
    out_w_hbm,
    keep_ref,
    gain_ref,
    token_hbm,
    ffn_gain_ref,
    proj_hbm,
    h_hbm,
    pre_grad_hbm,
    kept_hbm,
    near_hbm,
    residual_hbm,
    hidden_hbm,
    rest_hbm,
    act_two_ref,
    far_all,
    scale_ref,
    lower_ref,
    token_ref,
    out_w_ref,
    act_ref,
    mix_ref,
    grad_ref,
    down_ref,
    proj_ref,
    h_ref,
    pre_grad_ref,
    kept_ref,
    near_all,
    residual_ref,
    hidden_ref,
    rest_ref,
    raw,
    squares,
    part,
    theirs,
    outgoing,
    landing,
    own_two,
    two,
    pre_ref,
    grad_tmp,
    swap_send,
    swap_recv,
    send_sem,
    recv_sem,
    local_sem,
    move_sem,
    act_send,
    act_recv,
    line_send,
    line_recv,
):
    moves = []

    def move(src, dst):
        copy = pltpu.make_async_copy(src, dst, move_sem.at[len(moves)])
        copy.start()
        moves.append(copy)
        return copy

    loads = [
        move(*pair)
        for pair in ((act_hbm, act_ref), (mix_hbm, mix_ref), (grad_hbm, grad_ref), (out_w_hbm, out_w_ref), (token_hbm, token_ref))
    ]
    chips, core = places()
    sibling = device_at(chips[3], 1 - core)
    greet([device_at(chip, core) for chip in chips[:3]] + [sibling] + line_partners(groups))
    near = Line(groups, near_ref, near_all, line_send.at[0], line_recv.at[0], local_sem.at[1])
    far = Line(groups, far_ref, far_all, line_send.at[1], line_recv.at[1], local_sem.at[2])
    near.send(1)
    far.send(1)
    loads.append(move(down_hbm.at[pl.ds(0, down_ref.shape[0])], down_ref))
    rows, width = token_hbm.shape
    block = 2 * rows
    loads[3].wait()
    loads[4].wait()
    turned = jnp.transpose(out_w_ref[:, width:].astype(f32))
    lower_ref[...] = turned[0:1, :] + turned[1:2, :] + turned[2:3, :]
    loads[0].wait()
    loads[1].wait()

    def project(i, _):
        at = pl.ds(pl.multiple_of(i * block, block), block)
        proj_ref[at, :] = dot(act_ref[at, :], mix_ref[...])
        return 0

    lax.fori_loop(0, act_ref.shape[0] // block, project, 0)
    forward_scan(chan, proj_ref, keep_ref, lower_ref, gain_ref, h_ref, raw, squares)
    near.step(1)
    move(proj_ref, proj_hbm)
    move(h_ref, h_hbm)

    lane = lax.broadcasted_iota(jnp.int32, (rows, part.shape[1] - width), 1)

    def mixed(rank):
        at = pl.ds(pl.multiple_of(rank * rows, rows), rows)
        part[at, :width] = dot(raw[at, :], out_w_ref[:, :width]).astype(bf16)
        top, rest = split_hi_lo(squares[at, :])
        side = jnp.where(lane == 0, top.astype(f32), jnp.where(lane == 1, rest.astype(f32), 0.0))
        part[at, width:] = side.astype(bf16)
        return part.at[at]

    swaps = []
    for j, chip in enumerate(chips):
        swaps.append(
            remote(
                mixed(rank_at(chip, 1 - core)), theirs.at[j], swap_send.at[j], swap_recv.at[j], sibling
            )
        )
    scatter = Scatter([], theirs, outgoing, landing, send_sem, recv_sem)
    for j, chip in enumerate(chips):
        scatter.mine.append(mixed(rank_at(chip, core)))
        swaps[j].wait_recv()
        if j < 3:
            scatter.first(j)
    far.step(1)
    scatter.second()

    def finish(at, total):
        scale = lax.rsqrt((total[:, width : width + 1] + total[:, width + 1 : width + 2]) / width + EPS)
        scale_ref[at, :] = scale
        residual = token_ref[at, :].astype(f32) + total[:, :width] * scale
        residual_ref[at, :] = residual
        norm = lax.rsqrt(jnp.mean(residual * residual, axis=-1, keepdims=True) + EPS)
        own_two[at, :] = (residual * norm * ffn_gain_ref[...]).astype(bf16)

    scatter.totals(finish)
    move(residual_ref, residual_hbm)
    plane = Plane(own_two, two, local_sem.at[0], act_send, act_recv)
    plane.start(1)
    plane.start(2)
    plane.start_own()
    for copy in swaps:
        copy.wait_send()
    scatter.finish()
    near.step(2)
    plane.hand_on(1)
    plane.hand_on(2)
    far.step(2)
    plane.hand_on(0)
    for k in range(3, groups):
        near.step(k)
    plane.finish()
    near.finish()
    move(two, act_two_ref)
    move(near_all, near_hbm)
    loads[2].wait()
    loads[5].wait()

    some = hidden_ref.shape[1]
    depth = near_all.shape[1]

    def quarter(i, _):
        at = pl.ds(pl.multiple_of(i * block, block), block)
        act = two[pl.ds(2 * i, 2)].reshape(block, width)
        pre = jnp.zeros((block, near_all.shape[2]), f32)
        for g in range(groups):
            pre += dot(act[:, g * depth : (g + 1) * depth], near_all[g])
        pre_ref[...] = pre
        gate, up = pre_ref[:, :some], pre_ref[:, some : 2 * some]
        back = dot_nt(grad_ref[at, :], down_ref[...])
        sig = jax.nn.sigmoid(gate)
        gate_silu = gate * sig
        hidden_ref[at, :] = (gate_silu * up).astype(bf16)
        pre_ref[:, :some] = back * up * (sig * (1.0 + gate * (1.0 - sig)))
        pre_ref[:, some : 2 * some] = back * gate_silu
        pre_grad_ref[at, :] = pre_ref[:, : 2 * some].astype(bf16)
        return 0

    lax.fori_loop(0, act_ref.shape[0] // block, quarter, 0)

    def weights(i, _):
        at = pl.ds(pl.multiple_of(i * block, block), block)
        act = two[:, :, at].reshape(act_ref.shape[0], block)
        grad_tmp[:, : 2 * some] = dot_tn(act, pre_grad_ref[...])
        grad_tmp[:, 2 * some : 3 * some] = dot_tn(grad_ref[:, at], hidden_ref[...])
        kept = kept_ref.shape[1]
        kept_ref[at, :] = grad_tmp[:, :kept].astype(bf16)
        rest_ref[at, :] = grad_tmp[:, kept : 3 * some].astype(bf16)
        return 0

    lax.fori_loop(0, width // block, weights, 0)
    move(pre_grad_ref, pre_grad_hbm)
    move(kept_ref, kept_hbm)
    move(hidden_ref, hidden_hbm)
    move(rest_ref, rest_hbm)
    for k in range(3, groups):
        far.step(k)
    far.finish()
    for copy in moves[6:]:
        copy.wait()


def mixer(
    groups, chan, act, mix_w, out_ext, keep, gain, tokens, ffn_gain, grad, down, some, near, far, ident
):
    total, (rows, width) = act.shape[0], tokens.shape
    vmem, hbm = pl.BlockSpec(memory_space=pltpu.VMEM), pl.BlockSpec(memory_space=pl.ANY)
    dma = pltpu.SemaphoreType.DMA
    wide = width + 128
    kept = 3 * some // 128 * 128
    moved = [
        jax.ShapeDtypeStruct((total, 3 * chan), f32),
        jax.ShapeDtypeStruct((total, chan), f32),
        jax.ShapeDtypeStruct((total, 2 * some), bf16),
        jax.ShapeDtypeStruct((width, kept), bf16),
        jax.ShapeDtypeStruct((groups,) + near.shape, bf16),
        jax.ShapeDtypeStruct((rows, width), f32),
        jax.ShapeDtypeStruct((total, some), bf16),
        jax.ShapeDtypeStruct((width, 3 * some - kept), bf16),
    ]
    return pl.pallas_call(
        functools.partial(mixer_kernel, groups, chan),
        out_shape=moved
        + [
            jax.ShapeDtypeStruct((8, rows, width), bf16),
            jax.ShapeDtypeStruct((groups,) + far.shape, bf16),
            jax.ShapeDtypeStruct((rows, 1), f32),
            jax.ShapeDtypeStruct((1, chan), f32),
        ],
        in_specs=[hbm] * 7 + [vmem] * 2 + [hbm, vmem],
        out_specs=[hbm] * 10 + [vmem] * 2,
        scratch_shapes=[pltpu.VMEM(v.shape, v.dtype) for v in (tokens, out_ext, act, mix_w, grad)]
        + [pltpu.VMEM((some, width), bf16)]
        + [pltpu.VMEM(v.shape, v.dtype) for v in moved]
        + [
            pltpu.VMEM((total, chan), bf16),
            pltpu.VMEM((total, 1), f32),
            pltpu.VMEM((total, wide), bf16),
            pltpu.VMEM((4, rows, wide), bf16),
            pltpu.VMEM((6, rows // 2, wide), bf16),
            pltpu.VMEM((6, rows // 2, wide), bf16),
            pltpu.VMEM((rows, width), bf16),
            pltpu.VMEM((8, rows, width), bf16),
            pltpu.VMEM((2 * rows, near.shape[1]), f32),
            pltpu.VMEM((2 * rows, 3 * some), f32),
            dma((4,)),
            dma((4,)),
            dma((6,)),
            dma((6,)),
            dma((3,)),
            dma((15,)),
            dma((8,)),
            dma((8,)),
            dma((2, 2, groups - 1)),
            dma((2, 2, groups - 1)),
        ],
        compiler_params=pltpu.CompilerParams(
            collective_id=ident, has_side_effects=True, vmem_limit_bytes=60 * 2**20
        ),
    )(act, mix_w, grad, down, near, far, out_ext, keep, gain, tokens, ffn_gain)


def feed_kernel(
    first,
    act_hbm,
    grad_hbm,
    near_hbm,
    far_hbm,
    down_hbm,
    pre_first_ref,
    rest_ref,
    weights_hbm,
    pre_grad_hbm,
    hidden_hbm,
    act_ref,
    grad_ref,
    near_ref,
    far_ref,
    down_ref,
    weights_ref,
    pre_grad_ref,
    hidden_ref,
    wide_ref,
    side_ref,
    lead_ref,
    fold_ref,
    move_sem,
    store_sem,
):
    moves = []

    def move(src, dst):
        copy = pltpu.make_async_copy(src, dst, move_sem.at[len(moves)])
        copy.start()
        moves.append(copy)

    for pair in (
        (act_hbm, act_ref),
        (near_hbm, near_ref),
        (far_hbm, far_ref),
        (grad_hbm, grad_ref),
        (down_hbm, down_ref),
    ):
        move(*pair)
    loads = len(moves)
    for copy in moves[:3]:
        copy.wait()
    near, width = near_ref.shape[1], act_ref.shape[1]
    unit = down_ref.shape[0]
    some, lead = unit - first, near - 2 * first
    block = 256

    def tokens(i, _):
        at = pl.ds(pl.multiple_of(i * block, block), block)
        wide_ref[:, :near] = dot(act_ref[at, :], near_ref[...])
        wide_ref[:, near:] = dot(act_ref[at, :], far_ref[...])

        @pl.when(i == 0)
        def _():
            moves[3].wait()
            moves[4].wait()

        gate = wide_ref[:, 2 * first : 2 * first + some]
        up = wide_ref[:, 2 * first + some :]
        back = dot_nt(grad_ref[at, :], down_ref[first:, :])
        sig = jax.nn.sigmoid(gate)
        gate_silu = gate * sig
        hidden_ref[at, :] = (gate_silu * up).astype(bf16)
        wide_ref[:, : 2 * first] = pre_first_ref[at, :].astype(f32)
        wide_ref[:, 2 * first : 2 * first + some] = back * up * (sig * (1.0 + gate * (1.0 - sig)))
        wide_ref[:, 2 * first + some :] = back * gate_silu
        pre_grad_ref[at, :] = wide_ref[...].astype(bf16)
        return 0

    lax.fori_loop(0, act_ref.shape[0] // block, tokens, 0)
    move(pre_grad_ref, pre_grad_hbm)
    move(hidden_ref, hidden_hbm)

    groups = weights_ref.shape[0]
    part = width // groups
    rows = part // 8
    tail = 64

    def weights(g, _):
        at = pl.ds(pl.multiple_of(g * part, part), part)
        act, grad = act_ref[:, at], grad_ref[:, at]
        full = dot_tn(act, pre_grad_ref[:, near:]).astype(bf16)
        lead_ref[...] = dot_tn(act, pre_grad_ref[:, near - 128 : near])
        side_ref[:, :lead] = lead_ref[:, 128 - lead :]
        side_ref[:, lead : lead + some] = dot_tn(grad, hidden_ref[...])
        side_ref[:, lead + some :] = rest_ref[at, :].astype(f32)
        side = side_ref[...].astype(bf16)
        for k in range(8):
            for t in range(TILES):
                source, skipped = (full, 0) if t * 128 < 2 * unit - near else (side, 2 * unit - near)
                column = t * 128 - skipped
                place = (k * TILES + t) * rows
                weights_ref[g, place : place + rows, :] = source[
                    k * rows : (k + 1) * rows, column : column + 128
                ]
        last = side_ref.shape[1] - tail
        fold_ref[:, :tail] = side_ref[: part // 2, last:]
        fold_ref[:, tail:] = side_ref[part // 2 :, last:]
        weights_ref[g, 8 * TILES * rows :, :] = fold_ref[...].astype(bf16)
        store(g).start()
        return 0

    def store(g):
        return pltpu.make_async_copy(weights_ref.at[g], weights_hbm.at[g], store_sem.at[g])

    lax.fori_loop(0, groups, weights, 0)
    for g in range(groups):
        store(g).wait()
    for copy in moves[loads:]:
        copy.wait()


def feed(groups, act, grad, near, far, down, pre_first, rest):
    (total, width), unit, first = act.shape, down.shape[0], pre_first.shape[1] // 2
    side = near.shape[1] - 2 * first + unit - first + rest.shape[1]
    vmem, hbm = pl.BlockSpec(memory_space=pltpu.VMEM), pl.BlockSpec(memory_space=pl.ANY)
    outs = [
        jax.ShapeDtypeStruct((groups, (8 * TILES + 4) * (width // (8 * groups)), 128), bf16),
        jax.ShapeDtypeStruct((total, 2 * unit), bf16),
        jax.ShapeDtypeStruct((total, unit - first), bf16),
    ]
    return pl.pallas_call(
        functools.partial(feed_kernel, first),
        out_shape=outs,
        in_specs=[hbm] * 5 + [vmem] * 2,
        out_specs=[hbm] * 3,
        scratch_shapes=[pltpu.VMEM(v.shape, bf16) for v in (act, grad, near, far, down, *outs)]
        + [
            pltpu.VMEM((256, 2 * unit), f32),
            pltpu.VMEM((width // groups, side), f32),
            pltpu.VMEM((width // groups, 128), f32),
            pltpu.VMEM((width // (2 * groups), 128), f32),
            pltpu.SemaphoreType.DMA((7,)),
            pltpu.SemaphoreType.DMA((groups,)),
        ],
        compiler_params=pltpu.CompilerParams(vmem_limit_bytes=60 * 2**20),
    )(act, grad, near, far, down, pre_first, rest)


def backward_scan(
    chan, proj_ref, h_ref, do_ref, info_ref, keep_ref, lower_ref, gain_ref, grad_ref, o_ref, sums_ref
):
    lower = lower_ref[...]
    gain = gain_ref[...]
    row = lax.broadcasted_iota(jnp.int32, (ROWS, chan), 0)
    blocks = proj_ref.shape[0] // ROWS

    def step(j, carried):
        later, sum_lower = carried
        i = blocks - 1 - j
        rows = pl.ds(pl.multiple_of(i * ROWS, ROWS), ROWS)
        proj = proj_ref[rows, :]
        ip, sig_in, sf, forget = gates(proj, chan, lower)
        keep = keep_ref[rows, :]
        act_in = ip * sig_in
        h = h_ref[rows, :]
        before = h_ref[pl.ds(pl.multiple_of(jnp.maximum(i * ROWS - 8, 0), 8), 8), :][7:8, :]
        h_prev = jnp.where(row >= 1, pltpu.roll(h, 1, 0), before)
        scale = info_ref[rows, 0:1]
        mean = info_ref[rows, 1:2]
        hn = h.astype(bf16).astype(f32) * scale
        gate = proj[:, 2 * chan :]
        sig_gate = jax.nn.sigmoid(gate)
        gate_act = gate * sig_gate
        do = do_ref[rows, :]
        o_ref[rows, :] = (hn * gain * gate_act).astype(bf16)
        dgp = do * hn * gain * (sig_gate * (1.0 + gate * (1.0 - sig_gate)))
        dhb = scale * (do * gain * gate_act - hn * mean)
        d = dhb.astype(bf16).astype(f32)
        e = forget * keep
        c = jnp.where(row < ROWS - 1, pltpu.roll(e, ROWS - 1, 0), 1.0)
        shift = 1
        while shift < ROWS:
            inside = row < ROWS - shift
            d = d + c * jnp.where(inside, pltpu.roll(d, ROWS - shift, 0), 0.0)
            c = c * jnp.where(inside, pltpu.roll(c, ROWS - shift, 0), 1.0)
            shift *= 2
        dh = d + c * later
        dip = dh * (1.0 - forget) * (sig_in * (1.0 + ip * (1.0 - sig_in)))
        df = dh * (h_prev * keep - act_in)
        tail = df * (1.0 - sf)
        dfp = tail * (1.0 - lower) * sf
        grad_ref[rows, :] = jnp.concatenate([dip, dfp, dgp], axis=1).astype(bf16)
        sum_lower = sum_lower + jnp.sum(tail, axis=0, keepdims=True)
        return (e * dh)[0:1, :], sum_lower

    zero = jnp.zeros((1, chan), f32)
    _, sum_lower = lax.fori_loop(0, blocks, step, (zero, zero))
    sums_ref[...] = sum_lower


def kernel_call(kernel, outs, *args):
    vmem = pl.BlockSpec(memory_space=pltpu.VMEM)
    return pl.pallas_call(
        kernel,
        out_shape=outs,
        in_specs=[vmem] * len(args),
        out_specs=[vmem] * len(outs),
        compiler_params=pltpu.CompilerParams(vmem_limit_bytes=48 * 2**20),
    )(*args)


MESH = pl.DeviceIdType.MESH


def places():
    g, p, c, x = (lax.axis_index(a) for a in ALL)
    flips = ((1, 1), (0, 1), (1, 0), (0, 0))
    chips = [(g, p + dp * (1 - 2 * p), x + dx * (1 - 2 * x)) for dp, dx in flips]
    return chips, c


def device_at(chip, core):
    return (chip[0], chip[1], core, chip[2])


def rank_at(chip, core):
    return (chip[1] * 2 + core) * 2 + chip[2]


def greet(partners):
    barrier = pltpu.get_barrier_semaphore()
    for partner in partners:
        pl.semaphore_signal(barrier, inc=1, device_id=partner, device_id_type=MESH)
    pl.semaphore_wait(barrier, len(partners))


def remote(src, dst, send_sem, recv_sem, device):
    copy = pltpu.make_async_remote_copy(
        src_ref=src, dst_ref=dst, send_sem=send_sem, recv_sem=recv_sem, device_id=device, device_id_type=MESH
    )
    copy.start()
    return copy


class Line:
    def __init__(self, groups, own_ref, out_ref, send_sem, recv_sem, local_sem=None, part=None):
        self.groups, self.own, self.out, self.part = groups, own_ref, out_ref, part
        self.send_sem, self.recv_sem = send_sem, recv_sem
        self.g, self.p, self.c, self.x = (lax.axis_index(a) for a in ALL)
        self.kept = None
        if local_sem is not None:
            self.kept = pltpu.make_async_copy(own_ref, out_ref.at[self.g], local_sem)
            self.kept.start()

    def view(self, block):
        return self.out.at[block] if self.part is None else self.out.at[block, self.part]

    def at_step(self, way, k):
        block = self.g - (k - 1) if way == 0 else self.g + (k - 1)
        return pltpu.make_async_remote_copy(
            src_ref=self.own if k == 1 else self.view(block),
            dst_ref=self.view(block),
            send_sem=self.send_sem.at[way, k - 1],
            recv_sem=self.recv_sem.at[way, k - 1],
            device_id=(self.g + (1 if way == 0 else -1), self.p, self.c, self.x),
            device_id_type=MESH,
        )

    def behind(self, way, k):
        return self.g >= k if way == 0 else self.g + k < self.groups

    def sends(self, way, k):
        return self.behind(way, k - 1) & self.behind(1 - way, 1)

    def send(self, k):
        for way in (0, 1):

            @pl.when(self.sends(way, k))
            def _(way=way):
                self.at_step(way, k).start()

    def arrived(self, way, k):
        got = self.view(self.g - k if way == 0 else self.g + k)
        pltpu.make_async_remote_copy(
            src_ref=got,
            dst_ref=got,
            send_sem=self.send_sem.at[way, k - 1],
            recv_sem=self.recv_sem.at[way, k - 1],
            device_id=(self.g, self.p, self.c, self.x),
            device_id_type=MESH,
        ).wait_recv()

    def step(self, k):
        for way in (0, 1):

            @pl.when(self.behind(way, k))
            def _(way=way):
                self.arrived(way, k)

        if k + 1 < self.groups:
            self.send(k + 1)

    def finish(self):
        if self.kept is not None:
            self.kept.wait()
        for k in range(1, self.groups):
            for way in (0, 1):

                @pl.when(self.sends(way, k))
                def _(way=way, k=k):
                    self.at_step(way, k).wait_send()


def line_partners(groups):
    g, p, c, x = (lax.axis_index(a) for a in ALL)
    offsets = sorted({1 % groups, -1 % groups} - {0})
    return [(lax.rem(g + k, groups), p, c, x) for k in offsets]


class Plane:
    def __init__(self, own_ref, out_ref, local_sem, send_sem, recv_sem):
        self.own, self.out = own_ref, out_ref
        self.send_sem, self.recv_sem = send_sem, recv_sem
        self.chips, self.core = places()
        self.half = own_ref.shape[0] // 2
        self.slot = out_ref.at[rank_at(self.chips[3], self.core)]
        self.sibling = device_at(self.chips[3], 1 - self.core)
        self.local = pltpu.make_async_copy(own_ref, self.slot, local_sem)
        self.sent, self.passed = {}, []

    def send(self, n, src, dst, device):
        return remote(src, dst, self.send_sem.at[n], self.recv_sem.at[n], device)

    def start_own(self):
        self.local.start()
        self.passed.append(self.send(3, self.own, self.slot, self.sibling))

    def start(self, i):
        self.sent[i] = self.send(i, self.own, self.slot, device_at(self.chips[i], self.core))

    def hand_on(self, i):
        got = self.out.at[rank_at(self.chips[i], self.core)]
        if i:
            self.sent[i].wait_recv()
            n, first = (0, 0) if i == 1 else (7, self.half)
            part = got.at[pl.ds(first, self.half)]
            self.sent[n] = self.send(n, part, part, device_at(self.chips[3 - i], self.core))
        else:
            self.sent[0].wait_recv()
            self.sent[7].wait_recv()
        self.passed.append(self.send(4 + i, got, got, self.sibling))

    def finish(self):
        for copy in self.sent.values():
            copy.wait_send()
        for copy in self.passed:
            copy.wait()
        self.local.wait()


class Scatter:
    def __init__(self, mine, theirs, outgoing, landing, send_sem, recv_sem):
        self.mine, self.theirs, self.outgoing, self.landing = mine, theirs, outgoing, landing
        self.send_sem, self.recv_sem = send_sem, recv_sem
        self.chips, self.core = places()
        self.half = outgoing.shape[1]
        self.sent = []

    def both(self, j, at):
        return self.mine[j][at, :].astype(f32) + self.theirs[j, at, :].astype(f32)

    def send(self, n, j, bottom, to, arrived=None):
        def add(i, _):
            near = pl.ds(pl.multiple_of(i * ROWS, ROWS), ROWS)
            at = pl.ds(pl.multiple_of(i * ROWS + bottom * self.half, ROWS), ROWS)
            total = self.both(j, at)
            if arrived is not None:
                total = total + self.landing[arrived, near, :].astype(f32)
            self.outgoing[n, near, :] = total.astype(bf16)
            return 0

        lax.fori_loop(0, self.half // ROWS, add, 0)
        self.sent.append(
            remote(
                self.outgoing.at[n],
                self.landing.at[n],
                self.send_sem.at[n],
                self.recv_sem.at[n],
                device_at(self.chips[to], self.core),
            )
        )

    def first(self, j):
        if j in (0, 1):
            self.send(j, j, 0, 1)
        if j in (0, 2):
            self.send(2 if j == 0 else 3, j, 1, 2)

    def second(self):
        arrived = [self.sent[n].wait_recv for n in (0, 2, 1, 3)]
        arrived[0]()
        self.send(4, 2, 0, 2, 0)
        arrived[2]()
        self.send(5, 1, 1, 1, 2)
        arrived[1]()
        arrived[3]()
        self.sent[4].wait_recv()
        self.sent[5].wait_recv()

    def totals(self, use):
        for bottom in (0, 1):

            def one(i, _, bottom=bottom):
                near = pl.ds(pl.multiple_of(i * ROWS, ROWS), ROWS)
                at = pl.ds(pl.multiple_of(i * ROWS + bottom * self.half, ROWS), ROWS)
                total = self.both(3, at)
                for n in (1 + 2 * bottom, 4 + bottom):
                    total = total + self.landing[n, near, :].astype(f32)
                use(at, total)
                return 0

            lax.fori_loop(0, self.half // ROWS, one, 0)

    def finish(self):
        for copy in self.sent:
            copy.wait_send()


def gather_kernel(own_ref, out_ref, local_sem, send_sem, recv_sem):
    plane = Plane(own_ref, out_ref, local_sem, send_sem, recv_sem)
    greet([device_at(chip, plane.core) for chip in plane.chips[:3]] + [plane.sibling])
    plane.start(1)
    plane.start(2)
    plane.start_own()
    for i in (1, 2, 0):
        plane.hand_on(i)
    plane.finish()


def spread_kernel(
    groups,
    splits,
    *refs,
):
    mixers, units = refs[:3], refs[3:5]
    out_ref, act_ref, grad_ref, mix_all, out_all, act_all, grad_all, near_all, far_all = refs[5:14]
    mix_ref, near_ref, far_ref, wide_ref = refs[14:18]
    local_sem, swap_send, swap_recv = refs[18:21]
    mix_send, mix_recv, out_send, out_recv, act_send, act_recv, grad_send, grad_recv = refs[21:]
    chips, core = places()
    here, other = chips[3], chips[2]
    g = here[0]
    swaps = [device_at(here, 1 - core), device_at(other, core), device_at(other, 1 - core)]
    greet([device_at(chip, core) for chip in chips[:3]] + [swaps[0], swaps[2]] + line_partners(groups))
    own = here[1] * 2 + core
    targets = [here[1] * 2 + 1 - core, other[1] * 2 + core, other[1] * 2 + 1 - core]

    def swap(src, dst, first):
        return [
            remote(
                src.at[targets[i]], dst, swap_send.at[first + i], swap_recv.at[first + i], swaps[i]
            )
            for i in range(3)
        ]

    out_line = Line(groups, out_ref, out_all, out_send, out_recv)
    out_line.send(1)
    act = Plane(act_ref, act_all, local_sem.at[3], act_send, act_recv)
    grad = Plane(grad_ref, grad_all, local_sem.at[4], grad_send, grad_recv)
    act.start_own()
    grad.start_own()
    act.start(1)

    def gather_columns(pieces, m, x):
        place = 0
        for ref, size, first, last in pieces:
            for group in range(first // size, last // size):
                start = ((group * 4 + m) * 2 + x) * size
                wide_ref[:, place : place + size] = ref[:, start : start + size].astype(f32)
                place += size
        return place

    def fill(make):
        for x in (0, 1):

            @pl.when(here[2] == x)
            def _(x=x):
                for m in range(4):
                    make(m, x)

    def mix_columns(m, x):
        size = mixers[0].shape[1] // (8 * groups)
        place = gather_columns([(ref, size, 0, size * groups) for ref in mixers], m, x)
        mix_ref[m] = wide_ref[:, :place].astype(bf16)

    def unit_columns(m, x):
        size = units[0].shape[1] // (8 * groups)
        place = gather_columns(
            [(ref, size, first, last) for first, last in zip(splits[:-1], splits[1:]) for ref in units], m, x
        )
        near = near_ref.shape[2]
        near_ref[m] = wide_ref[:, :near].astype(bf16)
        far_ref[m] = wide_ref[:, near:place].astype(bf16)

    fill(mix_columns)
    mix_copies = swap(mix_ref, mix_all.at[g, own], 0)
    locals_ = [
        pltpu.make_async_copy(mix_ref.at[own], mix_all.at[g, own], local_sem.at[0]),
        pltpu.make_async_copy(out_ref, out_all.at[g], local_sem.at[2]),
    ]
    for copy in locals_:
        copy.start()
    mix_line = Line(groups, mix_all.at[g], mix_all, mix_send, mix_recv)
    for copy in mix_copies:
        copy.wait()
    locals_[0].wait()
    mix_line.send(1)
    act.start(2)
    fill(unit_columns)
    ffn_copies = swap(near_ref, near_all.at[own], 3) + swap(far_ref, far_all.at[own], 6)
    for copy in (
        pltpu.make_async_copy(near_ref.at[own], near_all.at[own], local_sem.at[1]),
        pltpu.make_async_copy(far_ref.at[own], far_all.at[own], local_sem.at[5]),
    ):
        copy.start()
        locals_.append(copy)
    out_line.step(1)
    act.hand_on(1)
    act.hand_on(2)
    grad.start(1)
    grad.start(2)
    mix_line.step(1)
    act.hand_on(0)
    for k in range(2, groups):
        out_line.step(k)
        mix_line.step(k)
        if k == 2:
            grad.hand_on(1)
            grad.hand_on(2)
    grad.hand_on(0)
    for copy in ffn_copies:
        copy.wait()
    for copy in locals_[1:]:
        copy.wait()
    out_line.finish()
    mix_line.finish()
    act.finish()
    grad.finish()


def spread(groups, splits, near, mixers, units, out, act, grad, ident):
    vmem, hbm, dma = (
        pl.BlockSpec(memory_space=pltpu.VMEM),
        pl.BlockSpec(memory_space=pl.ANY),
        pltpu.SemaphoreType.DMA,
    )
    rows = mixers[0].shape[0]
    mix = (4, rows, 3 * mixers[0].shape[1] // 8)
    sides = [(4, rows, near), (4, rows, 2 * splits[-1] - near)]
    return pl.pallas_call(
        functools.partial(spread_kernel, groups, splits),
        out_shape=[
            jax.ShapeDtypeStruct((groups,) + mix, bf16),
            jax.ShapeDtypeStruct((groups,) + out.shape, bf16),
            jax.ShapeDtypeStruct((8,) + act.shape, bf16),
            jax.ShapeDtypeStruct((8,) + grad.shape, bf16),
        ]
        + [jax.ShapeDtypeStruct(shape, bf16) for shape in sides],
        in_specs=[vmem] * 5 + [hbm] * 3,
        out_specs=[hbm] * 6,
        scratch_shapes=[pltpu.VMEM(shape, bf16) for shape in (mix, *sides)]
        + [pltpu.VMEM((rows, 2 * splits[-1]), f32)]
        + [dma((6,)), dma((9,)), dma((9,))]
        + [dma((2, groups - 1))] * 4
        + [dma((8,))] * 4,
        compiler_params=pltpu.CompilerParams(
            collective_id=ident, has_side_effects=True, vmem_limit_bytes=62 * 2**20
        ),
    )(*mixers, *units, out, act, grad)


def scatter_kernel(count, *refs):
    parts, outs = refs[:count], refs[count : 2 * count]
    mine, theirs, outgoing, landing, local_sem, send_sem, recv_sem = refs[2 * count :]
    chips, core = places()
    sibling = device_at(chips[3], 1 - core)
    greet([device_at(chip, core) for chip in chips[:3]] + [sibling])
    swaps, locals_, sent = [], [], []
    for n in range(count):
        for j, chip in enumerate(chips):
            swaps.append(
                remote(
                    parts[n].at[rank_at(chip, 1 - core)],
                    theirs.at[n, j],
                    send_sem.at[n, j],
                    recv_sem.at[n, j],
                    sibling,
                )
            )
            local = pltpu.make_async_copy(
                parts[n].at[rank_at(chip, core)], mine.at[n, j], local_sem.at[n, j]
            )
            local.start()
            locals_.append(local)
    scatters = []
    for n in range(count):
        scatter = Scatter(
            [mine.at[n, j] for j in range(4)],
            theirs.at[n],
            outgoing.at[n],
            landing.at[n],
            send_sem.at[n, pl.ds(4, 6)],
            recv_sem.at[n, pl.ds(4, 6)],
        )
        for j in range(4):
            locals_[4 * n + j].wait()
            swaps[4 * n + j].wait_recv()
            if j < 3:
                scatter.first(j)
        scatters.append(scatter)
    for n, scatter in enumerate(scatters):
        scatter.second()

        def store(at, total, n=n):
            outs[n][at, :] = total

        scatter.totals(store)
    for scatter in scatters:
        scatter.finish()
    for copy in swaps:
        copy.wait_send()


def collect_kernel(streams, segments, size, rows, *refs):
    count = len(streams)
    parts, outs = refs[:count], refs[count : count + 3]
    landing = refs[count + 3 : 2 * count + 3]
    wholes = refs[2 * count + 3 : 2 * count + 6]
    local_sem, send_sem, recv_sem = refs[2 * count + 6 :]
    chips, core = places()
    others = [(j, chips[j], other) for j in range(4) for other in (core, 1 - core)]
    own = rank_at(chips[3], core)
    targets = [(chip, other) for j, chip, other in others if not (j == 3 and other is core)]
    greet([device_at(chip, other) for chip, other in targets])

    def source(n, rank):
        base, among, step = streams[n]
        return parts[n].at[pl.ds(pl.multiple_of(base + lax.rem(rank, among) * step, step), step)]

    copies, locals_ = [], []
    for n in range(count):
        for i, (chip, other) in enumerate(targets):
            copies.append(
                remote(
                    source(n, rank_at(chip, other)),
                    landing[n].at[own],
                    send_sem.at[n, i],
                    recv_sem.at[n, i],
                    device_at(chip, other),
                )
            )
        local = pltpu.make_async_copy(source(n, own), landing[n].at[own], local_sem.at[n])
        local.start()
        locals_.append(local)
    for copy in locals_:
        copy.wait()
    for copy in copies:
        copy.wait_recv()

    def lay(which, place, n, k, low, high):
        if n == 0:
            wholes[which][:, place : place + high - low] = landing[0][k, :, low:high].astype(f32)
            return
        while low < high:
            tile = low // 128
            end = min(high, (tile + 1) * 128)
            at = slice(place, place + end - low)
            first, last = low - tile * 128, end - tile * 128
            if tile < TILES:
                wholes[which][:, at] = landing[1][k, tile * rows : (tile + 1) * rows, first:last].astype(f32)
            else:
                for side in (0, 1):

                    @pl.when(chips[3][1] == side)
                    def _(side=side, at=at, first=first, last=last):
                        wholes[which][:, at] = landing[2][k, :, 64 * side + first : 64 * side + last].astype(f32)

            place, low = place + end - low, end

    for n, column, which, first, length in segments:
        for group in range(first // size, -(-(first + length) // size)):
            low, high = max(first, group * size), min(first + length, (group + 1) * size)
            for k in range(8):
                lay(which, group * 7 * size + k * size + low, n, k, column + low - first, column + high - first)
    for out, whole in zip(outs, wholes):
        out[...] = whole[...].astype(bf16)
    for copy in copies:
        copy.wait_send()


def collect(parts, streams, rows, segments, size, wide, ident):
    count = len(parts)
    vmem = pl.BlockSpec(memory_space=pltpu.VMEM)
    dma = pltpu.SemaphoreType.DMA
    return pl.pallas_call(
        functools.partial(collect_kernel, streams, segments, size, rows),
        out_shape=[jax.ShapeDtypeStruct((rows, wide), bf16)] * 3,
        in_specs=[pl.BlockSpec(memory_space=pl.ANY)] * count,
        out_specs=[vmem] * 3,
        scratch_shapes=[
            pltpu.VMEM((8, stream[2], part.shape[1]), bf16) for part, stream in zip(parts, streams)
        ]
        + [pltpu.VMEM((rows, wide), f32)] * 3
        + [dma((count,)), dma((count, 7)), dma((count, 7))],
        compiler_params=pltpu.CompilerParams(
            collective_id=ident, has_side_effects=True, vmem_limit_bytes=48 * 2**20
        ),
    )(*parts)


def close_kernel(sum_ref, w_ref, gain_ref, prob_ref, out_ref, sums_ref, bound_ref):
    width = w_ref.shape[1]
    out = sum_ref[:, :width].astype(f32)
    out_ref[...] = out
    gains = jnp.sum(out * w_ref[...].astype(f32), axis=1, keepdims=True)
    side = sum_ref[:, width:].astype(f32)
    lane = lax.broadcasted_iota(jnp.int32, side.shape, 1)
    turned = jnp.transpose(jnp.where(lane == 2, gains, side))
    sums_ref[...] = turned[2:3, :] / gain_ref[...]
    layer = lax.broadcasted_iota(jnp.int32, prob_ref.shape, 0)
    probs = prob_ref[...]
    grads = jnp.where((layer >= 1) & (layer <= LAYER_AT), turned[0:1, :] + turned[1:2, :], 0.0)
    bound_ref[...] = probs * (grads - jnp.sum(probs * grads, axis=0, keepdims=True))


def gather_plane(v, ident):
    hbm = pl.BlockSpec(memory_space=pl.ANY)
    out = pl.pallas_call(
        gather_kernel,
        out_shape=jax.ShapeDtypeStruct((8,) + v.shape, v.dtype),
        in_specs=[hbm],
        out_specs=hbm,
        scratch_shapes=[
            pltpu.SemaphoreType.DMA,
            pltpu.SemaphoreType.DMA((8,)),
            pltpu.SemaphoreType.DMA((8,)),
        ],
        compiler_params=pltpu.CompilerParams(
            collective_id=ident, has_side_effects=True, vmem_limit_bytes=48 * 2**20
        ),
    )(v)
    return out.reshape(-1, v.shape[1])


def scatter_plane(parts, ident):
    count, rows, wide = len(parts), parts[0].shape[0] // 8, parts[0].shape[1]
    return pl.pallas_call(
        functools.partial(scatter_kernel, count),
        out_shape=[jax.ShapeDtypeStruct((rows, wide), f32)] * count,
        in_specs=[pl.BlockSpec(memory_space=pl.ANY)] * count,
        out_specs=[pl.BlockSpec(memory_space=pltpu.VMEM)] * count,
        scratch_shapes=[
            pltpu.VMEM((count, 4, rows, wide), bf16),
            pltpu.VMEM((count, 4, rows, wide), bf16),
            pltpu.VMEM((count, 6, rows // 2, wide), bf16),
            pltpu.VMEM((count, 6, rows // 2, wide), bf16),
            pltpu.SemaphoreType.DMA((count, 4)),
            pltpu.SemaphoreType.DMA((count, 10)),
            pltpu.SemaphoreType.DMA((count, 10)),
        ],
        compiler_params=pltpu.CompilerParams(
            collective_id=ident, has_side_effects=True, vmem_limit_bytes=48 * 2**20
        ),
    )(*[part.reshape(8, rows, wide) for part in parts])


def dot(a, b):
    return jnp.dot(a, b, preferred_element_type=f32)


def dot_nt(a, b):
    return lax.dot_general(a, b, (((1,), (1,)), ((), ())), preferred_element_type=f32)


def dot_tn(a, b):
    return lax.dot_general(a, b, (((0,), (0,)), ((), ())), preferred_element_type=f32)


def body(
    tokens,
    cotangent,
    domain_tags,
    doc_ids,
    counts,
    w_in,
    w_forget,
    w_gate_out,
    w_out,
    ffn_gate,
    ffn_up,
    ffn_down,
    norm_gain,
    out_gain,
    ffn_gain,
    bound_logits,
):
    groups = lax.axis_size("g")
    members = lax.axis_size("p") * lax.axis_size("c")
    copies = lax.axis_size("x")
    ranks = members * copies
    rows, width = tokens.shape
    plane_rows = rows * ranks
    units = ffn_gate.shape[1]
    g, x = lax.axis_index("g"), lax.axis_index("x")
    rank = (lax.axis_index("p") * lax.axis_size("c") + lax.axis_index("c")) * copies + x
    ce = width // (groups * ranks)
    fe = units // (groups * ranks)
    chan, unit = ce * groups, fe * groups
    splits = (0, unit // QUARTERS, unit)
    near = -(-2 * splits[1] // 128) * 128

    def half_rows(w):
        half = w.shape[0] // copies
        return lax.dynamic_slice_in_dim(w, x * half, half, axis=0)

    def gather_rows(v):
        return lax.all_gather(v, "g", axis=0, tiled=True)

    def own_columns(v, size):
        v = v.reshape(groups, ranks, size)
        return lax.dynamic_index_in_dim(v, rank, axis=1, keepdims=False).reshape(1, groups * size)

    layer_count = bound_logits.shape[0]
    layer_probs = jax.nn.softmax(bound_logits, axis=0)
    layer_index = jnp.arange(layer_count, dtype=jnp.int32)
    layer_pick = ((layer_index >= 1) & (layer_index <= LAYER_AT)).astype(f32)[:, None]
    own_lower = jnp.sum(layer_probs * layer_pick, axis=0)[:, None]
    top, rest = split_hi_lo(own_lower)
    out_own = jnp.concatenate(
        [
            half_rows(w_out),
            top,
            rest,
            (own_lower - top.astype(f32) - rest.astype(f32)).astype(bf16),
            jnp.zeros((ce, 125), bf16),
        ],
        axis=1,
    )
    gain = own_columns(out_gain, ce)

    places = jnp.arange(doc_ids.shape[0], dtype=jnp.int32)
    previous = jnp.concatenate([doc_ids[:1], doc_ids[:-1]])
    keep = ((places % SEQ_LEN != 0) & (doc_ids == previous)).astype(f32)[:, None]
    keep = lax.dynamic_slice_in_dim(keep, g * plane_rows, plane_rows, axis=0)

    token_f = tokens.astype(f32)
    scale_one = lax.rsqrt(jnp.mean(token_f * token_f, axis=-1, keepdims=True) + EPS)
    normed_one = token_f * scale_one
    act_one_own = (normed_one * norm_gain).astype(bf16)

    domain_count = counts.shape[0]
    domain_hits = domain_tags[:, None] == jnp.arange(domain_count, dtype=jnp.int32)[None, :]
    per_token = jnp.sum(jnp.where(domain_hits, counts[None, :], 0), axis=1).astype(f32)
    seq_total = doc_ids.shape[0] // SEQ_LEN
    grad_z = cotangent.astype(f32) * (seq_total / (domain_count * per_token))[:, None]

    mix_w, out_ext, act_one, grad_m, *ffn = spread(
        groups,
        splits,
        near,
        (w_in, w_forget, w_gate_out),
        (ffn_gate, ffn_up),
        out_own,
        act_one_own,
        grad_z.astype(bf16),
        0,
    )
    mix_w = mix_w.reshape(width, 3 * chan)
    down_half = ffn_down.shape[0] // copies
    down_w = gather_rows(jnp.where(x == 0, ffn_down[:down_half], ffn_down[down_half:]))
    act_one, grad_m = act_one.reshape(plane_rows, width), grad_m.reshape(plane_rows, width)
    out_ext = out_ext.reshape(chan, -1)
    out_w = out_ext[:, :width]

    (
        proj,
        states,
        pre_grad,
        grads_kept,
        ffn_near,
        residual,
        hidden,
        grads_rest,
        act_two,
        ffn_far,
        state_scale,
        lower,
    ) = mixer(
        groups,
        chan,
        act_one,
        mix_w,
        out_ext,
        keep,
        gain,
        tokens,
        ffn_gain.reshape(1, width),
        grad_m,
        down_w,
        splits[1],
        ffn[0].reshape(-1, near),
        ffn[1].reshape(-1, 2 * unit - near),
        1,
    )
    act_two = act_two.reshape(plane_rows, width)
    branch = residual - token_f
    scale_two = lax.rsqrt(jnp.mean(residual * residual, axis=-1, keepdims=True) + EPS)
    normed_two = residual * scale_two

    def scatter_rows(v):
        return lax.psum_scatter(v, "g", scatter_dimension=0, tiled=True)

    ffn_sums = [scatter_rows(grads_kept)]
    ffn_near, ffn_far = ffn_near.reshape(width, near), ffn_far.reshape(width, -1)
    far_grads, pre_grad, hidden_far = feed(
        groups, act_two, grad_m, ffn_near, ffn_far, down_w, pre_grad, grads_rest
    )
    ffn_sums.append(scatter_rows(far_grads.reshape(-1, 128)))
    back_part = dot_nt(pre_grad[:, :near], ffn_near) + dot_nt(pre_grad[:, near:], ffn_far)
    back_part = back_part.astype(bf16)
    down_part = dot(hidden, down_w[: splits[1]]) + dot(hidden_far, down_w[splits[1] :])
    down_part = down_part.astype(bf16)

    (back_term,) = scatter_plane([back_part], 3)
    scaled_two = back_term * ffn_gain
    grad_resid = grad_z + scale_two * (
        scaled_two - normed_two * jnp.mean(scaled_two * normed_two, axis=-1, keepdims=True)
    )
    grad_branch_own = grad_resid.astype(bf16)
    mean_out = jnp.sum(grad_branch_own.astype(f32) * branch, axis=-1, keepdims=True) / width
    sent = jnp.concatenate(
        [
            grad_branch_own,
            *split_hi_lo(state_scale),
            *split_hi_lo(mean_out),
            jnp.zeros((rows, 124), bf16),
        ],
        axis=1,
    )
    got = gather_plane(sent, 4)
    grad_branch = got[:, :width]
    info = got[:, width:].astype(f32)
    info = jnp.concatenate([info[:, 0:1] + info[:, 1:2], info[:, 2:3] + info[:, 3:4]], axis=1)
    grad_mixed = dot_nt(grad_branch, out_w)
    grad_proj, mixed_out, sums = kernel_call(
        functools.partial(backward_scan, chan),
        [
            jax.ShapeDtypeStruct((plane_rows, 3 * chan), bf16),
            jax.ShapeDtypeStruct((plane_rows, chan), bf16),
            jax.ShapeDtypeStruct((1, chan), f32),
        ],
        proj,
        states,
        grad_mixed,
        info,
        keep,
        lower,
        gain,
    )
    in_part = dot_nt(grad_proj, mix_w).astype(bf16)
    down_part, grad_proj = lax.optimization_barrier((down_part, grad_proj))
    (down_term,) = scatter_plane([down_part], 5)
    mix_grads = dot_tn(act_one, grad_proj).astype(bf16)
    top, rest = split_hi_lo(sums.reshape(chan, 1))
    out_grads = jnp.concatenate(
        [dot_tn(mixed_out, grad_branch).astype(bf16), top, rest, jnp.zeros((chan, 126), bf16)], axis=1
    )
    mix_grads, ffn_sums, in_part, out_grads, down_term = lax.optimization_barrier(
        (mix_grads, ffn_sums, in_part, out_grads, down_term)
    )
    mix_sum = scatter_rows(mix_grads)
    out_grads, mix_sum = lax.optimization_barrier((out_grads, mix_sum))
    out_sum = scatter_rows(out_grads)
    first_channel = (g * ranks + rank) * ce
    summed_wout, summed_outg, grad_bounds = kernel_call(
        close_kernel,
        [
            jax.ShapeDtypeStruct((ce, width), f32),
            jax.ShapeDtypeStruct((1, ce), f32),
            jax.ShapeDtypeStruct(bound_logits.shape, f32),
        ],
        out_sum,
        half_rows(w_out),
        lax.dynamic_slice_in_dim(out_gain, first_channel, ce, axis=0).reshape(1, ce),
        layer_probs,
    )
    summed_outg = summed_outg.reshape(ce)
    (grad_act,) = scatter_plane([in_part], 6)
    output_rows = (residual + down_term).astype(bf16)

    scaled_one = grad_act * norm_gain
    grad_tokens = grad_resid + scale_one * (
        scaled_one - normed_one * jnp.mean(scaled_one * normed_one, axis=-1, keepdims=True)
    )

    first, lead, kept = splits[1], near - 2 * splits[1], grads_kept.shape[1]
    some, far = unit - first, 2 * unit - near
    segments = (
        (0, 0, 0, 0, first),
        (0, first, 1, 0, first),
        (0, 2 * first, 2, 0, kept - 2 * first),
        (1, 0, 0, first + lead, some - lead),
        (1, some - lead, 1, first, some),
        (1, far, 0, first, lead),
        (1, far + lead, 2, first, some),
        (1, far + lead + some, 2, kept - 2 * first, 3 * first - kept),
    )
    summed_fgate, summed_fup, fdown = [
        v.astype(f32)
        for v in collect(
            [ffn_sums[0], ffn_sums[1], ffn_sums[1]],
            [(0, 8, ce), (0, 8, TILES * ce), (8 * TILES * ce, 4, ce)],
            ce,
            segments,
            fe,
            units,
            7,
        )
    ]
    summed_fdown = fdown.T
    summed_win, summed_wforget, summed_wgate = [
        v.astype(f32)
        for v in collect(
            [mix_sum], [(0, 8, ce)], ce, [(0, n * chan, n, 0, chan) for n in range(3)], ce, width, 8
        )
    ]
    first = (g * ranks + rank) * ce

    def own_gain(gain, pairs):
        total = sum(jnp.sum(grad * half_rows(w).astype(f32), axis=1) for grad, w in pairs)
        return total / lax.dynamic_slice_in_dim(gain, first, ce, axis=0)

    summed_norm = own_gain(
        norm_gain, ((summed_win, w_in), (summed_wforget, w_forget), (summed_wgate, w_gate_out))
    )
    summed_ffng = own_gain(ffn_gain, ((summed_fgate, ffn_gate), (summed_fup, ffn_up)))
    return (
        output_rows,
        grad_tokens,
        summed_win,
        summed_wforget,
        summed_wgate,
        summed_wout,
        summed_fgate,
        summed_fup,
        summed_fdown,
        summed_norm,
        summed_outg,
        summed_ffng,
        grad_bounds,
    )


def solution(mesh):
    seqs, copies = mesh.shape["seq"], mesh.shape["rep"]
    mesh = Mesh(mesh.devices.reshape(seqs // 4, 2, 2, copies), ALL)
    by_rows = P(ALL, None)
    by_seq = P(("g", "p", "c"), None)
    placed = (
        (by_rows, by_rows, P(ALL), P(), P()) + (by_seq,) * 7 + (P(), P(), P(), P(None, ALL))
    )
    return jax.shard_map(
        body,
        mesh=mesh,
        in_specs=placed,
        out_specs=(by_rows,) * 8 + (P(None, ALL),) + (P(ALL),) * 3 + (P(None, ALL),),
        check_vma=False,
    )
```
